32 devices in a mesh: section: 2 (over core), dp: 4 (over y, x), seq: 4 (over z).
Axes of the slice: x: 2, y: 2, z: 4, core: 2. Of those that a mesh axis runs over, the one named last changes fastest.
Arguments:
- inputs: bfloat16 [16, 512, 512], P('dp', 'seq'), may hold values from -6 to 6
- cotangent: bfloat16 [16, 512, 512], P('dp', 'seq'), may hold values from -6 to 6
- lengths: int32 [16, 4], P('dp'), may hold values from 0 to 512, as said below
- ffn_one_up: bfloat16 [2, 512, 2048], P('section'), may hold values from -0.25 to 0.25
- ffn_one_down: bfloat16 [2, 2048, 512], P('section'), may hold values from -0.125 to 0.125
- attn_project: bfloat16 [2, 512, 1536], P('section'), may hold values from -0.25 to 0.25
- attn_output: bfloat16 [2, 512, 512], P('section'), may hold values from -4 to 4
- conv_expand: bfloat16 [2, 512, 1024], P('section'), may hold values from -0.25 to 0.25
- conv_depthwise: bfloat16 [2, 9, 512], P('section'), may hold values from -2 to 2
- conv_project: bfloat16 [2, 512, 512], P('section'), may hold values from -0.25 to 0.25
- ffn_two_up: bfloat16 [2, 512, 2048], P('section'), may hold values from -0.25 to 0.25
- ffn_two_down: bfloat16 [2, 2048, 512], P('section'), may hold values from -0.125 to 0.125
- norm_gains: bfloat16 [2, 6, 512], P('section'), may hold values from 0.5 to 1.5
Outputs:
- activations: bfloat16 [2, 16, 512, 512], P('section', 'dp', 'seq')
- input_grad: float32 [2, 16, 512, 512], P('section', 'dp', 'seq')
- grad_ffn_one_up: float32 [2, 512, 2048], P('section', 'seq')
- grad_ffn_one_down: float32 [2, 2048, 512], P('section', 'seq')
- grad_attn_project: float32 [2, 512, 1536], P('section', 'seq')
- grad_attn_output: float32 [2, 512, 512], P('section', 'seq')
- grad_conv_expand: float32 [2, 512, 1024], P('section', 'seq')
- grad_conv_depthwise: float32 [2, 9, 512], P('section', None, 'seq')
- grad_conv_project: float32 [2, 512, 512], P('section', 'seq')
- grad_ffn_two_up: float32 [2, 512, 2048], P('section', 'seq')
- grad_ffn_two_down: float32 [2, 2048, 512], P('section', 'seq')
- grad_norm_gains: float32 [2, 6, 512], P('section', None, 'seq')
The draws below stay inside these ranges and needn't reach their ends.
Inputs may be any that keep to these rules, and one draw needn't show every extreme that they name: `lengths`: in each aligned group of 2 rows (one micro-batch of a replica), exactly one row, drawn from the seed, holds a single utterance of all 512 frames followed by zeros; every other row holds 4 utterances of 64 to 128 frames each, with padding after them.
All inputs are finite; a program needn't handle non-finite values.
Results may differ from the reference program's by a relative error of at most 0.025.
Values may be sent and summed in bfloat16 or wider, within the bound.
No kernel may reach another device: no remote copies, remote signals or barrier semaphores. Data moves between devices by JAX's collectives and lax.ppermute only.
A program may use at most 192 MiB of HBM per device.

```python
import jax
import jax.numpy as jnp
from jax import lax

D = 512
H = 8
HD = 64
F = 2048
K = 9
W = 128
BR = 2
UTT = 4
LENGTH = 512
ROWS = 16
N_SECTION = 2


def draw_lengths(key, part):
    key = jax.random.fold_in(key, 7)
    pick_key, clip_key = jax.random.split(key)
    groups = ROWS // BR
    longest = jax.random.randint(pick_key, (groups,), 0, BR)
    chosen = (jnp.arange(BR, dtype=jnp.int32)[None, :] == longest[:, None]).reshape(ROWS)
    clip_lengths = jax.random.randint(clip_key, (ROWS, UTT), LENGTH // (2 * UTT), LENGTH // UTT + 1)
    whole_row = jnp.concatenate([jnp.full((1,), LENGTH, jnp.int32), jnp.zeros((UTT - 1,), jnp.int32)])
    return jnp.where(chosen[:, None], whole_row[None, :], clip_lengths).astype(jnp.int32)


def steps_of(rng, shape, cuts, least, largest):
    level = 1.0
    for axis_at, parts in cuts:
        draws = jax.random.uniform(jax.random.fold_in(jax.random.fold_in(rng, 6), axis_at), (parts,), jnp.float32, least / len(cuts), largest / len(cuts))
        level = level * jnp.repeat(jnp.exp(draws), shape[axis_at] // parts).reshape((-1,) + (1,) * (len(shape) - 1 - axis_at))
    return level


def noise(stream_key, extent, spread, limit, pieces=(), kind=jnp.bfloat16):
    gain = steps_of(stream_key, extent, pieces, -0.22, 0.18) if pieces else 1.0
    values = jax.random.normal(stream_key, extent, jnp.float32) * spread * gain
    return jnp.minimum(jnp.maximum(values, -limit), limit).astype(kind)


def setup_inputs(seed: int = 0) -> dict:
    splits = jax.random.split(jax.random.key(seed), 14)
    return {
        "inputs": noise(splits[0], (ROWS, LENGTH, D), 1.0, 6.0, ((0, 4), (1, 4))),
        "cotangent": noise(splits[1], (ROWS, LENGTH, D), 1.0, 6.0, ((0, 4), (1, 4))),
        "lengths": draw_lengths(jax.random.fold_in(splits[13], 71), 0),
        "ffn_one_up": noise(splits[3], (N_SECTION, D, F), D ** -0.5, 0.25, ((0, 2),)),
        "ffn_one_down": noise(splits[4], (N_SECTION, F, D), F ** -0.5, 0.125, ((0, 2),)),
        "attn_project": noise(splits[5], (N_SECTION, D, 3 * D), D ** -0.5, 0.25, ((0, 2),)),
        "attn_output": noise(splits[6], (N_SECTION, D, D), (D // (2 * W + 1) + 1) ** -0.5, 4.0, ((0, 2),)),
        "conv_expand": noise(splits[7], (N_SECTION, D, 2 * D), D ** -0.5, 0.25, ((0, 2),)),
        "conv_depthwise": noise(splits[8], (N_SECTION, K, D), K ** -0.5, 2.0, ((0, 2),)),
        "conv_project": noise(splits[9], (N_SECTION, D, D), D ** -0.5, 0.25, ((0, 2),)),
        "ffn_two_up": noise(splits[10], (N_SECTION, D, F), D ** -0.5, 0.25, ((0, 2),)),
        "ffn_two_down": noise(splits[11], (N_SECTION, F, D), F ** -0.5, 0.125, ((0, 2),)),
        "norm_gains": jnp.clip(1.0 + 0.1 * jax.random.normal(splits[12], (N_SECTION, 6, D), jnp.float32), 0.5, 1.5).astype(jnp.bfloat16),
    }


@jax.custom_vjp
def low(v):
    return lax.optimization_barrier(v.astype(jnp.bfloat16)).astype(jnp.float32)

@jax.custom_vjp
def low_back(v):
    return v

def low_keep(v):
    return (low(v), None)

def low_pass(kept, grad):
    return (grad,)

def back_keep(v):
    return (v, None)

def back_low(kept, grad):
    return (low(grad),)
low.defvjp(low_keep, low_pass)
low_back.defvjp(back_keep, back_low)
EPSILON = 1e-05
MASKED = -1e+30
HIGHEST = lax.Precision.HIGHEST

def layer_norm(values, gain_row):
    average = lax.optimization_barrier(jnp.mean(values, axis=-1, keepdims=True))
    centred = values - average
    variance = lax.optimization_barrier(jnp.mean(centred * centred, axis=-1, keepdims=True))
    return centred * lax.rsqrt(variance + EPSILON) * gain_row

def matmul(first_mat, second_mat):
    return jnp.dot(first_mat, second_mat, precision=HIGHEST)

def segments(row_lengths):
    positions = jnp.arange(LENGTH, dtype=jnp.int32)
    bounds = jnp.cumsum(row_lengths).astype(jnp.int32)
    segment_ids = lax.optimization_barrier(jnp.sum((positions[:, None] >= bounds[None, :]).astype(jnp.int32), axis=1)).astype(jnp.int32)
    valid_rows = (positions < bounds[-1]).astype(jnp.float32)
    return (segment_ids, valid_rows)

def attention(queries, keys_all, values_all, segment_ids):
    context = W
    padded_keys = jnp.pad(keys_all, ((context, context), (0, 0), (0, 0)))
    padded_values = jnp.pad(values_all, ((context, context), (0, 0), (0, 0)))
    padded_ids = jnp.pad(segment_ids, (context, context), constant_values=-1)
    block_rows = min(512, LENGTH)
    key_span = block_rows + 2 * context
    scaling = HD ** (-0.5)

    def one_block(block_start):
        query_block = lax.dynamic_slice_in_dim(queries, block_start, block_rows, 0)
        key_block = lax.dynamic_slice_in_dim(padded_keys, block_start, key_span, 0)
        value_block = lax.dynamic_slice_in_dim(padded_values, block_start, key_span, 0)
        query_ids = lax.dynamic_slice_in_dim(segment_ids, block_start, block_rows, 0)
        key_ids = lax.dynamic_slice_in_dim(padded_ids, block_start, key_span, 0)
        offsets = jnp.arange(block_rows, dtype=jnp.int32)[:, None] + context - jnp.arange(key_span, dtype=jnp.int32)[None, :]
        allowed = (jnp.abs(offsets) <= context) & (query_ids[:, None] == key_ids[None, :])
        scores = low_back(jnp.einsum('qhd,khd->hqk', query_block, key_block, precision=HIGHEST) * scaling)
        scores = jnp.where(allowed[None], scores, MASKED)
        row_peak = lax.optimization_barrier(jnp.max(scores, axis=-1, keepdims=True))
        exponent = jnp.exp(scores - row_peak)
        weights = low(exponent / lax.optimization_barrier(jnp.sum(exponent, axis=-1, keepdims=True)))
        return jnp.einsum('hqk,khd->qhd', weights, value_block, precision=HIGHEST)
    starts = jnp.arange(LENGTH // block_rows, dtype=jnp.int32) * block_rows
    blocks = lax.map(jax.checkpoint(one_block), starts)
    return blocks.reshape(LENGTH, D)

def depthwise(gated_rows, depth_taps, segment_ids):
    half_kernel = (K - 1) // 2
    padded = jnp.pad(gated_rows, ((half_kernel, half_kernel), (0, 0)))
    padded_ids = jnp.pad(segment_ids, (half_kernel, half_kernel), constant_values=-1)
    running = jnp.zeros(gated_rows.shape, jnp.float32)
    for tap_index in range(K):
        same_segment = padded_ids[tap_index:tap_index + LENGTH] == segment_ids
        window = padded[tap_index:tap_index + LENGTH] * depth_taps[tap_index]
        running = running + jnp.where(same_segment[:, None], window, 0.0)
    return running

def layer(layer_input, layer_weights, segment_ids, valid_rows):
    up_first, down_first, qkv_proj, out_proj, expand_mat, depth_taps, project_mat, up_second, down_second, gain_table = layer_weights
    hidden_one = low(layer_norm(layer_input, gain_table[0]))
    inner_one = low_back(matmul(hidden_one, up_first))
    active_one = low(jax.nn.silu(inner_one))
    after_ffn = layer_input + 0.5 * low_back(matmul(active_one, down_first))
    hidden_two = low(layer_norm(after_ffn, gain_table[1]))
    projected = low(low_back(matmul(hidden_two, qkv_proj)))
    queries = projected[:, :D].reshape(LENGTH, H, HD)
    keys_all = projected[:, D:2 * D].reshape(LENGTH, H, HD)
    values_all = projected[:, 2 * D:].reshape(LENGTH, H, HD)
    attended = low(low_back(attention(queries, keys_all, values_all, segment_ids)))
    after_attn = after_ffn + low_back(matmul(attended, out_proj))
    hidden_three = low(layer_norm(after_attn, gain_table[2]))
    conv_pre = low_back(matmul(hidden_three, expand_mat))
    gated_rows = low(conv_pre[:, :D] * jax.nn.sigmoid(conv_pre[:, D:]))
    mixed_time = low_back(depthwise(gated_rows, depth_taps, segment_ids))
    conv_act = low(jax.nn.silu(layer_norm(mixed_time, gain_table[3])))
    after_conv = after_attn + low_back(matmul(conv_act, project_mat))
    hidden_four = low(layer_norm(after_conv, gain_table[4]))
    inner_two = low_back(matmul(hidden_four, up_second))
    active_two = low(jax.nn.silu(inner_two))
    after_second = after_conv + 0.5 * low_back(matmul(active_two, down_second))
    return layer_norm(after_second, gain_table[5]) * valid_rows[:, None]

def reference(inputs, cotangent, lengths, ffn_one_up, ffn_one_down, attn_project, attn_output, conv_expand, conv_depthwise, conv_project, ffn_two_up, ffn_two_down, norm_gains):
    stacked = (ffn_one_up, ffn_one_down, attn_project, attn_output, conv_expand, conv_depthwise, conv_project, ffn_two_up, ffn_two_down, norm_gains)
    per_section = [tuple((weight[section_index].astype(jnp.float32) for weight in stacked)) for section_index in range(N_SECTION)]
    zero_grads = tuple((jnp.zeros(weight.shape, jnp.float32) for weight in stacked))

    def per_row(totals, row_items):
        row_inputs, row_cotangent, row_lengths = row_items
        segment_ids, valid_rows = segments(row_lengths)

        def apply_layer(values, layer_weights):
            return layer(values, layer_weights, segment_ids, valid_rows)
        current = row_inputs.astype(jnp.float32)
        back_fns = []
        outputs = []
        for section_index in range(N_SECTION):
            if section_index > 0:
                current = low(current)
            current, back_fn = jax.vjp(apply_layer, current, per_section[section_index])
            back_fns.append(back_fn)
            outputs.append(current.astype(jnp.bfloat16))
        incoming = row_cotangent.astype(jnp.float32)
        input_grads = []
        weight_grads = []
        for section_index in reversed(range(N_SECTION)):
            if section_index < N_SECTION - 1:
                incoming = low(incoming)
            grad_input, grad_weights = back_fns[section_index](incoming)
            input_grads.insert(0, grad_input)
            weight_grads.insert(0, grad_weights)
            incoming = grad_input
        totals = tuple((running + jnp.stack([weight_grads[section_index][member] for section_index in range(N_SECTION)]) for member, running in enumerate(totals)))
        return (totals, (jnp.stack(outputs), jnp.stack(input_grads)))
    totals, (activations, input_grads) = lax.scan(per_row, zero_grads, (inputs, cotangent, lengths))
    activations = jnp.swapaxes(activations, 0, 1)
    input_grads = jnp.swapaxes(input_grads, 0, 1)
    return (activations, input_grads) + totals
```

```python
import functools
from types import SimpleNamespace

import jax
import jax.numpy as jnp
from jax import lax
from jax.experimental import pallas as pl
from jax.experimental.pallas import tpu as pltpu
from jax.sharding import PartitionSpec as P

D = 512
H = 8
HD = 64
F = 2048
FH = F // 2
K = 9
W = 128
UTT = 4
EPSILON = 1e-05
MASKED = -1e30
EDGE = 16
CHUNK = 512
MIB = 1024 * 1024
MESH_AXES = ("section", "dp", "seq")

BF = jnp.bfloat16
F32 = jnp.float32

UP1, DN1, QKV, OUT, EXP, PRJ, UP2, DN2 = range(8)


def dot(a, b):
    return jnp.dot(a, b, preferred_element_type=F32)


def dot_nt(a, b):
    return lax.dot_general(a, b, (((1,), (1,)), ((), ())), preferred_element_type=F32)


def dot_tn(a, b):
    return lax.dot_general(a, b, (((0,), (0,)), ((), ())), preferred_element_type=F32)


def sigmoid(v):
    return 0.5 * jnp.tanh(0.5 * v) + 0.5


def norm_stats(v):
    centred = v - jnp.mean(v, axis=-1, keepdims=True)
    inverse = lax.rsqrt(jnp.mean(centred * centred, axis=-1, keepdims=True) + EPSILON)
    return centred * inverse, inverse


def norm_back(upstream, normed, inverse, gain):
    gain_grad = jnp.sum(upstream * normed, axis=0, keepdims=True)
    scaled = upstream * gain
    value_grad = inverse * (
        scaled
        - jnp.mean(scaled, axis=-1, keepdims=True)
        - normed * jnp.mean(scaled * normed, axis=-1, keepdims=True)
    )
    return value_grad, gain_grad


CORE, ROW, FIRST, LENGTH, SIDE1, SIDE2, OTHER1, CHIP, ENDS = range(9)


class Ctx:
    def __init__(self, plan, scalars, table, held, waits):
        self.__dict__.update(table)
        self.plan = plan
        self.scalars = scalars
        self.held = held
        self.waits = waits
        self.core = scalars[CORE]
        self.first = scalars[FIRST]

    def weight(self, matrix, layer, part=None):
        queue = self.waits[(matrix, layer)]
        for index in range(len(queue)):
            if queue[index] is not None and (part is None or part == index):
                queue[index].wait()
                queue[index] = None
        return self.held[(matrix, layer)]

    def small(self, row, layer):
        mine = self.core == layer
        return jnp.where(mine, self.small_own[row : row + 1, :], self.small_other[row : row + 1, :])

    def taps(self, tap, layer):
        return self.small(6 + tap, layer)

    def seg(self, pos):
        total = jnp.zeros(pos.shape, jnp.int32)
        for u in range(UTT):
            total = total + (pos >= self.scalars[ENDS + u]).astype(jnp.int32)
        return total


def parts_of(matrix, shape):
    if matrix in (UP1, UP2):
        return [(slice(None), pl.ds(c, CHUNK)) for c in range(0, F, CHUNK)]
    if matrix in (DN1, DN2):
        return [(pl.ds(c, CHUNK), slice(None)) for c in range(0, F, CHUNK)]
    return [(slice(None), slice(None))]


def launch(plan, body, name, ins, outs, weights=(), scratch=None, far=None, far_outs=None, limit=16):
    scratch, far, far_outs = scratch or {}, far or {}, far_outs or {}
    near = dict(ins)
    if weights:
        near.update(small_own=plan.small_own, small_other=plan.small_other)
    if plan.token is not None:
        near.update(token_in=plan.token)
    pinned = [pltpu.with_memory_space_constraint(v, pltpu.VMEM) for v in near.values()]
    operands = [plan.scalars] + pinned + list(far.values())
    in_specs = [pl.BlockSpec(memory_space=pltpu.SMEM)]
    in_specs += [pl.BlockSpec(memory_space=pltpu.VMEM)] * len(near)
    in_specs += [pl.BlockSpec(memory_space=pl.ANY)] * len(far)
    copies = []
    for matrix, layer in weights:
        operands += [plan.own[matrix], plan.other[matrix]]
        in_specs += [pl.BlockSpec(memory_space=pl.ANY)] * 2
        copies.append(parts_of(matrix, plan.own[matrix].shape))
    held_shapes = [pltpu.VMEM(plan.own[m].shape, BF) for m, _ in weights]
    out_shape = [pltpu.VMEM(*s) for s in outs.values()]
    out_shape += [jax.ShapeDtypeStruct(*s) for s in far_outs.values()]
    out_shape += [pltpu.VMEM((8, 128), jnp.int32)]
    out_specs = [pl.BlockSpec(memory_space=pltpu.VMEM)] * len(outs)
    out_specs += [pl.BlockSpec(memory_space=pl.ANY)] * len(far_outs)
    out_specs += [pl.BlockSpec(memory_space=pltpu.VMEM)]
    sems = max(sum(len(c) for c in copies), 1) + 24

    def kernel(*refs):
        refs = list(refs)
        scalars = refs.pop(0)
        table = {}
        for n in list(near) + list(far):
            table[n] = refs.pop(0)
        sources = [(refs.pop(0), refs.pop(0)) for _ in weights]
        for n in list(outs) + list(far_outs):
            table[n] = refs.pop(0)
        refs.pop(0)
        for n in scratch:
            table[n] = refs.pop(0)
        held_refs = [refs.pop(0) for _ in weights]
        sem = refs.pop(0)
        core = scalars[CORE]
        held, waits = {}, {}
        for pair in weights:
            waits[pair] = []
        count = 0
        for part in range(max([len(c) for c in copies], default=0)):
            for pair, (own, other), into, slices in zip(weights, sources, held_refs, copies):
                held[pair] = into
                if part >= len(slices):
                    continue
                at = slices[part]

                @pl.when(core == pair[1])
                def _(own=own, into=into, at=at, count=count):
                    pltpu.make_async_copy(own.at[at], into.at[at], sem.at[count]).start()

                @pl.when(core != pair[1])
                def _(other=other, into=into, at=at, count=count):
                    pltpu.make_async_copy(other.at[at], into.at[at], sem.at[count]).start()

                waits[pair].append(pltpu.make_async_copy(own.at[at], into.at[at], sem.at[count]))
                count += 1
        ctx = Ctx(plan, scalars, table, held, waits)
        ctx.sems = [sem.at[sems - 24 + i] for i in range(24)]
        body(ctx)
        for pair in weights:
            ctx.weight(*pair)

    results = pl.pallas_call(
        kernel,
        out_shape=out_shape,
        in_specs=in_specs,
        out_specs=out_specs,
        scratch_shapes=[pltpu.VMEM(*s) for s in scratch.values()]
        + held_shapes
        + [pltpu.SemaphoreType.DMA((sems,))],
        compiler_params=pltpu.CompilerParams(vmem_limit_bytes=limit * MIB),
        name=name,
    )(*operands)
    plan.token = results[-1]
    return SimpleNamespace(**dict(zip(list(outs) + list(far_outs), results)))


def half_copies(ctx, value_ref, keep_ref, send_ref, keep_at, send_at, total, blocks):
    width = total // (2 * blocks)
    for j in range(blocks):
        mine = pl.multiple_of(j * 2 * width + ctx.core * width, width)
        theirs = pl.multiple_of(j * 2 * width + (1 - ctx.core) * width, width)
        keep_ref[:, keep_at + j * width : keep_at + (j + 1) * width] = value_ref[:, pl.ds(mine, width)]
        send_ref[:, send_at + j * width : send_at + (j + 1) * width] = value_ref[
            :, pl.ds(theirs, width)
        ]


def edge_rows(ctx, value_ref, send_ref, rows):
    frames = value_ref.shape[0]
    if ctx.plan.halos == 1:
        at = pl.multiple_of((1 - ctx.core) * (frames - rows), rows)
        send_ref[...] = value_ref[pl.ds(at, rows), :]
    else:
        send_ref[0:rows, :] = value_ref[frames - rows : frames, :]
        send_ref[rows : 2 * rows, :] = value_ref[0:rows, :]


def halo_starts(ctx, rows, frames):
    before = ctx.first - rows
    after = ctx.first + frames
    if ctx.plan.halos == 1:
        return [jnp.where(ctx.core == 0, after, before)]
    return [before, after]


def feed_forward(ctx, hidden, up, down, layer, keep_ref, send_ref, send_at, slope_ref):
    frames = hidden.shape[0]
    total = jnp.zeros((frames, D), F32)
    for part, c in enumerate(range(0, F, CHUNK)):
        at = slice(c, c + CHUNK)
        inner = dot(hidden, ctx.weight(up, layer, part)[:, at])
        logistic = sigmoid(inner)
        active = (inner * logistic).astype(BF)
        slope_ref[:, at] = (logistic * (1.0 + inner * (1.0 - logistic))).astype(BF)
        ctx.act[:, at] = active
        total = total + dot(active, ctx.weight(down, layer, part)[at, :])
    half_copies(ctx, ctx.act, keep_ref, send_ref, 0, send_at, F, ctx.plan.blocks)
    return total


def fwd_first(ctx, x, layer):
    normed, _ = norm_stats(x)
    hidden = (normed * ctx.small(0, layer)).astype(BF)
    ctx.p1[:, 0:D] = hidden
    ffn = feed_forward(ctx, hidden, UP1, DN1, layer, ctx.a1, ctx.p1, 2 * D, ctx.s1)
    r1 = x + 0.5 * ffn
    ctx.r1[...] = r1
    normed, _ = norm_stats(r1)
    hidden = (normed * ctx.small(1, layer)).astype(BF)
    ctx.p1[:, D : 2 * D] = hidden
    ctx.qkv[...] = dot(hidden, ctx.weight(QKV, layer)[...]).astype(BF)
    edge_rows(ctx, ctx.qkv.at[:, D : 3 * D], ctx.kvs, W)


def first_outs(plan):
    t = plan.frames
    return dict(
        p1=((t, 2 * D + FH), BF),
        a1=((t, FH), BF),
        s1=((t, F), BF),
        r1=((t, D), F32),
        qkv=((t, 3 * D), BF),
        kvs=((plan.halos * W, 2 * D), BF),
    )


def call_first(plan, pieces):
    def body(ctx):
        join_frames(ctx, ctx.x)
        fwd_first(ctx, ctx.x[...].astype(F32), 0)

    t = plan.frames
    return launch(
        plan, body, "first", pieces, dict(x=((t, D), BF), **first_outs(plan)),
        [(UP1, 0), (DN1, 0), (QKV, 0)], dict(act=((t, F), BF)),
    )


def allowed_bias(ctx, key_start, keys):
    frames = ctx.plan.frames
    shape = (frames, keys)
    query = ctx.first + lax.broadcasted_iota(jnp.int32, shape, 0)
    key = key_start + lax.broadcasted_iota(jnp.int32, shape, 1)
    near = jnp.abs(query - key) <= W
    inside = (key >= 0) & (key < ctx.scalars[LENGTH])
    same = ctx.seg(query) == ctx.seg(key)
    return jnp.where(near & inside & same, 0.0, MASKED).astype(F32)


def fwd_attend(ctx, layer):
    t = ctx.plan.frames
    halos = ctx.plan.halos
    qkv, kvh, probs, p2, bias = ctx.qkv, ctx.kvh, ctx.probs, ctx.p2, ctx.bias
    starts = halo_starts(ctx, W, t)
    bias[:, 0:t] = allowed_bias(ctx, ctx.first, t)
    for h in range(halos):
        bias[:, t + h * W : t + (h + 1) * W] = allowed_bias(ctx, starts[h], W)
    lane = lax.broadcasted_iota(jnp.int32, (t, 2 * HD), 1)
    for p in range(H // 2):
        at = 2 * HD * p
        q = qkv[:, at : at + 2 * HD] * jnp.asarray(HD ** (-0.5), BF)
        k = qkv[:, D + at : D + at + 2 * HD]
        v = qkv[:, 2 * D + at : 2 * D + at + 2 * HD]
        kh = kvh[:, at : at + 2 * HD]
        vh = kvh[:, D + at : D + at + 2 * HD]
        outs = []
        for e in range(2):
            mine = (lane // HD) == e
            qm = jnp.where(mine, q, jnp.zeros_like(q))
            so = dot_nt(qm, k) + bias[:, 0:t]
            sh = dot_nt(qm, kh) + bias[:, t:]
            peak = jnp.maximum(
                jnp.max(so, axis=-1, keepdims=True), jnp.max(sh, axis=-1, keepdims=True)
            )
            eo = jnp.exp(so - peak)
            eh = jnp.exp(sh - peak)
            scale = 1.0 / (
                jnp.sum(eo, axis=-1, keepdims=True) + jnp.sum(eh, axis=-1, keepdims=True)
            )
            po = (eo * scale).astype(BF)
            ph = (eh * scale).astype(BF)
            probs[2 * p + e, :, 0:t] = po
            probs[2 * p + e, :, t:] = ph
            outs.append(dot(po, v) + dot(ph, vh))
        p2[:, at : at + 2 * HD] = jnp.where(lane < HD, outs[0], outs[1]).astype(BF)
    r2 = ctx.r1[...] + dot(p2[:, 0:D], ctx.weight(OUT, layer)[...])
    ctx.r2[...] = r2
    normed, _ = norm_stats(r2)
    hidden = (normed * ctx.small(2, layer)).astype(BF)
    p2[:, D : 2 * D] = hidden
    expand = ctx.weight(EXP, layer)
    linear = dot(hidden, expand[:, 0:D])
    logistic = sigmoid(dot(hidden, expand[:, D : 2 * D]))
    gated = linear * logistic
    ctx.g[...] = gated.astype(BF)
    ctx.gs[...] = logistic.astype(BF)
    ctx.gt[...] = (gated * (1.0 - logistic)).astype(BF)
    edge_rows(ctx, ctx.g, ctx.gsend, EDGE)


def call_attend(plan, layer, first, kvh):
    t = plan.frames
    keys = t + plan.halos * W
    return launch(
        plan,
        lambda ctx: fwd_attend(ctx, layer),
        "attend",
        dict(qkv=first.qkv, kvh=kvh, r1=first.r1),
        dict(
            probs=((H, t, keys), BF),
            p2=((t, 2 * D), BF),
            r2=((t, D), F32),
            g=((t, D), BF),
            gs=((t, D), BF),
            gt=((t, D), BF),
            gsend=((plan.halos * EDGE, D), BF),
        ),
        [(OUT, layer), (EXP, layer)],
        dict(bias=((t, keys), F32)),
    )


def fill_extended(ctx, ext, own, halo):
    t = ctx.plan.frames
    before = halo[EDGE - 8 : EDGE, :]
    after = halo[0:8, :] if ctx.plan.halos == 1 else halo[EDGE : EDGE + 8, :]
    ext[0:8, :] = before.astype(F32)
    ext[8 : 8 + t, :] = own[...].astype(F32)
    ext[8 + t : 16 + t, :] = after.astype(F32)


def tap_masks(ctx, row, rows):
    pos = ctx.first + row + lax.broadcasted_iota(jnp.int32, (rows, 128), 0)
    here = ctx.seg(pos)
    masks = []
    for k in range(K):
        there = pos + (k - K // 2)
        masks.append((ctx.seg(there) == here) & (there >= 0) & (there < ctx.scalars[LENGTH]))
    return masks


def mix_time(ctx, ext, z_ref, layer):
    t = ctx.plan.frames
    taps = [ctx.taps(k, layer) for k in range(K)]
    block = 64
    for row in range(0, t, block):
        masks = tap_masks(ctx, row, block)
        for c in range(0, D, 128):
            total = jnp.zeros((block, 128), F32)
            for k in range(K):
                at = 8 + row + k - K // 2
                window = ext[at : at + block, c : c + 128] * taps[k][:, c : c + 128]
                total = total + jnp.where(masks[k], window, 0.0)
            z_ref[row : row + block, c : c + 128] = total


def valid_rows(ctx):
    pos = ctx.first + lax.broadcasted_iota(jnp.int32, (ctx.plan.frames, 1), 0)
    return (pos < ctx.scalars[ENDS + UTT - 1]).astype(F32)


def fwd_conv(ctx, layer):
    fill_extended(ctx, ctx.ext, ctx.g, ctx.gh)
    mix_time(ctx, ctx.ext, ctx.z, layer)
    normed, _ = norm_stats(ctx.z[...])
    mixed = normed * ctx.small(3, layer)
    active = (mixed * sigmoid(mixed)).astype(BF)
    ctx.p3[:, 0:D] = active
    r3 = ctx.r2[...] + dot(active, ctx.weight(PRJ, layer)[...])
    ctx.r3[...] = r3
    normed, _ = norm_stats(r3)
    hidden = (normed * ctx.small(4, layer)).astype(BF)
    ctx.p3[:, D : 2 * D] = hidden
    ffn = feed_forward(ctx, hidden, UP2, DN2, layer, ctx.a2, ctx.p3, 2 * D, ctx.s2)
    r4 = r3 + 0.5 * ffn
    ctx.r4[...] = r4
    normed, _ = norm_stats(r4)
    result = (normed * ctx.small(5, layer) * valid_rows(ctx)).astype(BF)
    ctx.y[...] = result
    return result


def conv_outs(plan):
    t = plan.frames
    return dict(
        z=((t, D), F32),
        p3=((t, 2 * D + FH), BF),
        a2=((t, FH), BF),
        s2=((t, F), BF),
        r3=((t, D), F32),
        r4=((t, D), F32),
        y=((t, D), BF),
    )


def conv_scratch(plan):
    t = plan.frames
    return dict(ext=((t + 16, D), F32), act=((t, F), BF))


def call_conv_first(plan, mid, gh):
    def body(ctx):
        fwd_first(ctx, fwd_conv(ctx, 0).astype(F32), 1)

    return launch(
        plan, body, "conv_first", dict(g=mid.g, gh=gh, r2=mid.r2),
        dict(conv_outs(plan), **first_outs(plan)),
        [(PRJ, 0), (UP2, 0), (DN2, 0), (UP1, 1), (DN1, 1), (QKV, 1)],
        conv_scratch(plan), limit=20,
    )


def call_conv_last(plan, mid, gh, pieces):
    def body(ctx):
        fwd_conv(ctx, 1)
        join_frames(ctx, ctx.dy)
        bwd_last(ctx, ctx.dy[...], 1)

    return launch(
        plan, body, "conv_last", dict(g=mid.g, gh=gh, r2=mid.r2, **pieces),
        dict(conv_outs(plan), **last_outs(plan)),
        [(PRJ, 1), (UP2, 1), (DN2, 1)],
        dict(conv_scratch(plan), dy=((plan.frames, D), BF)), limit=20,
    )


def feed_forward_back(ctx, step, up, down, layer, slope_ref, keep_ref, send_ref, send_at):
    total = jnp.zeros((step.shape[0], D), F32)
    for part, c in enumerate(range(0, F, CHUNK)):
        at = slice(c, c + CHUNK)
        grad = dot_nt(step, ctx.weight(down, layer, part)[at, :]) * slope_ref[:, at].astype(F32)
        grad = grad.astype(BF)
        ctx.act[:, at] = grad
        total = total + dot_nt(grad, ctx.weight(up, layer, part)[:, at])
    half_copies(ctx, ctx.act, keep_ref, send_ref, 0, send_at, F, 1)
    return total


def bwd_last(ctx, dy, layer):
    upstream = dy.astype(F32) * valid_rows(ctx)
    smalls = ctx.smalls
    smalls[...] = jnp.zeros(smalls.shape, F32)
    normed, inverse = norm_stats(ctx.r4[...])
    stream, gg = norm_back(upstream, normed, inverse, ctx.small(5, layer))
    smalls[5:6, :] = gg
    step = (0.5 * stream).astype(BF)
    ctx.q3[:, 0:D] = step
    inner = feed_forward_back(ctx, step, UP2, DN2, layer, ctx.s2, ctx.k3, ctx.q3, D)
    normed, inverse = norm_stats(ctx.r3[...])
    branch, gg = norm_back(inner, normed, inverse, ctx.small(4, layer))
    smalls[4:5, :] = gg
    stream = stream + branch
    ctx.dr3[...] = stream
    step = stream.astype(BF)
    ctx.act[:, 0:D] = step
    half_copies(ctx, ctx.act.at[:, 0:D], ctx.k3, ctx.q3, FH, D + FH, D, 1)
    normed, inverse = norm_stats(ctx.z[...])
    gain = ctx.small(3, layer)
    mixed = normed * gain
    logistic = sigmoid(mixed)
    slope = logistic * (1.0 + mixed * (1.0 - logistic))
    mix, gg = norm_back(dot_nt(step, ctx.weight(PRJ, layer)[...]) * slope, normed, inverse, gain)
    smalls[3:4, :] = gg
    ctx.dz[...] = mix.astype(BF)
    edge_rows(ctx, ctx.dz, ctx.dzs, EDGE)


def last_outs(plan):
    t = plan.frames
    return dict(
        smalls=((16, D), F32),
        q3=((t, D + FH + D // 2), BF),
        k3=((t, FH + D // 2), BF),
        dr3=((t, D), F32),
        dz=((t, D), BF),
        dzs=((plan.halos * EDGE, D), BF),
    )


def call_last(plan, late, dy):
    t = plan.frames
    return launch(
        plan, lambda ctx: bwd_last(ctx, ctx.dy[...], 0), "last",
        dict(dy=dy, r4=late.r4, r3=late.r3, z=late.z, s2=late.s2),
        last_outs(plan),
        [(DN2, 0), (UP2, 0), (PRJ, 0)],
        dict(act=((t, F), BF)),
    )


def mix_time_back(ctx, layer):
    t = ctx.plan.frames
    grads, gated = ctx.ext, ctx.ext2
    weights = [ctx.taps(k, layer) for k in range(K)]
    block = 64
    taps = [[jnp.zeros((8, 128), F32) for _ in range(D // 128)] for _ in range(K)]
    for row in range(0, t, block):
        masks = tap_masks(ctx, row, block)
        for ci, c in enumerate(range(0, D, 128)):
            own = grads[8 + row : 8 + row + block, c : c + 128]
            total = jnp.zeros((block, 128), F32)
            for k in range(K):
                at = 8 + row + k - K // 2
                product = jnp.where(masks[k], own * gated[at : at + block, c : c + 128], 0.0)
                taps[k][ci] = taps[k][ci] + jnp.sum(product.reshape(block // 8, 8, 128), axis=0)
                window = grads[at : at + block, c : c + 128] * weights[K - 1 - k][:, c : c + 128]
                total = total + jnp.where(masks[k], window, 0.0)
            ctx.dg[row : row + block, c : c + 128] = total
    for k in range(K):
        for ci, c in enumerate(range(0, D, 128)):
            ctx.smalls[6 + k : 7 + k, c : c + 128] = jnp.sum(taps[k][ci], axis=0, keepdims=True)


def bwd_attend(ctx, layer):
    t = ctx.plan.frames
    fill_extended(ctx, ctx.ext, ctx.dz, ctx.dzh)
    fill_extended(ctx, ctx.ext2, ctx.g, ctx.gh)
    ctx.smalls[...] = ctx.smalls_in[...]
    mix_time_back(ctx, layer)
    gated = ctx.dg[...]
    act = ctx.act
    act[:, 0:D] = (gated * ctx.gs[...].astype(F32)).astype(BF)
    act[:, D : 2 * D] = (gated * ctx.gt[...].astype(F32)).astype(BF)
    half_copies(ctx, act, ctx.k2, ctx.q2, 0, 0, 2 * D, 1)
    normed, inverse = norm_stats(ctx.r2[...])
    branch, gg = norm_back(
        dot_nt(act[...], ctx.weight(EXP, layer)[...]), normed, inverse, ctx.small(2, layer)
    )
    ctx.smalls[2:3, :] = gg
    stream = ctx.dr3[...] + branch
    ctx.dr2[...] = stream
    step = stream.astype(BF)
    act[:, 0:D] = step
    half_copies(ctx, act.at[:, 0:D], ctx.k2, ctx.q2, D, D, D, 1)
    grad_o = ctx.do
    grad_o[...] = dot_nt(step, ctx.weight(OUT, layer)[...]).astype(BF)
    qkv, kvh, probs, p2 = ctx.qkv, ctx.kvh, ctx.probs, ctx.p2
    lane = lax.broadcasted_iota(jnp.int32, (t, 2 * HD), 1)
    laneh = lax.broadcasted_iota(jnp.int32, (ctx.plan.halos * W, 2 * HD), 1)
    scale = HD ** (-0.5)
    for p in range(H // 2):
        at = 2 * HD * p
        q = qkv[:, at : at + 2 * HD] * jnp.asarray(scale, BF)
        k = qkv[:, D + at : D + at + 2 * HD]
        v = qkv[:, 2 * D + at : 2 * D + at + 2 * HD]
        kh = kvh[:, at : at + 2 * HD]
        vh = kvh[:, D + at : D + at + 2 * HD]
        do = grad_o[:, at : at + 2 * HD]
        spread = do.astype(F32) * p2[:, at : at + 2 * HD].astype(F32)
        parts = []
        for e in range(2):
            mine = (lane // HD) == e
            dom = jnp.where(mine, do, jnp.zeros_like(do))
            delta = jnp.sum(jnp.where(mine, spread, 0.0), axis=-1, keepdims=True)
            po = probs[2 * p + e, :, 0:t]
            ph = probs[2 * p + e, :, t:]
            so = (po.astype(F32) * (dot_nt(dom, v) - delta)).astype(BF)
            sh = (ph.astype(F32) * (dot_nt(dom, vh) - delta)).astype(BF)
            parts.append(
                (
                    dot(so, k) + dot(sh, kh),
                    dot_tn(so, q),
                    dot_tn(sh, q),
                    dot_tn(po, do),
                    dot_tn(ph, do),
                )
            )
        one, two = parts
        ctx.dq[:, at : at + 2 * HD] = (jnp.where(lane < HD, one[0], two[0]) * scale).astype(BF)
        ctx.dkv[:, at : at + 2 * HD] = jnp.where(lane < HD, one[1], two[1])
        ctx.dkvh[:, at : at + 2 * HD] = jnp.where(laneh < HD, one[2], two[2]).astype(BF)
        ctx.dkv[:, D + at : D + at + 2 * HD] = jnp.where(lane < HD, one[3], two[3])
        ctx.dkvh[:, D + at : D + at + 2 * HD] = jnp.where(laneh < HD, one[4], two[4]).astype(BF)


def call_attend_back(plan, layer, first, mid, last, kvh, gh, dzh):
    t = plan.frames
    return launch(
        plan,
        lambda ctx: bwd_attend(ctx, layer),
        "attend_back",
        dict(
            dz=last.dz, dzh=dzh, dr3=last.dr3, smalls_in=last.smalls,
            g=mid.g, gh=gh, gs=mid.gs, gt=mid.gt, r2=mid.r2,
            probs=mid.probs, p2=mid.p2, qkv=first.qkv, kvh=kvh,
        ),
        dict(
            smalls=((16, D), F32),
            q2=((t, D + D // 2), BF),
            k2=((t, D + D // 2), BF),
            dr2=((t, D), F32),
            dq=((t, D), BF),
            dkv=((t, 2 * D), F32),
            dkvh=((plan.halos * W, 2 * D), BF),
        ),
        [(EXP, layer), (OUT, layer)],
        dict(
            ext=((t + 16, D), F32), ext2=((t + 16, D), F32), dg=((t, D), F32),
            act=((t, 2 * D), BF), do=((t, D), BF),
        ),
    )


def bwd_first(ctx, layer):
    t = ctx.plan.frames
    ctx.smalls[...] = ctx.smalls_in[...]
    grads, acc, back = ctx.act, ctx.acc, ctx.back
    grads[:, 0:D] = ctx.dq[...]
    acc[...] = ctx.dkv[...]
    if ctx.plan.halos == 1:
        at = pl.multiple_of((1 - ctx.core) * (t - W), W)
        acc[pl.ds(at, W), :] += back[...].astype(F32)
    else:
        acc[t - W : t, :] += back[0:W, :].astype(F32)
        acc[0:W, :] += back[W : 2 * W, :].astype(F32)
    grads[:, D : 3 * D] = acc[...].astype(BF)
    half_copies(ctx, grads.at[:, 0 : 3 * D], ctx.k1, ctx.q1, FH, D + FH, 3 * D, 1)
    normed, inverse = norm_stats(ctx.r1[...])
    branch, gg = norm_back(
        dot_nt(grads[:, 0 : 3 * D], ctx.weight(QKV, layer)[...]), normed, inverse, ctx.small(1, layer)
    )
    ctx.smalls[1:2, :] = gg
    stream = ctx.dr2[...] + branch
    step = (0.5 * stream).astype(BF)
    ctx.q1[:, 0:D] = step
    inner = feed_forward_back(ctx, step, UP1, DN1, layer, ctx.s1, ctx.k1, ctx.q1, D)
    normed, inverse = norm_stats(ctx.x[...].astype(F32))
    branch, gg = norm_back(inner, normed, inverse, ctx.small(0, layer))
    ctx.smalls[0:1, :] = gg
    ctx.ig[...] = (stream + branch).astype(BF)


def call_first_back(plan, layer, x, first, att, back):
    t = plan.frames
    return launch(
        plan,
        lambda ctx: bwd_first(ctx, layer),
        "first_back",
        dict(
            x=x, r1=first.r1, s1=first.s1, dr2=att.dr2, dq=att.dq, dkv=att.dkv, back=back,
            smalls_in=att.smalls,
        ),
        dict(
            smalls=((16, D), F32),
            q1=((t, D + FH + 3 * D // 2), BF),
            k1=((t, FH + 3 * D // 2), BF),
            ig=((t, D), BF),
        ),
        [(QKV, layer), (DN1, layer), (UP1, layer)],
        dict(act=((t, F), BF), acc=((t, 2 * D), F32)),
    )


SIDE = (2, 4, 128, D)


def both_tn(left, left_got, right, right_got):
    return dot_tn(left, right) + dot_tn(left_got, right_got)


def put_part(ref, value, q, at, col):
    width = value.shape[1]
    for b in range(2):
        ref[b, q, at : at + 64, col : col + width] = value[64 * b : 64 * (b + 1), :].astype(BF)


def call_ffn_bucket(plan, fwd, fwd_got, act, bwd, bwd_got, keep, hid_at):
    def body(ctx):
        side = ctx.scalars[SIDE1]
        step, step_got = ctx.bwd[:, 0:D], ctx.bwd_got[:, 0:D]
        hid, hid_got = ctx.fwd[:, hid_at : hid_at + D], ctx.fwd_got[:, hid_at : hid_at + D]
        for ref, a in ((ctx.send, 1 - side), (ctx.keep, side)):
            for q in range(4):
                at = pl.multiple_of(q * 256 + a * 128, 128)
                got = pl.multiple_of(2 * D + q * 256 + a * 128, 128)
                value = both_tn(
                    ctx.act_own[:, pl.ds(at, 128)], ctx.fwd_got[:, pl.ds(got, 128)], step, step_got
                )
                put_part(ref, value, q, 0, 0)
            at = pl.multiple_of(a * D, D)
            got = pl.multiple_of(D + a * D, D)
            value = both_tn(hid, hid_got, ctx.inner[:, pl.ds(at, D)], ctx.bwd_got[:, pl.ds(got, D)])
            for q in range(4):
                put_part(ref, value[q * 128 : (q + 1) * 128, :], q, 64, 0)

    return launch(
        plan, body, "ffn_bucket",
        dict(fwd=fwd, fwd_got=fwd_got, act_own=act, bwd=bwd, bwd_got=bwd_got, inner=keep),
        dict(send=(SIDE, BF), keep=(SIDE, BF)),
    )


def call_mid_bucket(plan, f, g):
    def body(ctx):
        side = ctx.scalars[SIDE1]
        at = pl.multiple_of(8 * ctx.core, 8)
        small = ctx.smalls[pl.ds(at, 8), :] + ctx.smalls_got[pl.ds(at, 8), :]
        small = jnp.concatenate([small, jnp.zeros((56, D), F32)], axis=0).astype(BF)

        def product(left, left_got, left_at, right, own_at, right_got, got_at, width, a):
            own = pl.multiple_of(own_at + a * width, 128)
            got = pl.multiple_of(got_at + a * width, 128)
            return both_tn(
                left[:, left_at : left_at + D], left_got[:, left_at : left_at + D],
                right[:, pl.ds(own, width)], right_got[:, pl.ds(got, width)],
            )

        for ref, a in ((ctx.send, 1 - side), (ctx.keep, side)):

            def place(value, at, col):
                for q in range(4):
                    put_part(ref, value[q * 128 : (q + 1) * 128, :], q, at, col)

            place(product(ctx.p1, ctx.p1_got, D, ctx.k1, FH, ctx.q1_got, D + FH, 384, a), 0, 0)
            place(product(ctx.p2, ctx.p2_got, 0, ctx.k2, D, ctx.q2_got, D, 128, a), 0, 384)
            place(product(ctx.p2, ctx.p2_got, D, ctx.k2, 0, ctx.q2_got, 0, 256, a), 64, 0)
            place(product(ctx.p3, ctx.p3_got, 0, ctx.k3, FH, ctx.q3_got, D + FH, 128, a), 64, 256)
            for q in range(4):
                for b in range(2):
                    ref[b, q, 64:128, 384:512] = small[:, q * 128 : (q + 1) * 128]

    return launch(
        plan, body, "mid_bucket",
        dict(
            p1=f.p1, p2=f.p2, p3=f.p3, k1=f.k1, k2=f.k2, k3=f.k3, smalls=f.smalls,
            p1_got=g.p1, p2_got=g.p2, p3_got=g.p3, q1_got=g.q1, q2_got=g.q2, q3_got=g.q3,
            smalls_got=g.smalls,
        ),
        dict(send=(SIDE, BF), keep=(SIDE, BF)),
    )


def exchange(plan, value, stage):
    pairs = []
    for core in range(2):
        bit = 1 if (core == 0) == (stage == 0) else 2
        pairs += [(core * 4 + i, core * 4 + (i ^ bit)) for i in range(4)]
    return lax.ppermute(value, MESH_AXES[:2], pairs)


def exchange_seq(value, bit):
    return lax.ppermute(value, MESH_AXES[2], [(i, i ^ bit) for i in range(4)])


def call_second(plan, keep, got):
    def body(ctx):
        side = ctx.scalars[SIDE2]
        for ref, at in ((ctx.send, 1 - side), (ctx.mine, side)):
            ref[...] = (ctx.keep[at].astype(F32) + ctx.got[at].astype(F32)).astype(BF)

    return launch(
        plan, body, "second", dict(keep=keep, got=got),
        dict(send=(SIDE[1:], BF), mine=(SIDE[1:], BF)),
    )


def call_third(plan, keeps, gots):
    count = len(keeps)

    def body(ctx):
        side = ctx.scalars[CHIP] // 2
        for ref, half in ((ctx.send, 1 - side), (ctx.mine, side)):
            at = pl.ds(2 * half, 2)
            for i in range(count):
                keep, got = getattr(ctx, "k%d" % i), getattr(ctx, "g%d" % i)
                ref[i] = (keep[at].astype(F32) + got[at].astype(F32)).astype(BF)

    ins = {"k%d" % i: v for i, v in enumerate(keeps)}
    ins.update({"g%d" % i: v for i, v in enumerate(gots)})
    shape = (count, 2, 128, D)
    return launch(plan, body, "third", ins, dict(send=(shape, BF), mine=(shape, BF)))


def call_fourth(plan, keep, got):
    count = keep.shape[0]

    def body(ctx):
        side = ctx.scalars[CHIP] % 2
        for ref, at in ((ctx.send, 1 - side), (ctx.mine, side)):
            for i in range(count):
                ref[i] = (ctx.keep[i, at].astype(F32) + ctx.got[i, at].astype(F32)).astype(BF)

    shape = (count, 128, D)
    return launch(plan, body, "fourth", dict(keep=keep, got=got), dict(send=(shape, BF), mine=(shape, BF)))


def call_total(plan, keep, got):
    def body(ctx):
        ctx.own[...] = (ctx.keep[...].astype(F32) + ctx.got[...].astype(F32)).astype(BF)

    return launch(plan, body, "total", dict(keep=keep, got=got), dict(own=(keep.shape, BF))).own


def call_pair(plan, own, got):
    def body(ctx):
        side = ctx.scalars[SIDE2]
        ctx.pair[side] = ctx.own[...]
        ctx.pair[1 - side] = ctx.got[...]

    return launch(plan, body, "pair", dict(own=own, got=got), dict(pair=((2,) + own.shape, BF))).pair


def swap(value):
    return lax.ppermute(value, MESH_AXES[0], [(0, 1), (1, 0)])


def to_layer(value, layer):
    return lax.ppermute(value, MESH_AXES[0], [(1 - layer, layer)])


def call_unpack(plan, kind, spots, groups):
    far = {}
    for layer in range(2):
        group, _ = spots[layer]
        for i, value in enumerate(groups[layer][group]):
            far["l%d_%d" % (layer, i)] = value
    if kind == 0:
        outs = dict(up=((128, F), F32), dn=((512, D), F32))
    else:
        outs = dict(
            qkv=((128, 3 * D), F32), out=((128, D), F32), exp=((128, 2 * D), F32),
            prj=((128, D), F32), sml=((16, 128), F32),
        )

    def body(ctx):
        stage = ctx.stage
        waits = []
        for i in range(4):
            for layer in range(2):
                bucket = spots[layer][1]
                source = getattr(ctx, "l%d_%d" % (layer, i))

                @pl.when(ctx.core == layer)
                def _(i=i, source=source, bucket=bucket):
                    for b in range(2):
                        pltpu.make_async_copy(
                            source.at[b, bucket], stage.at[i, b], ctx.sems[2 * i + b]
                        ).start()

            for b in range(2):
                waits.append(pltpu.make_async_copy(source.at[b, 0], stage.at[i, b], ctx.sems[2 * i + b]))
        for wait in waits:
            wait.wait()
        for source, (half, first) in enumerate(
            ((ctx.core, ctx.scalars[SIDE1]), (1 - ctx.core, ctx.scalars[OTHER1]))
        ):
            for which in range(2):
                a = first if which == 0 else 1 - first
                index = 2 * source + which
                for b in range(2):
                    rows = slice(64 * b, 64 * b + 64)
                    upper = stage[index, b, 0:64, :].astype(F32)
                    lower = stage[index, b, 64:128, :].astype(F32)
                    if kind == 0:
                        at = pl.multiple_of(half * 256 + a * 128 + b * 64, 64)
                        ctx.dn[pl.ds(at, 64), :] = upper
                        at = pl.multiple_of(half * FH + a * D, D)
                        ctx.up[rows, pl.ds(at, D)] = lower
                    else:
                        at = pl.multiple_of(half * 768 + a * 384, 128)
                        ctx.qkv[rows, pl.ds(at, 384)] = upper[:, 0:384]
                        at = pl.multiple_of(half * 256 + a * 128, 128)
                        ctx.out[rows, pl.ds(at, 128)] = upper[:, 384:512]
                        ctx.prj[rows, pl.ds(at, 128)] = lower[:, 256:384]
                        at = pl.multiple_of(half * 512 + a * 256, 256)
                        ctx.exp[rows, pl.ds(at, 256)] = lower[:, 0:256]
                        if which == 0 and b == 0:
                            at = pl.multiple_of(half * 8, 8)
                            ctx.sml[pl.ds(at, 8), :] = lower[0:8, 384:512]

    return launch(
        plan, body, "unpack", {}, outs, (), dict(stage=((4, 2, 128, D), BF)), far=far,
    )


def row_pairs(plan, k, core_of):
    pairs = []
    for chip in range(plan.seq):
        group, i = divmod(chip, plan.rows)
        target = group * plan.rows + (i ^ k)
        for core in core_of(i):
            pairs.append((core * plan.seq + chip, core * plan.seq + target))
    return pairs


def to_rows(plan, value):
    half = plan.rows // 2
    size = value.shape[1]

    def body(ctx):
        copies = []
        for k in range(plan.rows):
            copies.append(
                pltpu.make_async_copy(
                    ctx.value.at[ctx.scalars[ROW] ^ k], getattr(ctx, "piece%d" % k), ctx.sems[k]
                )
            )
        for copy in copies:
            copy.start()
        for copy in copies:
            copy.wait()

    outs = {"piece%d" % k: ((size, D), BF) for k in range(plan.rows)}
    pieces = launch(plan, body, "pick_rows", {}, outs, far=dict(value=value), limit=4).__dict__
    for k in range(1, plan.rows):
        pieces["piece%d" % k] = lax.ppermute(
            pieces["piece%d" % k], MESH_AXES[::2], row_pairs(plan, k, lambda i: (i // half,))
        )
    return pieces


def join_frames(ctx, target):
    plan = ctx.plan
    half = plan.rows // 2
    size = plan.frames // half
    for k in range(plan.rows):
        source = ctx.scalars[ROW] ^ k

        @pl.when(source // half == ctx.core)
        def _(k=k, source=source):
            at = pl.multiple_of((source % half) * size, size)
            target[pl.ds(at, size), :] = getattr(ctx, "piece%d" % k)[...]


def split_layers(plan, layer0, layer1):
    def body(ctx):
        @pl.when(ctx.core == 0)
        def _():
            ctx.keep[...] = ctx.layer0[...]
            ctx.send[...] = ctx.layer1[...]

        @pl.when(ctx.core != 0)
        def _():
            ctx.keep[...] = ctx.layer1[...]
            ctx.send[...] = ctx.layer0[...]

    shape = (plan.frames, D)
    out = launch(
        plan, body, "split", dict(layer0=layer0, layer1=layer1),
        dict(keep=(shape, BF), send=(shape, BF)), limit=8,
    )
    return out.keep, swap(out.send)


def deal_rows(plan, keep, got):
    half = plan.rows // 2
    size = plan.frames // half

    def body(ctx):
        for k in range(plan.rows):
            chip = ctx.scalars[ROW] ^ k
            at = pl.multiple_of((chip % half) * size, size)
            piece = getattr(ctx, "piece%d" % k)

            @pl.when(chip // half == ctx.core)
            def _(piece=piece, at=at):
                piece[...] = ctx.keep[pl.ds(at, size), :]

            @pl.when(chip // half != ctx.core)
            def _(piece=piece, at=at):
                piece[...] = ctx.got[pl.ds(at, size), :]

    outs = {"piece%d" % k: ((size, D), BF) for k in range(plan.rows)}
    pieces = launch(plan, body, "deal_rows", dict(keep=keep, got=got), outs, limit=8).__dict__
    for k in range(1, plan.rows):
        pieces["piece%d" % k] = lax.ppermute(
            pieces["piece%d" % k], MESH_AXES[::2], row_pairs(plan, k, lambda i: (0, 1))
        )
    return pieces


def place_rows(plan, pieces, dtype):
    def body(ctx):
        for k in range(plan.rows):
            ctx.all[ctx.scalars[ROW] ^ k] = getattr(ctx, "piece%d" % k)[...].astype(dtype)

    shape = (plan.rows,) + pieces["piece0"].shape
    return launch(plan, body, "place_rows", pieces, dict(all=(shape, dtype)), limit=8).all


def halo_exchange(plan, send, rows):
    if plan.halos == 1:
        return swap(send)
    return jnp.concatenate(
        [
            lax.ppermute(send[0:rows], MESH_AXES[::2], plan.to_right),
            lax.ppermute(send[rows:], MESH_AXES[::2], plan.to_left),
        ],
        axis=0,
    )


def halo_return(plan, grads, rows):
    if plan.halos == 1:
        return swap(grads)
    return jnp.concatenate(
        [
            lax.ppermute(grads[rows:], MESH_AXES[::2], plan.to_left),
            lax.ppermute(grads[0:rows], MESH_AXES[::2], plan.to_right),
        ],
        axis=0,
    )


def plain_gradients(plan, layers):
    def whole(keep, send):
        return jnp.where(
            plan.core == 0,
            jnp.concatenate([keep, send], axis=1),
            jnp.concatenate([send, keep], axis=1),
        )

    stacked = []
    for f in layers:
        p1, p2, p3, q1, q2, q3, k1, k2, k3 = f.p1, f.p2, f.p3, f.q1, f.q2, f.q3, f.k1, f.k2, f.k3
        operands = (
            (p1[:, :D], whole(k1[:, :FH], q1[:, D : D + FH])),
            (whole(f.a1, p1[:, 2 * D :]), q1[:, :D]),
            (p1[:, D : 2 * D], whole(k1[:, FH:], q1[:, D + FH :])),
            (p2[:, :D], whole(k2[:, D:], q2[:, D:])),
            (p2[:, D:], whole(k2[:, :D], q2[:, :D])),
            (p3[:, :D], whole(k3[:, FH:], q3[:, D + FH :])),
            (p3[:, D : 2 * D], whole(k3[:, :FH], q3[:, D : D + FH])),
            (whole(f.a2, p3[:, 2 * D :]), q3[:, :D]),
        )
        grads = [dot_tn(a, b).astype(BF) for a, b in operands]
        grads.append(f.smalls[0:6].astype(BF))
        grads.append(f.smalls[6:15].astype(BF))
        stacked.append(grads)
    result = []
    for index in range(10):
        both = jnp.stack([stacked[0][index], stacked[1][index]])
        mine = lax.psum_scatter(both, MESH_AXES[0], scatter_dimension=0, tiled=False)
        dim = 0 if index < 8 else 1
        mine = lax.psum_scatter(mine, MESH_AXES[2], scatter_dimension=dim, tiled=True)
        result.append(lax.psum(mine, MESH_AXES[1]).astype(F32))
    up1, dn1, qkv, out, exp, prj, up2, dn2, gains, taps = result
    return up1, dn1, qkv, out, exp, taps, prj, up2, dn2, gains


def make_plan(mesh_shape, inputs, lengths, weights, taps, gains):
    plan = SimpleNamespace(token=None)
    plan.rows = inputs.shape[0]
    local = inputs.shape[1]
    plan.dp, plan.seq = mesh_shape[MESH_AXES[1]], mesh_shape[MESH_AXES[2]]
    plan.frames = plan.rows * local // 2
    plan.halos = 1 if plan.seq == plan.rows else 2
    plan.direct = plan.dp == 4 and plan.seq == 4
    plan.blocks = plan.seq if plan.direct else 1
    core, replica, chip = (lax.axis_index(name) for name in MESH_AXES)
    plan.core = core
    row = chip % plan.rows
    fast, slow = replica % 2, (replica // 2) % 2
    ends = jnp.cumsum(lax.dynamic_index_in_dim(lengths, row, 0, keepdims=False))
    plan.scalars = jnp.concatenate(
        [
            jnp.stack(
                [
                    core,
                    row,
                    ((chip // plan.rows) * 2 + core) * plan.frames,
                    jnp.asarray(local * plan.seq, jnp.int32),
                    jnp.where(core == 0, fast, slow),
                    jnp.where(core == 0, slow, fast),
                    jnp.where(core == 0, slow, fast),
                    chip,
                ]
            ).astype(jnp.int32),
            ends.astype(jnp.int32),
        ]
    )
    seq = plan.seq
    plan.to_right = [(q, seq + q) for q in range(seq)]
    plan.to_right += [(seq + q, q + plan.rows) for q in range(seq - plan.rows)]
    plan.to_left = [(b, a) for a, b in plan.to_right]
    plan.own = [w[0] for w in weights]
    plan.small_own = jnp.concatenate(
        [gains[0].astype(F32), taps[0].astype(F32), jnp.zeros((1, D), F32)], axis=0
    )
    return plan


def per_device(
    mesh_shape,
    inputs,
    cotangent,
    lengths,
    ffn_one_up,
    ffn_one_down,
    attn_project,
    attn_output,
    conv_expand,
    conv_depthwise,
    conv_project,
    ffn_two_up,
    ffn_two_down,
    norm_gains,
):
    matrices = (
        ffn_one_up, ffn_one_down, attn_project, attn_output, conv_expand, conv_project, ffn_two_up,
        ffn_two_down,
    )
    plan = make_plan(mesh_shape, inputs, lengths, matrices, conv_depthwise, norm_gains)
    pieces = to_rows(plan, inputs)
    plan.small_other = swap(plan.small_own)
    plan.other = [swap(w) for w in plan.own]

    first0 = call_first(plan, pieces)
    kvh0 = halo_exchange(plan, first0.kvs, W)
    mid0 = call_attend(plan, 0, first0, kvh0)
    gh0 = halo_exchange(plan, mid0.gsend, EDGE)
    turn = call_conv_first(plan, mid0, gh0)
    kvh1 = halo_exchange(plan, turn.kvs, W)
    pieces = to_rows(plan, cotangent)
    mid1 = call_attend(plan, 1, turn, kvh1)
    gh1 = halo_exchange(plan, mid1.gsend, EDGE)
    end = call_conv_last(plan, mid1, gh1, pieces)
    dzh1 = halo_exchange(plan, end.dzs, EDGE)
    direct = plan.direct

    def got_of(value):
        return swap(value) if direct else None

    p1g1, p2g1, p3g1, q3g1 = got_of(turn.p1), got_of(mid1.p2), got_of(end.p3), got_of(end.q3)
    if direct:
        two1 = call_ffn_bucket(plan, end.p3, p3g1, end.a2, end.q3, q3g1, end.k3, D)
        two1.got = exchange(plan, two1.send, 0)
    att1 = call_attend_back(plan, 1, turn, mid1, end, kvh1, gh1, dzh1)
    back1 = halo_return(plan, att1.dkvh, W)
    if direct:
        two1s = call_second(plan, two1.keep, two1.got)
        two1s.got = exchange(plan, two1s.send, 1)
    beg1 = call_first_back(plan, 1, turn.y, turn, att1, back1)
    own1 = SimpleNamespace(
        p1=turn.p1, a1=turn.a1, p2=mid1.p2, p3=end.p3, a2=end.a2, q3=end.q3, k3=end.k3,
        q2=att1.q2, k2=att1.k2, q1=beg1.q1, k1=beg1.k1, smalls=beg1.smalls,
    )
    if direct:
        got1 = SimpleNamespace(
            p1=p1g1, p2=p2g1, p3=p3g1, q3=q3g1, q2=swap(att1.q2), q1=swap(beg1.q1),
            smalls=swap(beg1.smalls),
        )
        mid1b = call_mid_bucket(plan, own1, got1)
        mid1b.got = exchange(plan, mid1b.send, 0)
        one1 = call_ffn_bucket(plan, turn.p1, p1g1, turn.a1, beg1.q1, got1.q1, beg1.k1, 0)
        one1.got = exchange(plan, one1.send, 0)
    last0 = call_last(plan, turn, beg1.ig)
    dzh0 = halo_exchange(plan, last0.dzs, EDGE)
    p1g0, p2g0, p3g0, q3g0 = got_of(first0.p1), got_of(mid0.p2), got_of(turn.p3), got_of(last0.q3)
    if direct:
        mid1s = call_second(plan, mid1b.keep, mid1b.got)
        mid1s.got = exchange(plan, mid1s.send, 1)
        two0 = call_ffn_bucket(plan, turn.p3, p3g0, turn.a2, last0.q3, q3g0, last0.k3, D)
        two0.got = exchange(plan, two0.send, 0)
        one1s = call_second(plan, one1.keep, one1.got)
        one1s.got = exchange(plan, one1s.send, 1)
    att0 = call_attend_back(plan, 0, first0, mid0, last0, kvh0, gh0, dzh0)
    back0 = halo_return(plan, att0.dkvh, W)
    if direct:
        seq1 = call_third(
            plan, [two1s.mine, mid1s.mine, one1s.mine], [two1s.got, mid1s.got, one1s.got]
        )
        seq1.got = exchange_seq(seq1.send, 2)
        two0s = call_second(plan, two0.keep, two0.got)
        two0s.got = exchange(plan, two0s.send, 1)
    beg0 = call_first_back(plan, 0, first0.x, first0, att0, back0)
    own0 = SimpleNamespace(
        p1=first0.p1, a1=first0.a1, p2=mid0.p2, p3=turn.p3, a2=turn.a2, q3=last0.q3, k3=last0.k3,
        q2=att0.q2, k2=att0.k2, q1=beg0.q1, k1=beg0.k1, smalls=beg0.smalls,
    )
    if direct:
        got0 = SimpleNamespace(
            p1=p1g0, p2=p2g0, p3=p3g0, q3=q3g0, q2=swap(att0.q2), q1=swap(beg0.q1),
            smalls=swap(beg0.smalls),
        )
        mid0b = call_mid_bucket(plan, own0, got0)
        mid0b.got = exchange(plan, mid0b.send, 0)
        one0 = call_ffn_bucket(plan, first0.p1, p1g0, first0.a1, beg0.q1, got0.q1, beg0.k1, 0)
        one0.got = exchange(plan, one0.send, 0)
        seq1b = call_fourth(plan, seq1.mine, seq1.got)
        seq1b.got = exchange_seq(seq1b.send, 1)
        mid0s = call_second(plan, mid0b.keep, mid0b.got)
        mid0s.got = exchange(plan, mid0s.send, 1)
    keep, got = split_layers(plan, turn.y, end.y)
    keep_ig, got_ig = split_layers(plan, beg0.ig, beg1.ig)
    act_pieces = deal_rows(plan, keep, got)
    if direct:
        own_sum1 = call_total(plan, seq1b.mine, seq1b.got)
        part_got1 = exchange(plan, own_sum1, 1)
        one0s = call_second(plan, one0.keep, one0.got)
        one0s.got = exchange(plan, one0s.send, 1)
        seq0 = call_third(plan, [two0s.mine, mid0s.mine], [two0s.got, mid0s.got])
        seq0.got = exchange_seq(seq0.send, 2)
        pair1 = call_pair(plan, own_sum1, part_got1)
        pair_got1 = exchange(plan, pair1, 0)
    ig_pieces = deal_rows(plan, keep_ig, got_ig)
    if direct:
        seq0c = call_third(plan, [one0s.mine], [one0s.got])
        seq0c.got = exchange_seq(seq0c.send, 2)
        seq0b = call_fourth(plan, seq0.mine, seq0.got)
        seq0b.got = exchange_seq(seq0b.send, 1)
    activations = place_rows(plan, act_pieces, BF)
    if direct:
        seq0d = call_fourth(plan, seq0c.mine, seq0c.got)
        seq0d.got = exchange_seq(seq0d.send, 1)
        own_sum0 = call_total(plan, seq0b.mine, seq0b.got)
        part_got0 = exchange(plan, own_sum0, 1)
        own_sum0c = call_total(plan, seq0d.mine, seq0d.got)
        part_got0c = exchange(plan, own_sum0c, 1)
        pair0 = call_pair(plan, own_sum0, part_got0)
        pair_got0 = exchange(plan, pair0, 0)
        pair0c = call_pair(plan, own_sum0c, part_got0c)
        pair_got0c = exchange(plan, pair0c, 0)
    input_grads = place_rows(plan, ig_pieces, F32)
    if direct:
        def finished(pair, pair_got, layer):
            return pair, pair_got, to_layer(pair, layer), to_layer(pair_got, layer)

        groups = [
            [finished(pair0, pair_got0, 0), finished(pair0c, pair_got0c, 0)],
            [finished(pair1, pair_got1, 1)],
        ]
        two = call_unpack(plan, 0, ((0, 0), (0, 0)), groups)
        middle = call_unpack(plan, 1, ((0, 1), (0, 1)), groups)
        one = call_unpack(plan, 0, ((1, 0), (0, 2)), groups)
        results = (
            one.up, one.dn, middle.qkv, middle.out, middle.exp, middle.sml[6:15], middle.prj,
            two.up, two.dn, middle.sml[0:6],
        )
    else:
        results = plain_gradients(plan, (own0, own1))
    return (activations[None], input_grads[None]) + tuple(r[None] for r in results)


def solution(mesh):
    section, dp, seq = MESH_AXES
    whole = P(section, None, None)
    sliced = P(section, seq, None)
    across = P(section, None, seq)
    framed = P(section, dp, seq, None)
    return jax.shard_map(
        functools.partial(per_device, dict(mesh.shape)),
        mesh=mesh,
        in_specs=(P(dp, seq, None), P(dp, seq, None), P(dp, None)) + (whole,) * 10,
        out_specs=(framed, framed) + (sliced,) * 5 + (across,) + (sliced,) * 3 + (across,),
        check_vma=False,
    )
```

```python
import functools
from types import SimpleNamespace

import jax
import jax.numpy as jnp
from jax import lax
from jax.experimental import pallas as pl
from jax.experimental.pallas import tpu as pltpu
from jax.sharding import PartitionSpec as P

D = 512
H = 8
HD = 64
F = 2048
FH = F // 2
K = 9
W = 128
UTT = 4
EPSILON = 1e-05
MASKED = -1e30
EDGE = 16
Q2_AT = D + FH + 3 * D // 2
CHUNK = 512
MIB = 1024 * 1024
COST = 10**10
LIMITS = (16, 16, 20, 20, 16, 16, 16, 16)
MESH_AXES = ("section", "dp", "seq")

BF = jnp.bfloat16
F32 = jnp.float32

UP1, DN1, QKV, OUT, EXP, PRJ, UP2, DN2 = range(8)


def dot(a, b):
    return jnp.dot(a, b, preferred_element_type=F32)


def dot_nt(a, b):
    return lax.dot_general(a, b, (((1,), (1,)), ((), ())), preferred_element_type=F32)


def dot_tn(a, b):
    return lax.dot_general(a, b, (((0,), (0,)), ((), ())), preferred_element_type=F32)


def sigmoid(v):
    return 0.5 * jnp.tanh(0.5 * v) + 0.5


def norm_stats(v):
    centred = v - jnp.mean(v, axis=-1, keepdims=True)
    inverse = lax.rsqrt(jnp.mean(centred * centred, axis=-1, keepdims=True) + EPSILON)
    return centred * inverse, inverse


def norm_back(upstream, normed, inverse, gain):
    gain_grad = jnp.sum(upstream * normed, axis=0, keepdims=True)
    scaled = upstream * gain
    value_grad = inverse * (
        scaled
        - jnp.mean(scaled, axis=-1, keepdims=True)
        - normed * jnp.mean(scaled * normed, axis=-1, keepdims=True)
    )
    return value_grad, gain_grad


class Place:
    def __init__(self, plan, lengths):
        core, replica, chip = (lax.axis_index(name) for name in MESH_AXES)
        self.core, self.chip = core, chip
        self.row = lax.rem(chip, plan.rows)
        self.first = (lax.div(chip, plan.rows) * 2 + core) * plan.frames
        self.length = plan.length
        self.fast = lax.rem(replica, 2)
        self.slow = lax.rem(lax.div(replica, 2), 2)
        self.side1 = jnp.where(core == 0, self.fast, self.slow)
        self.side2 = jnp.where(core == 0, self.slow, self.fast)
        self.ends = []
        total = 0
        for u in range(UTT):
            total = total + lengths[self.row, u]
            self.ends.append(total)


class Ctx:
    def __init__(self, plan, place, table, held, waits):
        self.__dict__.update(place.__dict__)
        self.__dict__.update(table)
        self.plan = plan
        self.held = held
        self.waits = waits

    def weight(self, matrix, layer, part=None):
        queue = self.waits[(matrix, layer)]
        for index in range(len(queue)):
            if queue[index] is not None and (part is None or part == index):
                queue[index].wait()
                queue[index] = None
        return self.held[(matrix, layer)]

    def small(self, row, layer):
        mine = self.core == layer
        return jnp.where(mine, self.small_own[row : row + 1, :], self.small_other[row : row + 1, :])

    def taps(self, tap, layer):
        return self.small(6 + tap, layer)

    def seg(self, pos):
        total = jnp.zeros(pos.shape, jnp.int32)
        for u in range(UTT):
            total = total + (pos >= self.ends[u]).astype(jnp.int32)
        return total


def parts_of(matrix, shape):
    if matrix in (UP1, UP2):
        return [(slice(None), pl.ds(c, CHUNK)) for c in range(0, F, CHUNK)]
    if matrix in (DN1, DN2):
        return [(pl.ds(c, CHUNK), slice(None)) for c in range(0, F, CHUNK)]
    return [(slice(None), slice(None))]


def launch(plan, body, name, ins, outs, weights=(), scratch=None, far=None, results=None, settle=(),
           limit=16):
    scratch, far, results = scratch or {}, far or {}, results or {}
    near = dict(ins)
    near.update({"settle%d" % i: v for i, v in enumerate(settle)})
    if weights:
        near.update(small_own=plan.small_own, small_other=plan.small_other)
    if plan.token is not None:
        near.update(token_in=plan.token)
    pinned = [pltpu.with_memory_space_constraint(v, pltpu.VMEM) for v in near.values()]
    operands = [plan.lengths] + pinned
    operands += [pltpu.with_memory_space_constraint(v, pltpu.HBM) for v in far.values()]
    in_specs = [pl.BlockSpec(memory_space=pltpu.SMEM)]
    in_specs += [pl.BlockSpec(memory_space=pltpu.VMEM)] * len(near)
    in_specs += [pl.BlockSpec(memory_space=pl.ANY)] * len(far)
    copies = []
    for matrix, layer in weights:
        operands += [
            pltpu.with_memory_space_constraint(plan.own[matrix], pltpu.HBM),
            plan.other[matrix],
        ]
        in_specs += [pl.BlockSpec(memory_space=pl.ANY)] * 2
        copies.append(parts_of(matrix, plan.own[matrix].shape))
    held_shapes = [pltpu.VMEM(plan.own[m].shape, BF) for m, _ in weights]
    out_shape = [pltpu.VMEM(*s) for s in outs.values()]
    out_shape += [jax.ShapeDtypeStruct(*s) for s in results.values()]
    out_shape += [pltpu.VMEM((8, 128), jnp.int32)]
    out_specs = [pl.BlockSpec(memory_space=pltpu.VMEM)] * len(out_shape)
    sems = max(sum(len(c) for c in copies), 1) + 24

    def kernel(*refs):
        refs = list(refs)
        place = Place(plan, refs.pop(0))
        table = {}
        for n in list(near) + list(far):
            table[n] = refs.pop(0)
        sources = [(refs.pop(0), refs.pop(0)) for _ in weights]
        for n in list(outs) + list(results):
            table[n] = refs.pop(0)
        refs.pop(0)
        for n in scratch:
            table[n] = refs.pop(0)
        held_refs = [refs.pop(0) for _ in weights]
        sem = refs.pop(0)
        core = place.core
        held, waits = {}, {}
        for pair in weights:
            waits[pair] = []
        count = 0
        for part in range(max([len(c) for c in copies], default=0)):
            for pair, (own, other), into, slices in zip(weights, sources, held_refs, copies):
                held[pair] = into
                if part >= len(slices):
                    continue
                at = slices[part]

                @pl.when(core == pair[1])
                def _(own=own, into=into, at=at, count=count):
                    pltpu.make_async_copy(own.at[at], into.at[at], sem.at[count]).start()

                @pl.when(core != pair[1])
                def _(other=other, into=into, at=at, count=count):
                    pltpu.make_async_copy(other.at[at], into.at[at], sem.at[count]).start()

                waits[pair].append(pltpu.make_async_copy(own.at[at], into.at[at], sem.at[count]))
                count += 1
        ctx = Ctx(plan, place, table, held, waits)
        ctx.sems = [sem.at[sems - 24 + i] for i in range(24)]
        body(ctx)
        for pair in weights:
            ctx.weight(*pair)

    made = pl.pallas_call(
        kernel,
        out_shape=out_shape,
        in_specs=in_specs,
        out_specs=out_specs,
        scratch_shapes=[pltpu.VMEM(*s) for s in scratch.values()]
        + held_shapes
        + [pltpu.SemaphoreType.DMA((sems,))],
        compiler_params=pltpu.CompilerParams(vmem_limit_bytes=limit * MIB),
        cost_estimate=pl.CostEstimate(flops=COST, transcendentals=0, bytes_accessed=1),
        name=name,
    )(*operands)
    plan.token = made[-1]
    return SimpleNamespace(**dict(zip(list(outs) + list(results), made)))


def half_copies(ctx, value_ref, keep_ref, send_ref, keep_at, send_at, total, blocks):
    width = total // (2 * blocks)
    for j in range(blocks):
        mine = pl.multiple_of(j * 2 * width + ctx.core * width, width)
        theirs = pl.multiple_of(j * 2 * width + (1 - ctx.core) * width, width)
        keep_ref[:, keep_at + j * width : keep_at + (j + 1) * width] = value_ref[:, pl.ds(mine, width)]
        send_ref[:, send_at + j * width : send_at + (j + 1) * width] = value_ref[
            :, pl.ds(theirs, width)
        ]


def edge_rows(ctx, value_ref, send_ref, rows):
    frames = value_ref.shape[0]
    if ctx.plan.halos == 1:
        at = pl.multiple_of((1 - ctx.core) * (frames - rows), rows)
        send_ref[...] = value_ref[pl.ds(at, rows), :]
    else:
        send_ref[0:rows, :] = value_ref[frames - rows : frames, :]
        send_ref[rows : 2 * rows, :] = value_ref[0:rows, :]


def halo_starts(ctx, rows, frames):
    before = ctx.first - rows
    after = ctx.first + frames
    if ctx.plan.halos == 1:
        return [jnp.where(ctx.core == 0, after, before)]
    return [before, after]


def feed_forward(ctx, hidden, up, down, layer, keep_ref, send_ref, send_at, slope_ref):
    frames = hidden.shape[0]
    total = jnp.zeros((frames, D), F32)
    for part, c in enumerate(range(0, F, CHUNK)):
        at = slice(c, c + CHUNK)
        inner = dot(hidden, ctx.weight(up, layer, part)[:, at])
        logistic = sigmoid(inner)
        active = (inner * logistic).astype(BF)
        slope_ref[:, at] = (logistic * (1.0 + inner * (1.0 - logistic))).astype(BF)
        ctx.act[:, at] = active
        total = total + dot(active, ctx.weight(down, layer, part)[at, :])
    half_copies(ctx, ctx.act, keep_ref, send_ref, 0, send_at, F, ctx.plan.blocks)
    return total


def fwd_first(ctx, x, layer):
    normed, _ = norm_stats(x)
    hidden = (normed * ctx.small(0, layer)).astype(BF)
    ctx.p1[:, 0:D] = hidden
    ffn = feed_forward(ctx, hidden, UP1, DN1, layer, ctx.a1, ctx.p1, 2 * D, ctx.s1)
    r1 = x + 0.5 * ffn
    ctx.r1[...] = r1
    normed, _ = norm_stats(r1)
    hidden = (normed * ctx.small(1, layer)).astype(BF)
    ctx.p1[:, D : 2 * D] = hidden
    ctx.qkv[...] = dot(hidden, ctx.weight(QKV, layer)[...]).astype(BF)
    edge_rows(ctx, ctx.qkv.at[:, D : 3 * D], ctx.kvs, W)


def first_outs(plan):
    t = plan.frames
    return dict(
        p1=((t, 2 * D + FH), BF),
        a1=((t, FH), BF),
        s1=((t, F), BF),
        r1=((t, D), F32),
        qkv=((t, 3 * D), BF),
        kvs=((plan.halos * W, 2 * D), BF),
    )


def call_first(plan, pieces):
    def body(ctx):
        join_frames(ctx, ctx.x)
        fwd_first(ctx, ctx.x[...].astype(F32), 0)

    t = plan.frames
    return launch(
        plan, body, "first", pieces, dict(x=((t, D), BF), **first_outs(plan)),
        [(UP1, 0), (DN1, 0), (QKV, 0)], dict(act=((t, F), BF)), limit=LIMITS[0],
    )


def allowed_bias(ctx, key_start, keys):
    frames = ctx.plan.frames
    shape = (frames, keys)
    query = ctx.first + lax.broadcasted_iota(jnp.int32, shape, 0)
    key = key_start + lax.broadcasted_iota(jnp.int32, shape, 1)
    near = jnp.abs(query - key) <= W
    inside = (key >= 0) & (key < ctx.length)
    same = ctx.seg(query) == ctx.seg(key)
    return jnp.where(near & inside & same, 0.0, MASKED).astype(F32)


def fwd_attend(ctx, layer):
    t = ctx.plan.frames
    halos = ctx.plan.halos
    qkv, kvh, probs, p2, bias = ctx.qkv, ctx.kvh, ctx.probs, ctx.p2, ctx.bias
    starts = halo_starts(ctx, W, t)
    bias[:, 0:t] = allowed_bias(ctx, ctx.first, t)
    for h in range(halos):
        bias[:, t + h * W : t + (h + 1) * W] = allowed_bias(ctx, starts[h], W)
    lane = lax.broadcasted_iota(jnp.int32, (t, 2 * HD), 1)
    for p in range(H // 2):
        at = 2 * HD * p
        q = qkv[:, at : at + 2 * HD] * jnp.asarray(HD ** (-0.5), BF)
        k = qkv[:, D + at : D + at + 2 * HD]
        v = qkv[:, 2 * D + at : 2 * D + at + 2 * HD]
        kh = kvh[:, at : at + 2 * HD]
        vh = kvh[:, D + at : D + at + 2 * HD]
        outs = []
        for e in range(2):
            mine = (lane // HD) == e
            qm = jnp.where(mine, q, jnp.zeros_like(q))
            so = dot_nt(qm, k) + bias[:, 0:t]
            sh = dot_nt(qm, kh) + bias[:, t:]
            peak = jnp.maximum(
                jnp.max(so, axis=-1, keepdims=True), jnp.max(sh, axis=-1, keepdims=True)
            )
            eo = jnp.exp(so - peak)
            eh = jnp.exp(sh - peak)
            scale = 1.0 / (
                jnp.sum(eo, axis=-1, keepdims=True) + jnp.sum(eh, axis=-1, keepdims=True)
            )
            po = (eo * scale).astype(BF)
            ph = (eh * scale).astype(BF)
            probs[2 * p + e, :, 0:t] = po
            probs[2 * p + e, :, t:] = ph
            outs.append(dot(po, v) + dot(ph, vh))
        p2[:, at : at + 2 * HD] = jnp.where(lane < HD, outs[0], outs[1]).astype(BF)
    r2 = ctx.r1[...] + dot(p2[:, 0:D], ctx.weight(OUT, layer)[...])
    ctx.r2[...] = r2
    normed, _ = norm_stats(r2)
    hidden = (normed * ctx.small(2, layer)).astype(BF)
    p2[:, D : 2 * D] = hidden
    expand = ctx.weight(EXP, layer)
    linear = dot(hidden, expand[:, 0:D])
    logistic = sigmoid(dot(hidden, expand[:, D : 2 * D]))
    gated = linear * logistic
    ctx.g[...] = gated.astype(BF)
    ctx.gs[...] = logistic.astype(BF)
    ctx.gt[...] = (gated * (1.0 - logistic)).astype(BF)
    edge_rows(ctx, ctx.g, ctx.gsend, EDGE)


def call_attend(plan, layer, first, kvh, settle=()):
    t = plan.frames
    keys = t + plan.halos * W
    return launch(
        plan,
        lambda ctx: fwd_attend(ctx, layer),
        "attend",
        dict(qkv=first.qkv, kvh=kvh, r1=first.r1),
        dict(
            probs=((H, t, keys), BF),
            p2=((t, 2 * D), BF),
            r2=((t, D), F32),
            g=((t, D), BF),
            gs=((t, D), BF),
            gt=((t, D), BF),
            gsend=((plan.halos * EDGE, D), BF),
        ),
        [(OUT, layer), (EXP, layer)],
        dict(bias=((t, keys), F32)),
        settle=settle, limit=LIMITS[1],
    )


def fill_extended(ctx, ext, own, halo):
    t = ctx.plan.frames
    before = halo[EDGE - 8 : EDGE, :]
    after = halo[0:8, :] if ctx.plan.halos == 1 else halo[EDGE : EDGE + 8, :]
    ext[0:8, :] = before.astype(F32)
    ext[8 : 8 + t, :] = own[...].astype(F32)
    ext[8 + t : 16 + t, :] = after.astype(F32)


def tap_masks(ctx, row, rows):
    pos = ctx.first + row + lax.broadcasted_iota(jnp.int32, (rows, 128), 0)
    here = ctx.seg(pos)
    masks = []
    for k in range(K):
        there = pos + (k - K // 2)
        masks.append((ctx.seg(there) == here) & (there >= 0) & (there < ctx.length))
    return masks


def mix_time(ctx, ext, z_ref, layer):
    t = ctx.plan.frames
    taps = [ctx.taps(k, layer) for k in range(K)]
    block = 64
    for row in range(0, t, block):
        masks = tap_masks(ctx, row, block)
        for c in range(0, D, 128):
            total = jnp.zeros((block, 128), F32)
            for k in range(K):
                at = 8 + row + k - K // 2
                window = ext[at : at + block, c : c + 128] * taps[k][:, c : c + 128]
                total = total + jnp.where(masks[k], window, 0.0)
            z_ref[row : row + block, c : c + 128] = total


def valid_rows(ctx):
    pos = ctx.first + lax.broadcasted_iota(jnp.int32, (ctx.plan.frames, 1), 0)
    return (pos < ctx.ends[UTT - 1]).astype(F32)


def fwd_conv(ctx, layer):
    fill_extended(ctx, ctx.ext, ctx.g, ctx.gh)
    mix_time(ctx, ctx.ext, ctx.z, layer)
    normed, _ = norm_stats(ctx.z[...])
    mixed = normed * ctx.small(3, layer)
    active = (mixed * sigmoid(mixed)).astype(BF)
    ctx.p3[:, 0:D] = active
    r3 = ctx.r2[...] + dot(active, ctx.weight(PRJ, layer)[...])
    ctx.r3[...] = r3
    normed, _ = norm_stats(r3)
    hidden = (normed * ctx.small(4, layer)).astype(BF)
    ctx.p3[:, D : 2 * D] = hidden
    ffn = feed_forward(ctx, hidden, UP2, DN2, layer, ctx.a2, ctx.p3, 2 * D, ctx.s2)
    r4 = r3 + 0.5 * ffn
    ctx.r4[...] = r4
    normed, _ = norm_stats(r4)
    result = (normed * ctx.small(5, layer) * valid_rows(ctx)).astype(BF)
    ctx.y[...] = result
    return result


def conv_outs(plan):
    t = plan.frames
    return dict(
        z=((t, D), F32),
        p3=((t, 2 * D + FH), BF),
        a2=((t, FH), BF),
        s2=((t, F), BF),
        r3=((t, D), F32),
        r4=((t, D), F32),
        y=((t, D), BF),
    )


def conv_scratch(plan):
    t = plan.frames
    return dict(ext=((t + 16, D), F32), act=((t, F), BF))


def call_conv_first(plan, mid, gh):
    def body(ctx):
        fwd_first(ctx, fwd_conv(ctx, 0).astype(F32), 1)

    return launch(
        plan, body, "conv_first", dict(g=mid.g, gh=gh, r2=mid.r2),
        dict(conv_outs(plan), **first_outs(plan)),
        [(PRJ, 0), (UP2, 0), (DN2, 0), (UP1, 1), (DN1, 1), (QKV, 1)],
        conv_scratch(plan), limit=LIMITS[2],
    )


def call_conv_last(plan, mid, gh, pieces, settle):
    outs = dict(conv_outs(plan), **last_outs(plan))
    del outs["p3"], outs["q3"]
    outs["c3"] = ((plan.frames, 2 * D + FH + D + FH + D // 2), BF)

    def body(ctx):
        ctx.p3, ctx.q3 = ctx.c3.at[:, 0 : 2 * D + FH], ctx.c3.at[:, 2 * D + FH :]
        fwd_conv(ctx, 1)
        join_frames(ctx, ctx.dy)
        bwd_last(ctx, ctx.dy[...], 1)

    return launch(
        plan, body, "conv_last", dict(g=mid.g, gh=gh, r2=mid.r2, **pieces), outs,
        [(PRJ, 1), (UP2, 1), (DN2, 1)],
        dict(conv_scratch(plan), dy=((plan.frames, D), BF)), settle=settle, limit=LIMITS[3],
    )


def feed_forward_back(ctx, step, up, down, layer, slope_ref, keep_ref, send_ref, send_at):
    total = jnp.zeros((step.shape[0], D), F32)
    for part, c in enumerate(range(0, F, CHUNK)):
        at = slice(c, c + CHUNK)
        grad = dot_nt(step, ctx.weight(down, layer, part)[at, :]) * slope_ref[:, at].astype(F32)
        grad = grad.astype(BF)
        ctx.act[:, at] = grad
        total = total + dot_nt(grad, ctx.weight(up, layer, part)[:, at])
    half_copies(ctx, ctx.act, keep_ref, send_ref, 0, send_at, F, 1)
    return total


def bwd_last(ctx, dy, layer):
    upstream = dy.astype(F32) * valid_rows(ctx)
    smalls = ctx.smalls
    smalls[...] = jnp.zeros(smalls.shape, F32)
    normed, inverse = norm_stats(ctx.r4[...])
    stream, gg = norm_back(upstream, normed, inverse, ctx.small(5, layer))
    smalls[5:6, :] = gg
    step = (0.5 * stream).astype(BF)
    ctx.q3[:, 0:D] = step
    inner = feed_forward_back(ctx, step, UP2, DN2, layer, ctx.s2, ctx.k3, ctx.q3, D)
    normed, inverse = norm_stats(ctx.r3[...])
    branch, gg = norm_back(inner, normed, inverse, ctx.small(4, layer))
    smalls[4:5, :] = gg
    stream = stream + branch
    ctx.dr3[...] = stream
    step = stream.astype(BF)
    ctx.act[:, 0:D] = step
    half_copies(ctx, ctx.act.at[:, 0:D], ctx.k3, ctx.q3, FH, D + FH, D, 1)
    normed, inverse = norm_stats(ctx.z[...])
    gain = ctx.small(3, layer)
    mixed = normed * gain
    logistic = sigmoid(mixed)
    slope = logistic * (1.0 + mixed * (1.0 - logistic))
    mix, gg = norm_back(dot_nt(step, ctx.weight(PRJ, layer)[...]) * slope, normed, inverse, gain)
    smalls[3:4, :] = gg
    ctx.dz[...] = mix.astype(BF)
    edge_rows(ctx, ctx.dz, ctx.dzs, EDGE)


def last_outs(plan):
    t = plan.frames
    return dict(
        smalls=((16, D), F32),
        q3=((t, D + FH + D // 2), BF),
        k3=((t, FH + D // 2), BF),
        dr3=((t, D), F32),
        dz=((t, D), BF),
        dzs=((plan.halos * EDGE, D), BF),
    )


def call_last(plan, late, dy, settle):
    t = plan.frames
    return launch(
        plan, lambda ctx: bwd_last(ctx, ctx.dy[...], 0), "last",
        dict(dy=dy, r4=late.r4, r3=late.r3, z=late.z, s2=late.s2),
        last_outs(plan),
        [(DN2, 0), (UP2, 0), (PRJ, 0)],
        dict(act=((t, F), BF)),
        settle=settle, limit=LIMITS[4],
    )


def mix_time_back(ctx, layer):
    t = ctx.plan.frames
    grads, gated = ctx.ext, ctx.ext2
    weights = [ctx.taps(k, layer) for k in range(K)]
    block = 64
    taps = [[jnp.zeros((8, 128), F32) for _ in range(D // 128)] for _ in range(K)]
    for row in range(0, t, block):
        masks = tap_masks(ctx, row, block)
        for ci, c in enumerate(range(0, D, 128)):
            own = grads[8 + row : 8 + row + block, c : c + 128]
            total = jnp.zeros((block, 128), F32)
            for k in range(K):
                at = 8 + row + k - K // 2
                product = jnp.where(masks[k], own * gated[at : at + block, c : c + 128], 0.0)
                taps[k][ci] = taps[k][ci] + jnp.sum(product.reshape(block // 8, 8, 128), axis=0)
                window = grads[at : at + block, c : c + 128] * weights[K - 1 - k][:, c : c + 128]
                total = total + jnp.where(masks[k], window, 0.0)
            ctx.dg[row : row + block, c : c + 128] = total
    for k in range(K):
        for ci, c in enumerate(range(0, D, 128)):
            ctx.smalls[6 + k : 7 + k, c : c + 128] = jnp.sum(taps[k][ci], axis=0, keepdims=True)


def bwd_attend(ctx, layer):
    t = ctx.plan.frames
    fill_extended(ctx, ctx.ext, ctx.dz, ctx.dzh)
    fill_extended(ctx, ctx.ext2, ctx.g, ctx.gh)
    ctx.smalls[...] = ctx.smalls_in[...]
    mix_time_back(ctx, layer)
    gated = ctx.dg[...]
    act = ctx.act
    act[:, 0:D] = (gated * ctx.gs[...].astype(F32)).astype(BF)
    act[:, D : 2 * D] = (gated * ctx.gt[...].astype(F32)).astype(BF)
    half_copies(ctx, act, ctx.k2, ctx.q2, 0, 0, 2 * D, 1)
    normed, inverse = norm_stats(ctx.r2[...])
    branch, gg = norm_back(
        dot_nt(act[...], ctx.weight(EXP, layer)[...]), normed, inverse, ctx.small(2, layer)
    )
    ctx.smalls[2:3, :] = gg
    stream = ctx.dr3[...] + branch
    ctx.dr2[...] = stream
    step = stream.astype(BF)
    act[:, 0:D] = step
    half_copies(ctx, act.at[:, 0:D], ctx.k2, ctx.q2, D, D, D, 1)
    grad_o = ctx.do
    grad_o[...] = dot_nt(step, ctx.weight(OUT, layer)[...]).astype(BF)
    qkv, kvh, probs, p2 = ctx.qkv, ctx.kvh, ctx.probs, ctx.p2
    lane = lax.broadcasted_iota(jnp.int32, (t, 2 * HD), 1)
    laneh = lax.broadcasted_iota(jnp.int32, (ctx.plan.halos * W, 2 * HD), 1)
    scale = HD ** (-0.5)
    for p in range(H // 2):
        at = 2 * HD * p
        q = qkv[:, at : at + 2 * HD] * jnp.asarray(scale, BF)
        k = qkv[:, D + at : D + at + 2 * HD]
        v = qkv[:, 2 * D + at : 2 * D + at + 2 * HD]
        kh = kvh[:, at : at + 2 * HD]
        vh = kvh[:, D + at : D + at + 2 * HD]
        do = grad_o[:, at : at + 2 * HD]
        spread = do.astype(F32) * p2[:, at : at + 2 * HD].astype(F32)
        parts = []
        for e in range(2):
            mine = (lane // HD) == e
            dom = jnp.where(mine, do, jnp.zeros_like(do))
            delta = jnp.sum(jnp.where(mine, spread, 0.0), axis=-1, keepdims=True)
            po = probs[2 * p + e, :, 0:t]
            ph = probs[2 * p + e, :, t:]
            so = (po.astype(F32) * (dot_nt(dom, v) - delta)).astype(BF)
            sh = (ph.astype(F32) * (dot_nt(dom, vh) - delta)).astype(BF)
            parts.append(
                (
                    dot(so, k) + dot(sh, kh),
                    dot_tn(so, q),
                    dot_tn(sh, q),
                    dot_tn(po, do),
                    dot_tn(ph, do),
                )
            )
        one, two = parts
        ctx.dq[:, at : at + 2 * HD] = (jnp.where(lane < HD, one[0], two[0]) * scale).astype(BF)
        ctx.dkv[:, at : at + 2 * HD] = jnp.where(lane < HD, one[1], two[1])
        ctx.dkvh[:, at : at + 2 * HD] = jnp.where(laneh < HD, one[2], two[2]).astype(BF)
        ctx.dkv[:, D + at : D + at + 2 * HD] = jnp.where(lane < HD, one[3], two[3])
        ctx.dkvh[:, D + at : D + at + 2 * HD] = jnp.where(laneh < HD, one[4], two[4]).astype(BF)


def call_attend_back(plan, layer, first, mid, last, kvh, gh, dzh, settle):
    t = plan.frames
    return launch(
        plan,
        lambda ctx: bwd_attend(ctx, layer),
        "attend_back",
        dict(
            dz=last.dz, dzh=dzh, dr3=last.dr3, smalls_in=last.smalls,
            g=mid.g, gh=gh, gs=mid.gs, gt=mid.gt, r2=mid.r2,
            probs=mid.probs, p2=mid.p2, qkv=first.qkv, kvh=kvh,
        ),
        dict(
            smalls=((16, D), F32),
            q2=((t, D + D // 2), BF),
            k2=((t, D + D // 2), BF),
            dr2=((t, D), F32),
            dq=((t, D), BF),
            dkv=((t, 2 * D), F32),
            dkvh=((plan.halos * W, 2 * D), BF),
        ),
        [(EXP, layer), (OUT, layer)],
        dict(
            ext=((t + 16, D), F32), ext2=((t + 16, D), F32), dg=((t, D), F32),
            act=((t, 2 * D), BF), do=((t, D), BF),
        ),
        settle=settle, limit=LIMITS[5],
    )


def bwd_first(ctx, layer):
    t = ctx.plan.frames
    ctx.smalls[...] = ctx.smalls_in[...]
    grads, acc, back = ctx.act, ctx.acc, ctx.back
    grads[:, 0:D] = ctx.dq[...]
    acc[...] = ctx.dkv[...]
    if ctx.plan.halos == 1:
        at = pl.multiple_of((1 - ctx.core) * (t - W), W)
        acc[pl.ds(at, W), :] += back[...].astype(F32)
    else:
        acc[t - W : t, :] += back[0:W, :].astype(F32)
        acc[0:W, :] += back[W : 2 * W, :].astype(F32)
    grads[:, D : 3 * D] = acc[...].astype(BF)
    half_copies(ctx, grads.at[:, 0 : 3 * D], ctx.k1, ctx.q1.at[0:t], FH, D + FH, 3 * D, 1)
    normed, inverse = norm_stats(ctx.r1[...])
    branch, gg = norm_back(
        dot_nt(grads[:, 0 : 3 * D], ctx.weight(QKV, layer)[...]), normed, inverse, ctx.small(1, layer)
    )
    ctx.smalls[1:2, :] = gg
    stream = ctx.dr2[...] + branch
    step = (0.5 * stream).astype(BF)
    ctx.q1[0:t, 0:D] = step
    inner = feed_forward_back(ctx, step, UP1, DN1, layer, ctx.s1, ctx.k1, ctx.q1.at[0:t], D)
    normed, inverse = norm_stats(ctx.x[...].astype(F32))
    branch, gg = norm_back(inner, normed, inverse, ctx.small(0, layer))
    ctx.smalls[0:1, :] = gg
    ctx.ig[...] = (stream + branch).astype(BF)
    ctx.q1[t : t + EDGE, 0:D] = ctx.smalls[...].astype(BF)
    ctx.q1[0:t, Q2_AT : Q2_AT + D + D // 2] = ctx.q2[...]


def call_first_back(plan, layer, x, first, att, back, settle):
    t = plan.frames
    return launch(
        plan,
        lambda ctx: bwd_first(ctx, layer),
        "first_back",
        dict(
            x=x, r1=first.r1, s1=first.s1, dr2=att.dr2, dq=att.dq, dkv=att.dkv, back=back,
            smalls_in=att.smalls, q2=att.q2,
        ),
        dict(
            smalls=((16, D), F32),
            q1=((t + EDGE, Q2_AT + D + D // 2), BF),
            k1=((t, FH + 3 * D // 2), BF),
            ig=((t, D), BF),
        ),
        [(QKV, layer), (DN1, layer), (UP1, layer)],
        dict(act=((t, F), BF), acc=((t, 2 * D), F32)),
        settle=settle, limit=LIMITS[6],
    )


ROWS = (128, 64, 192)


def both_tn(left, left_got, right, right_got):
    return dot_tn(left, right) + dot_tn(left_got, right_got)


def put_part(ref, value, q, at, col):
    width = value.shape[1]
    for b in range(2):
        ref[b, q, at : at + 64, col : col + width] = value[64 * b : 64 * (b + 1), :].astype(BF)


def put_ffn(ref, a, row, step, step_got, hid, hid_got, act, fwd_got, inner, bwd_got):
    for q in range(4):
        at = pl.multiple_of(q * 256 + a * 128, 128)
        got = pl.multiple_of(2 * D + q * 256 + a * 128, 128)
        value = both_tn(act[:, pl.ds(at, 128)], fwd_got[:, pl.ds(got, 128)], step, step_got)
        put_part(ref, value, q, row, 0)
    at = pl.multiple_of(a * D, D)
    got = pl.multiple_of(D + a * D, D)
    value = both_tn(hid, hid_got, inner[:, pl.ds(at, D)], bwd_got[:, pl.ds(got, D)])
    for q in range(4):
        put_part(ref, value[q * 128 : (q + 1) * 128, :], q, row + 64, 0)


def put_matrix(ref, a, left, left_got, left_at, right, own_at, right_got, got_at, width, at, col):
    own = pl.multiple_of(own_at + a * width, 128)
    got = pl.multiple_of(got_at + a * width, 128)
    value = both_tn(
        left[:, left_at : left_at + D], left_got[:, left_at : left_at + D],
        right[:, pl.ds(own, width)], right_got[:, pl.ds(got, width)],
    )
    for q in range(4):
        put_part(ref, value[q * 128 : (q + 1) * 128, :], q, at, col)


def call_bucket(plan, kinds, f, g):
    joint = hasattr(f, "c3")

    def body(ctx):
        side = ctx.side1
        t = plan.frames
        if joint and kinds != (2,):
            cut = 2 * D + FH
            ctx.p3, ctx.q3 = ctx.c3.at[:, 0:cut], ctx.c3.at[:, cut:]
            ctx.p3_got, ctx.q3_got = ctx.c3_got.at[:, 0:cut], ctx.c3_got.at[:, cut:]
        if kinds != (0,):
            q1_got = ctx.q1_got.at[0:t]
            q2_got = ctx.q1_got.at[0:t, Q2_AT : Q2_AT + D + D // 2]
        if 2 in kinds:
            small = ctx.smalls[...] + ctx.q1_got[t : t + EDGE, 0:D].astype(F32)
            small = jnp.where(ctx.core == 0, small[0:8], small[8:16])
            small = jnp.concatenate([small, jnp.zeros((56, D), F32)], axis=0).astype(BF)
        for ref, a in ((ctx.send, 1 - side), (ctx.keep, side)):
            at = 0
            if 0 in kinds:
                put_ffn(
                    ref, a, at, ctx.q3[:, 0:D], ctx.q3_got[:, 0:D], ctx.p3[:, D : 2 * D],
                    ctx.p3_got[:, D : 2 * D], ctx.a2, ctx.p3_got, ctx.k3, ctx.q3_got,
                )
                at += ROWS[0]
            if 1 in kinds:
                put_matrix(ref, a, ctx.p2, ctx.p2_got, D, ctx.k2, 0, q2_got, 0, 256, at, 0)
                put_matrix(ref, a, ctx.p2, ctx.p2_got, 0, ctx.k2, D, q2_got, D, 128, at, 256)
                put_matrix(ref, a, ctx.p3, ctx.p3_got, 0, ctx.k3, FH, ctx.q3_got, D + FH, 128, at, 384)
                at += ROWS[1]
            if 2 in kinds:
                put_ffn(
                    ref, a, at, ctx.q1[0:t, 0:D], ctx.q1_got[0:t, 0:D], ctx.p1[:, 0:D],
                    ctx.p1_got[:, 0:D], ctx.a1, ctx.p1_got, ctx.k1, q1_got,
                )
                put_matrix(
                    ref, a, ctx.p1, ctx.p1_got, D, ctx.k1, FH, q1_got, D + FH, 384, at + 128, 0
                )
                for q in range(4):
                    for b in range(2):
                        ref[b, q, at + 128 : at + 192, 384:512] = small[:, q * 128 : (q + 1) * 128]

    ins = {}
    names = ()
    if 2 in kinds:
        names += ("p1", "q1")
        ins.update(a1=f.a1, k1=f.k1, smalls=f.smalls)
    if kinds != (2,):
        names += ("c3",) if joint else ("p3", "q3")
        ins.update(k3=f.k3)
    if 0 in kinds:
        ins.update(a2=f.a2)
    if 1 in kinds:
        names += ("p2",)
        ins.update(k2=f.k2, q1_got=g.q1)
    for name in names:
        ins[name] = getattr(f, name)
        ins[name + "_got"] = getattr(g, name)
    shape = (2, 4, sum(ROWS[k] for k in kinds), D)
    part = launch(plan, body, "bucket", ins, dict(send=(shape, BF), keep=(shape, BF)), limit=LIMITS[7])
    part.got = exchange(plan, part.send, 0)
    return part


def exchange(plan, value, stage):
    pairs = []
    for core in range(2):
        bit = 1 if (core == 0) == (stage == 0) else 2
        pairs += [(core * 4 + i, core * 4 + (i ^ bit)) for i in range(4)]
    return lax.ppermute(value, MESH_AXES[:2], pairs)


def call_second(plan, parts):
    count = len(parts)
    rows = [p.keep.shape[2] for p in parts]

    def body(ctx):
        side = ctx.side2
        for ref, at in ((ctx.send, 1 - side), (ctx.mine, side)):
            row = 0
            for i in range(count):
                keep, got = getattr(ctx, "m%d" % i), getattr(ctx, "g%d" % i)
                value = keep[at].astype(F32) + got[at].astype(F32)
                ref[:, row : row + rows[i], :] = value.astype(BF)
                row += rows[i]

    ins = {"m%d" % i: p.keep for i, p in enumerate(parts)}
    ins.update({"g%d" % i: p.got for i, p in enumerate(parts)})
    shape = (4, sum(rows), D)
    half = launch(plan, body, "second", ins, dict(send=(shape, BF), mine=(shape, BF)), limit=16)
    half.got = exchange(plan, half.send, 1)
    return half


def call_third(plan, halves):
    rows = [h.mine.shape[1] for h in halves]

    def body(ctx):
        side = lax.rem(ctx.chip, 2)
        for ref, near in ((ctx.send, 1 - side), (ctx.mine, side)):
            at = 0
            for i, count in enumerate(rows):
                mine, got = getattr(ctx, "m%d" % i), getattr(ctx, "g%d" % i)
                for far in range(2):
                    q = 2 * far + near
                    value = mine[q].astype(F32) + got[q].astype(F32)
                    ref[far, at : at + count, :] = value.astype(BF)
                at += count

    ins = {"m%d" % i: h.mine for i, h in enumerate(halves)}
    ins.update({"g%d" % i: h.got for i, h in enumerate(halves)})
    shape = (2, sum(rows), D)
    made = launch(plan, body, "third", ins, dict(send=(shape, BF), mine=(shape, BF)), limit=4)
    made.got = exchange_seq(made.send, 1)
    return made


def call_fourth(plan, half):
    def body(ctx):
        side = lax.div(ctx.chip, 2)
        for ref, at in ((ctx.send, 1 - side), (ctx.mine, side)):
            ref[...] = (ctx.keep[at].astype(F32) + ctx.got[at].astype(F32)).astype(BF)

    shape = half.mine.shape[1:]
    made = launch(
        plan, body, "fourth", dict(keep=half.mine, got=half.got),
        dict(send=(shape, BF), mine=(shape, BF)), limit=4,
    )
    made.got = exchange_seq(made.send, 2)
    return made


def exchange_seq(value, bit):
    return lax.ppermute(value, MESH_AXES[2], [(i, i ^ bit) for i in range(4)])


def call_total(plan, half):
    def body(ctx):
        ctx.own[...] = (ctx.mine[...].astype(F32) + ctx.got[...].astype(F32)).astype(BF)

    total = launch(
        plan, body, "total", dict(mine=half.mine, got=half.got), dict(own=(half.mine.shape, BF)), limit=4
    )
    total.got = exchange(plan, total.own, 1)
    return total


def call_pair(plan, total, layer):
    def body(ctx):
        ctx.pair[ctx.side2] = ctx.own[...]
        ctx.pair[1 - ctx.side2] = ctx.got[...]

    shape = (2,) + total.own.shape
    pair = launch(
        plan, body, "pair", dict(own=total.own, got=total.got), dict(pair=(shape, BF)), limit=4
    ).pair
    pair_got = exchange(plan, pair, 0)
    over = [(1 - layer, layer)]
    return (
        pair, pair_got, lax.ppermute(pair, MESH_AXES[0], over), lax.ppermute(pair_got, MESH_AXES[0], over)
    )


def swap(value):
    return lax.ppermute(value, MESH_AXES[0], [(0, 1), (1, 0)])


def call_unpack(plan, which, spots):
    ins = {}
    for layer in range(2):
        for k in range(4):
            ins["l%d_%d" % (layer, k)] = spots[layer][1][k]
    ffn = dict(up=((128, F), F32), dn=((512, D), F32))
    rest = dict(out=((128, D), F32), exp=((128, 2 * D), F32), prj=((128, D), F32))
    last = dict(qkv=((128, 3 * D), F32), sml=((16, 128), F32))
    results = (ffn, rest, dict(ffn, **last))[which]

    def body(ctx):
        for layer in range(2):

            @pl.when(ctx.core == layer)
            def _(layer=layer):
                start = spots[layer][0]
                for k in range(4):
                    half = layer if k < 2 else 1 - layer
                    side = ctx.fast if half == 0 else ctx.slow
                    a = side if k % 2 == 0 else 1 - side
                    source = getattr(ctx, "l%d_%d" % (layer, k))
                    for b in range(2):
                        rows = slice(64 * b, 64 * b + 64)
                        first = source[b, start : start + 64, :].astype(F32)
                        if which != 1:
                            at = pl.multiple_of(half * 256 + a * 128 + b * 64, 64)
                            ctx.dn[pl.ds(at, 64), :] = first
                            at = pl.multiple_of(half * FH + a * D, D)
                            ctx.up[rows, pl.ds(at, D)] = source[b, start + 64 : start + 128, :].astype(F32)
                        else:
                            at = pl.multiple_of(half * 512 + a * 256, 256)
                            ctx.exp[rows, pl.ds(at, 256)] = first[:, 0:256]
                            at = pl.multiple_of(half * 256 + a * 128, 128)
                            ctx.out[rows, pl.ds(at, 128)] = first[:, 256:384]
                            ctx.prj[rows, pl.ds(at, 128)] = first[:, 384:512]
                        if which == 2:
                            third = source[b, start + 128 : start + 192, :].astype(F32)
                            at = pl.multiple_of(half * 768 + a * 384, 128)
                            ctx.qkv[rows, pl.ds(at, 384)] = third[:, 0:384]
                            if k % 2 == 0 and b == 0:
                                ctx.sml[half * 8 : half * 8 + 8, :] = third[0:8, 384:512]

    return launch(plan, body, "unpack", ins, {}, results=results, limit=16)


def pick_rows(plan, arrays, gains, taps):
    size = arrays[0].shape[1]
    half = plan.rows // 2

    def body(ctx):
        near = lax.div(ctx.row, half) == ctx.core
        copies = []
        for i in range(len(arrays)):
            source = getattr(ctx, "value%d" % i)
            for k in range(3):
                other = jnp.where(near, k, (0, 2, 3, 1)[k])
                copies.append(
                    pltpu.make_async_copy(
                        source.at[ctx.row ^ other], getattr(ctx, "p%d_%d" % (i, k)), ctx.sems[len(copies)]
                    )
                )
        for copy in copies:
            copy.start()
        ctx.small[0:6, :] = ctx.gains[0].astype(F32)
        ctx.small[6:15, :] = ctx.taps[0].astype(F32)
        ctx.small[15:16, :] = jnp.zeros((1, D), F32)
        for copy in copies:
            copy.wait()

    names = [["p%d_%d" % (i, k) for k in range(3)] for i in range(len(arrays))]
    outs = {n: ((size, D), BF) for group in names for n in group}
    far = {"value%d" % i: v for i, v in enumerate(arrays)}
    picked = launch(
        plan, body, "pick_rows", dict(gains=gains, taps=taps), dict(outs, small=((16, D), F32)),
        far=far, limit=16,
    )
    result = []
    for group in names:
        sent = [getattr(picked, n) for n in group]
        both, third = [], []
        for chip in range(plan.seq):
            c = (chip % 4) // 2
            both.append((c * plan.seq + chip, c * plan.seq + (chip ^ 1)))
            both.append(((1 - c) * plan.seq + chip, c * plan.seq + (chip ^ 2)))
            third.append(((1 - c) * plan.seq + chip, c * plan.seq + (chip ^ 3)))
        pieces = [
            sent[0], lax.ppermute(sent[1], MESH_AXES[::2], both),
            lax.ppermute(sent[2], MESH_AXES[::2], third),
        ]
        result.append({"piece%d" % k: v for k, v in enumerate(pieces)})
    return result, picked.small


def join_frames(ctx, target):
    plan = ctx.plan
    half = plan.rows // 2
    size = plan.frames // half
    near = lax.div(ctx.row, half) == ctx.core

    def put(piece, source):
        at = pl.multiple_of(lax.rem(source, half) * size, size)
        target[pl.ds(at, size), :] = piece[...]

    @pl.when(near)
    def _():
        put(ctx.piece0, ctx.row)
        put(ctx.piece1, ctx.row ^ 1)

    @pl.when(jnp.logical_not(near))
    def _():
        put(ctx.piece1, ctx.row ^ 2)
        put(ctx.piece2, ctx.row ^ 3)


def split_layers(plan, layers, settle):
    count = len(layers[0])

    def body(ctx):
        for layer in range(2):
            for i in range(count):
                value = getattr(ctx, "l%d_%d" % (layer, i))

                @pl.when(ctx.core == layer)
                def _(value=value, i=i):
                    ctx.keep[i] = value[...]

                @pl.when(ctx.core != layer)
                def _(value=value, i=i):
                    ctx.send[i] = value[...]

    shape = (count, plan.frames, D)
    ins = {"l%d_%d" % (l, i): v for l in range(2) for i, v in enumerate(layers[l])}
    out = launch(
        plan, body, "split", ins, dict(keep=(shape, BF), send=(shape, BF)), settle=settle, limit=16
    )
    return out.keep, swap(out.send)


def chips_apart(plan, value, bit):
    pairs = [(c * plan.seq + i, c * plan.seq + (i ^ bit)) for c in range(2) for i in range(plan.seq)]
    return lax.ppermute(value, MESH_AXES[::2], pairs)


def deal_rows(plan, keep, got):
    size = plan.frames // 2

    def body(ctx):
        for distance, target in ((0, ctx.rest.at[0]), (2, ctx.rest.at[1]), (1, ctx.near.at[0]), (3, ctx.near.at[1])):
            chip = ctx.row ^ distance
            at = pl.multiple_of(lax.rem(chip, 2) * size, size)

            @pl.when(lax.div(chip, 2) == ctx.core)
            def _(target=target, at=at):
                target[...] = ctx.keep[:, pl.ds(at, size), :]

            @pl.when(lax.div(chip, 2) != ctx.core)
            def _(target=target, at=at):
                target[...] = ctx.got[:, pl.ds(at, size), :]

    shape = (2, keep.shape[0], size, D)
    dealt = launch(
        plan, body, "deal_rows", dict(keep=keep, got=got), dict(near=(shape, BF), rest=(shape, BF)), limit=8
    )
    dealt.got = chips_apart(plan, dealt.near, 1)
    return dealt


def deal_far(plan, dealt):
    def body(ctx):
        ctx.far[0] = ctx.rest[1]
        ctx.far[1] = ctx.got[1]

    dealt.far = launch(
        plan, body, "deal_far", dict(rest=dealt.rest, got=dealt.got),
        dict(far=(dealt.rest.shape, BF)), limit=8,
    ).far
    dealt.far_got = chips_apart(plan, dealt.far, 2)
    return dealt


def place_rows(plan, dealt):
    def body(ctx):
        pieces = (ctx.rest.at[0], ctx.got.at[0], ctx.far.at[0], ctx.far.at[1])
        for distance, piece in enumerate(pieces):
            ctx.activations[ctx.row ^ distance] = piece[0]
            ctx.input_grads[ctx.row ^ distance] = piece[1].astype(F32)

    shape = (plan.rows,) + dealt.rest.shape[2:]
    return launch(
        plan, body, "place_rows", dict(rest=dealt.rest, got=dealt.got, far=dealt.far_got), {},
        results=dict(activations=(shape, BF), input_grads=(shape, F32)), limit=8,
    )


def halo_exchange(plan, send, rows):
    if plan.halos == 1:
        return swap(send)
    return jnp.concatenate(
        [
            lax.ppermute(send[0:rows], MESH_AXES[::2], plan.to_right),
            lax.ppermute(send[rows:], MESH_AXES[::2], plan.to_left),
        ],
        axis=0,
    )


def halo_return(plan, grads, rows):
    if plan.halos == 1:
        return swap(grads)
    return jnp.concatenate(
        [
            lax.ppermute(grads[0:rows], MESH_AXES[::2], plan.to_left),
            lax.ppermute(grads[rows:], MESH_AXES[::2], plan.to_right),
        ],
        axis=0,
    )


def plain_gradients(plan, layers):
    def whole(keep, send):
        return jnp.where(
            plan.core == 0,
            jnp.concatenate([keep, send], axis=1),
            jnp.concatenate([send, keep], axis=1),
        )

    stacked = []
    for f in layers:
        p1, p2, p3, q1, q2, q3, k1, k2, k3 = f.p1, f.p2, f.p3, f.q1, f.q2, f.q3, f.k1, f.k2, f.k3
        q1 = q1[: plan.frames]
        operands = (
            (p1[:, :D], whole(k1[:, :FH], q1[:, D : D + FH])),
            (whole(f.a1, p1[:, 2 * D :]), q1[:, :D]),
            (p1[:, D : 2 * D], whole(k1[:, FH:], q1[:, D + FH : Q2_AT])),
            (p2[:, :D], whole(k2[:, D:], q2[:, D:])),
            (p2[:, D:], whole(k2[:, :D], q2[:, :D])),
            (p3[:, :D], whole(k3[:, FH:], q3[:, D + FH :])),
            (p3[:, D : 2 * D], whole(k3[:, :FH], q3[:, D : D + FH])),
            (whole(f.a2, p3[:, 2 * D :]), q3[:, :D]),
        )
        grads = [dot_tn(a, b).astype(BF) for a, b in operands]
        grads.append(f.smalls[0:6].astype(BF))
        grads.append(f.smalls[6:15].astype(BF))
        stacked.append(grads)
    result = []
    for index in range(10):
        both = jnp.stack([stacked[0][index], stacked[1][index]])
        mine = lax.psum_scatter(both, MESH_AXES[0], scatter_dimension=0, tiled=False)
        dim = 0 if index < 8 else 1
        mine = lax.psum_scatter(mine, MESH_AXES[2], scatter_dimension=dim, tiled=True)
        result.append(lax.psum(mine, MESH_AXES[1]).astype(F32))
    up1, dn1, qkv, out, exp, prj, up2, dn2, gains, taps = result
    return up1, dn1, qkv, out, exp, taps, prj, up2, dn2, gains


def make_plan(mesh_shape, inputs, lengths, weights):
    plan = SimpleNamespace(token=None, lengths=lengths)
    plan.rows = inputs.shape[0]
    assert plan.rows == 4
    plan.dp, plan.seq = mesh_shape[MESH_AXES[1]], mesh_shape[MESH_AXES[2]]
    plan.length = inputs.shape[1] * plan.seq
    plan.frames = plan.rows * inputs.shape[1] // 2
    plan.halos = 1 if plan.seq == plan.rows else 2
    plan.direct = plan.dp == 4 and plan.seq == 4
    plan.blocks = plan.seq if plan.direct else 1
    plan.core = lax.axis_index(MESH_AXES[0])
    seq = plan.seq
    plan.to_right = [(q, seq + q) for q in range(seq)]
    plan.to_right += [(seq + q, q + plan.rows) for q in range(seq - plan.rows)]
    plan.to_left = [(b, a) for a, b in plan.to_right]
    plan.own = [w[0] for w in weights]
    return plan


def per_device(
    mesh_shape,
    inputs,
    cotangent,
    lengths,
    ffn_one_up,
    ffn_one_down,
    attn_project,
    attn_output,
    conv_expand,
    conv_depthwise,
    conv_project,
    ffn_two_up,
    ffn_two_down,
    norm_gains,
):
    matrices = (
        ffn_one_up, ffn_one_down, attn_project, attn_output, conv_expand, conv_project, ffn_two_up,
        ffn_two_down,
    )
    plan = make_plan(mesh_shape, inputs, lengths, matrices)
    direct = plan.direct
    (pieces, cotangent_pieces), plan.small_own = pick_rows(
        plan, (inputs, cotangent), norm_gains, conv_depthwise
    )
    plan.small_other = swap(plan.small_own)
    plan.other = [swap(w) for w in plan.own]

    def over(value):
        return swap(value) if direct else None

    def after(value, other):
        return lax.optimization_barrier((value, other))[0]

    def there(*values):
        return values if direct else ()

    first0 = call_first(plan, pieces)
    kvh0 = halo_exchange(plan, first0.kvs, W)
    mid0 = call_attend(plan, 0, first0, kvh0)
    gh0 = halo_exchange(plan, mid0.gsend, EDGE)
    turn = call_conv_first(plan, mid0, gh0)
    kvh1 = halo_exchange(plan, turn.kvs, W)
    got0 = SimpleNamespace(p1=over(first0.p1), p2=over(mid0.p2))
    mid1 = call_attend(plan, 1, turn, kvh1, there(got0.p1, got0.p2))
    gh1 = halo_exchange(plan, mid1.gsend, EDGE)
    got0.p3, got1 = over(turn.p3), SimpleNamespace(p1=over(turn.p1))
    end = call_conv_last(plan, mid1, gh1, cotangent_pieces, there(got0.p3, got1.p1))
    dzh1 = halo_exchange(plan, end.dzs, EDGE)
    launch(plan, lambda ctx: None, "between", {}, {}, limit=1)
    got1.c3, got1.p2 = over(after(end.c3, dzh1)), over(after(mid1.p2, dzh1))
    own1 = SimpleNamespace(
        p1=turn.p1, a1=turn.a1, p2=mid1.p2, c3=end.c3, a2=end.a2, k3=end.k3
    )
    own0 = SimpleNamespace(
        p1=first0.p1, a1=first0.a1, p2=mid0.p2, p3=turn.p3, a2=turn.a2
    )
    att1 = call_attend_back(plan, 1, turn, mid1, end, kvh1, gh1, dzh1, ())
    back1 = halo_return(plan, att1.dkvh, W)
    own1.q2, own1.k2 = att1.q2, att1.k2
    if direct:
        two1 = call_bucket(plan, (0,), own1, got1)
    beg1 = call_first_back(plan, 1, turn.y, turn, att1, back1, there(got1.p2))
    own1.q1, own1.k1, own1.smalls = beg1.q1, beg1.k1, beg1.smalls
    got1.q1 = over(beg1.q1)
    last0 = call_last(plan, turn, beg1.ig, ())
    dzh0 = halo_exchange(plan, last0.dzs, EDGE)
    own0.q3, own0.k3 = last0.q3, last0.k3
    got0.q3 = over(last0.q3)
    if direct:
        one1 = call_bucket(plan, (2,), own1, got1)
    att0 = call_attend_back(plan, 0, first0, mid0, last0, kvh0, gh0, dzh0, there(got0.q3))
    back0 = halo_return(plan, att0.dkvh, W)
    own0.q2, own0.k2 = att0.q2, att0.k2
    if direct:
        mid1b = call_bucket(plan, (1,), own1, got1)
    beg0 = call_first_back(plan, 0, first0.x, first0, att0, back0, ())
    own0.q1, own0.k1, own0.smalls = beg0.q1, beg0.k1, beg0.smalls
    got0.q1 = over(beg0.q1)
    keep, got = split_layers(plan, ((turn.y, beg0.ig), (end.y, beg1.ig)), ())
    if direct:
        two0 = call_bucket(plan, (0,), own0, got0)
    dealt = deal_rows(plan, keep, got)
    if direct:
        one1 = call_second(plan, [one1])
        early1 = call_second(plan, [two1, mid1b])
        mid0b = call_bucket(plan, (1,), own0, got0)
        one0 = call_bucket(plan, (2,), own0, got0)
    dealt = deal_far(plan, dealt)
    if direct:
        early0 = call_second(plan, [two0, mid0b])
        one1 = call_third(plan, [one1])
    framed = place_rows(plan, dealt)
    if direct:
        early1 = call_third(plan, [early1])
        one1 = call_fourth(plan, one1)
        early0 = call_third(plan, [early0])
        one0 = call_second(plan, [one0])
        early1 = call_fourth(plan, early1)
        one0 = call_third(plan, [one0])
        one1 = call_total(plan, one1)
        early0 = call_fourth(plan, early0)
        early1 = call_total(plan, early1)
        one1 = call_pair(plan, one1, 1)
        early1 = call_pair(plan, early1, 1)
        one0 = call_fourth(plan, one0)
        early0 = call_total(plan, early0)
        early0 = call_pair(plan, early0, 0)
        one0 = call_total(plan, one0)
        one0 = call_pair(plan, one0, 0)
        middle_at = ROWS[0]
        two = call_unpack(plan, 0, ((0, early0), (0, early1)))
        middle = call_unpack(plan, 1, ((middle_at, early0), (middle_at, early1)))
        one = call_unpack(plan, 2, ((0, one0), (0, one1)))
        results = (
            one.up, one.dn, one.qkv, middle.out, middle.exp, one.sml[6:15], middle.prj,
            two.up, two.dn, one.sml[0:6],
        )
    else:
        own1.p3, own1.q3 = end.c3[:, : 2 * D + FH], end.c3[:, 2 * D + FH :]
        results = plain_gradients(plan, (own0, own1))
    activations, input_grads = framed.activations, framed.input_grads
    return (activations[None], input_grads[None]) + tuple(r[None] for r in results)


def solution(mesh):
    section, dp, seq = MESH_AXES
    whole = P(section, None, None)
    sliced = P(section, seq, None)
    across = P(section, None, seq)
    framed = P(section, dp, seq, None)
    return jax.shard_map(
        functools.partial(per_device, dict(mesh.shape)),
        mesh=mesh,
        in_specs=(P(dp, seq, None), P(dp, seq, None), P(dp, None)) + (whole,) * 10,
        out_specs=(framed, framed) + (sliced,) * 5 + (across,) + (sliced,) * 3 + (across,),
        check_vma=False,
    )
```

```python
import functools
from types import SimpleNamespace

import jax
import jax.numpy as jnp
from jax import lax
from jax.experimental import pallas as pl
from jax.experimental.pallas import tpu as pltpu
from jax.sharding import PartitionSpec as P

D = 512
H = 8
HD = 64
F = 2048
FH = F // 2
K = 9
W = 128
UTT = 4
EPSILON = 1e-05
MASKED = -1e30
EDGE = 16
Q2_AT = D + FH + 3 * D // 2
CHUNK = 2048
MIB = 1024 * 1024
COST = 10**10
LIMITS = (16, 16, 20, 20, 16, 16, 16, 16)
MESH_AXES = ("section", "dp", "seq")

BF = jnp.bfloat16
F32 = jnp.float32

UP1, DN1, QKV, OUT, EXP, PRJ, UP2, DN2 = range(8)


def dot(a, b):
    return jnp.dot(a, b, preferred_element_type=F32)


def dot_nt(a, b):
    return lax.dot_general(a, b, (((1,), (1,)), ((), ())), preferred_element_type=F32)


def dot_tn(a, b):
    return lax.dot_general(a, b, (((0,), (0,)), ((), ())), preferred_element_type=F32)


def sigmoid(v):
    return 0.5 * jnp.tanh(0.5 * v) + 0.5


def norm_stats(v):
    centred = v - jnp.mean(v, axis=-1, keepdims=True)
    inverse = lax.rsqrt(jnp.mean(centred * centred, axis=-1, keepdims=True) + EPSILON)
    return centred * inverse, inverse


def norm_back(upstream, normed, inverse, gain):
    gain_grad = jnp.sum(upstream * normed, axis=0, keepdims=True)
    scaled = upstream * gain
    value_grad = inverse * (
        scaled
        - jnp.mean(scaled, axis=-1, keepdims=True)
        - normed * jnp.mean(scaled * normed, axis=-1, keepdims=True)
    )
    return value_grad, gain_grad


class Place:
    def __init__(self, plan, lengths):
        core, replica, chip = (lax.axis_index(name) for name in MESH_AXES)
        self.core, self.chip = core, chip
        self.row = lax.rem(chip, plan.rows)
        self.first = (lax.div(chip, plan.rows) * 2 + core) * plan.frames
        self.length = plan.length
        self.fast = lax.rem(replica, 2)
        self.slow = lax.rem(lax.div(replica, 2), 2)
        self.side1 = jnp.where(core == 0, self.fast, self.slow)
        self.side2 = jnp.where(core == 0, self.slow, self.fast)
        self.ends = []
        total = 0
        for u in range(UTT):
            total = total + lengths[self.row, u]
            self.ends.append(total)


class Ctx:
    def __init__(self, plan, place, table, held, waits):
        self.__dict__.update(place.__dict__)
        self.__dict__.update(table)
        self.plan = plan
        self.held = held
        self.waits = waits

    def weight(self, matrix, layer, part=None):
        queue = self.waits[(matrix, layer)]
        for index in range(len(queue)):
            if queue[index] is not None and (part is None or part == index):
                queue[index].wait()
                queue[index] = None
        return self.held[(matrix, layer)]

    def small(self, row, layer):
        mine = self.core == layer
        return jnp.where(mine, self.small_own[row : row + 1, :], self.small_other[row : row + 1, :])

    def taps(self, tap, layer):
        return self.small(6 + tap, layer)

    def segment(self, pos):
        start, stop = jnp.zeros(pos.shape, jnp.int32), jnp.full(pos.shape, self.length, jnp.int32)
        for end in self.ends:
            start = jnp.maximum(start, jnp.where(pos >= end, end, 0))
            stop = jnp.minimum(stop, jnp.where(pos >= end, self.length, end))
        return start, stop


def parts_of(matrix, shape):
    if matrix in (UP1, UP2):
        return [(slice(None), pl.ds(c, CHUNK)) for c in range(0, F, CHUNK)]
    if matrix in (DN1, DN2):
        return [(pl.ds(c, CHUNK), slice(None)) for c in range(0, F, CHUNK)]
    return [(slice(None), slice(None))]


def launch(plan, body, name, ins, outs, weights=(), scratch=None, far=None, results=None, settle=(),
           limit=16):
    scratch, far, results = scratch or {}, far or {}, results or {}
    near = dict(ins)
    near.update({"settle%d" % i: v for i, v in enumerate(settle)})
    if weights:
        near.update(small_own=plan.small_own, small_other=plan.small_other)
    if plan.token is not None:
        near.update(token_in=plan.token)
    pinned = [pltpu.with_memory_space_constraint(v, pltpu.VMEM) for v in near.values()]
    operands = [pltpu.with_memory_space_constraint(plan.lengths, pltpu.HBM)] + pinned
    operands += [pltpu.with_memory_space_constraint(v, pltpu.HBM) for v in far.values()]
    in_specs = [pl.BlockSpec(memory_space=pltpu.SMEM)]
    in_specs += [pl.BlockSpec(memory_space=pltpu.VMEM)] * len(near)
    in_specs += [pl.BlockSpec(memory_space=pl.ANY)] * len(far)
    copies = []
    for matrix, layer in weights:
        operands += [
            pltpu.with_memory_space_constraint(plan.own[matrix], pltpu.HBM),
            plan.other[matrix],
        ]
        in_specs += [pl.BlockSpec(memory_space=pl.ANY)] * 2
        copies.append(parts_of(matrix, plan.own[matrix].shape))
    held_shapes = [pltpu.VMEM(plan.own[m].shape, BF) for m, _ in weights]
    out_shape = [pltpu.VMEM(*s) for s in outs.values()]
    out_shape += [jax.ShapeDtypeStruct(*s) for s in results.values()]
    out_shape += [pltpu.VMEM((8, 128), jnp.int32)]
    out_specs = [pl.BlockSpec(memory_space=pltpu.VMEM)] * len(out_shape)
    sems = max(sum(len(c) for c in copies), 1) + 24

    def kernel(*refs):
        refs = list(refs)
        place = Place(plan, refs.pop(0))
        table = {}
        for n in list(near) + list(far):
            table[n] = refs.pop(0)
        sources = [(refs.pop(0), refs.pop(0)) for _ in weights]
        for n in list(outs) + list(results):
            table[n] = refs.pop(0)
        refs.pop(0)
        for n in scratch:
            table[n] = refs.pop(0)
        held_refs = [refs.pop(0) for _ in weights]
        sem = refs.pop(0)
        core = place.core
        held, waits = {}, {}
        for pair in weights:
            waits[pair] = []
        count = 0
        for part in range(max([len(c) for c in copies], default=0)):
            for pair, (own, other), into, slices in zip(weights, sources, held_refs, copies):
                held[pair] = into
                if part >= len(slices):
                    continue
                at = slices[part]

                @pl.when(core == pair[1])
                def _(own=own, into=into, at=at, count=count):
                    pltpu.make_async_copy(own.at[at], into.at[at], sem.at[count]).start()

                @pl.when(core != pair[1])
                def _(other=other, into=into, at=at, count=count):
                    pltpu.make_async_copy(other.at[at], into.at[at], sem.at[count]).start()

                waits[pair].append(pltpu.make_async_copy(own.at[at], into.at[at], sem.at[count]))
                count += 1
        ctx = Ctx(plan, place, table, held, waits)
        ctx.sems = [sem.at[sems - 24 + i] for i in range(24)]
        body(ctx)
        for pair in weights:
            ctx.weight(*pair)

    made = pl.pallas_call(
        kernel,
        out_shape=out_shape,
        in_specs=in_specs,
        out_specs=out_specs,
        scratch_shapes=[pltpu.VMEM(*s) for s in scratch.values()]
        + held_shapes
        + [pltpu.SemaphoreType.DMA((sems,))],
        compiler_params=pltpu.CompilerParams(vmem_limit_bytes=limit * MIB),
        cost_estimate=pl.CostEstimate(flops=COST, transcendentals=0, bytes_accessed=1),
        name=name,
    )(*operands)
    plan.token = made[-1]
    return SimpleNamespace(**dict(zip(list(outs) + list(results), made)))


def half_copies(ctx, value_ref, keep_ref, send_ref, keep_at, send_at, total, blocks):
    width = total // (2 * blocks)
    for j in range(blocks):
        mine = pl.multiple_of(j * 2 * width + ctx.core * width, width)
        theirs = pl.multiple_of(j * 2 * width + (1 - ctx.core) * width, width)
        keep_ref[:, keep_at + j * width : keep_at + (j + 1) * width] = value_ref[:, pl.ds(mine, width)]
        send_ref[:, send_at + j * width : send_at + (j + 1) * width] = value_ref[
            :, pl.ds(theirs, width)
        ]


def edge_rows(ctx, value_ref, send_ref, rows):
    frames = value_ref.shape[0]
    if ctx.plan.halos == 1:
        at = pl.multiple_of((1 - ctx.core) * (frames - rows), rows)
        send_ref[...] = value_ref[pl.ds(at, rows), :]
    else:
        send_ref[0:rows, :] = value_ref[frames - rows : frames, :]
        send_ref[rows : 2 * rows, :] = value_ref[0:rows, :]


def halo_starts(ctx, rows, frames):
    before = ctx.first - rows
    after = ctx.first + frames
    if ctx.plan.halos == 1:
        return [jnp.where(ctx.core == 0, after, before)]
    return [before, after]


def feed_forward(ctx, hidden, up, down, layer, keep_ref, send_ref, send_at, slope_ref):
    frames = hidden.shape[0]
    total = jnp.zeros((frames, D), F32)
    for part, c in enumerate(range(0, F, CHUNK)):
        at = slice(c, c + CHUNK)
        inner = dot(hidden, ctx.weight(up, layer, part)[:, at])
        logistic = sigmoid(inner)
        active = (inner * logistic).astype(BF)
        slope_ref[:, at] = (logistic * (1.0 + inner * (1.0 - logistic))).astype(BF)
        ctx.act[:, at] = active
        total = total + dot(active, ctx.weight(down, layer, part)[at, :])
    half_copies(ctx, ctx.act, keep_ref, send_ref, 0, send_at, F, ctx.plan.blocks)
    return total


def fwd_first(ctx, x, layer):
    normed, _ = norm_stats(x)
    hidden = (normed * ctx.small(0, layer)).astype(BF)
    ctx.p1[:, 0:D] = hidden
    ffn = feed_forward(ctx, hidden, UP1, DN1, layer, ctx.a1, ctx.p1, 2 * D, ctx.s1)
    r1 = x + 0.5 * ffn
    ctx.r1[...] = r1
    normed, _ = norm_stats(r1)
    hidden = (normed * ctx.small(1, layer)).astype(BF)
    ctx.p1[:, D : 2 * D] = hidden
    ctx.qkv[...] = dot(hidden, ctx.weight(QKV, layer)[...]).astype(BF)
    edge_rows(ctx, ctx.qkv.at[:, D : 3 * D], ctx.kvs, W)


def first_outs(plan):
    t = plan.frames
    return dict(
        p1=((t, 2 * D + FH), BF),
        a1=((t, FH), BF),
        s1=((t, F), BF),
        r1=((t, D), F32),
        qkv=((t, 3 * D), BF),
        kvs=((plan.halos * W, 2 * D), BF),
    )


def call_first(plan, pieces):
    def body(ctx):
        join_frames(ctx, ctx.x)
        fwd_first(ctx, ctx.x[...].astype(F32), 0)

    t = plan.frames
    return launch(
        plan, body, "first", pieces, dict(x=((t, D), BF), **first_outs(plan)),
        [(UP1, 0), (DN1, 0), (QKV, 0)], dict(act=((t, F), BF)), limit=LIMITS[0],
    )


def allowed_bias(ctx, key_start, keys):
    frames = ctx.plan.frames
    query = ctx.first + lax.broadcasted_iota(jnp.int32, (frames, 1), 0)
    start, stop = ctx.segment(query)
    low, high = jnp.maximum(start, query - W), jnp.minimum(stop - 1, query + W)
    key = key_start + lax.broadcasted_iota(jnp.int32, (frames, keys), 1)
    return jnp.where((key >= low) & (key <= high), 0.0, MASKED).astype(F32)


def stacked_heads(value, lane):
    zero = jnp.zeros_like(value)
    return jnp.concatenate([jnp.where(lane < HD, value, zero), jnp.where(lane < HD, zero, value)], axis=0)


def fwd_attend(ctx, layer):
    t = ctx.plan.frames
    halos = ctx.plan.halos
    qkv, probs, p2, bias, kx = ctx.qkv, ctx.probs, ctx.p2, ctx.bias, ctx.kx
    kx[0:t, :] = qkv[:, D : 3 * D]
    kx[t:, :] = ctx.kvh[...]
    starts = halo_starts(ctx, W, t)
    bias[:, 0:t] = allowed_bias(ctx, ctx.first, t)
    for h in range(halos):
        bias[:, t + h * W : t + (h + 1) * W] = allowed_bias(ctx, starts[h], W)
    lane = lax.broadcasted_iota(jnp.int32, (t, 2 * HD), 1)
    for p in range(H // 2):
        at = 2 * HD * p
        q = stacked_heads(qkv[:, at : at + 2 * HD] * jnp.asarray(HD ** (-0.5), BF), lane)
        scores = dot_nt(q, kx[:, at : at + 2 * HD]).reshape(2, t, -1) + bias[...][None]
        exponent = jnp.exp(scores - jnp.max(scores, axis=-1, keepdims=True))
        scale = 1.0 / jnp.sum(exponent, axis=-1, keepdims=True)
        weights = (exponent * scale).astype(BF).reshape(2 * t, -1)
        probs[p] = weights
        out = dot(weights, kx[:, D + at : D + at + 2 * HD])
        p2[:, at : at + 2 * HD] = jnp.where(lane < HD, out[0:t], out[t:]).astype(BF)
    r2 = ctx.r1[...] + dot(p2[:, 0:D], ctx.weight(OUT, layer)[...])
    ctx.r2[...] = r2
    normed, _ = norm_stats(r2)
    hidden = (normed * ctx.small(2, layer)).astype(BF)
    p2[:, D : 2 * D] = hidden
    expand = ctx.weight(EXP, layer)
    linear = dot(hidden, expand[:, 0:D])
    logistic = sigmoid(dot(hidden, expand[:, D : 2 * D]))
    gated = linear * logistic
    ctx.g[...] = gated.astype(BF)
    ctx.gs[...] = logistic.astype(BF)
    ctx.gt[...] = (gated * (1.0 - logistic)).astype(BF)
    edge_rows(ctx, ctx.g, ctx.gsend, EDGE)


def call_attend(plan, layer, first, kvh, settle=()):
    t = plan.frames
    keys = t + plan.halos * W
    return launch(
        plan,
        lambda ctx: fwd_attend(ctx, layer),
        "attend",
        dict(qkv=first.qkv, kvh=kvh, r1=first.r1),
        dict(
            probs=((H // 2, 2 * t, keys), BF),
            kx=((keys, 2 * D), BF),
            p2=((t, 2 * D), BF),
            r2=((t, D), F32),
            g=((t, D), BF),
            gs=((t, D), BF),
            gt=((t, D), BF),
            gsend=((plan.halos * EDGE, D), BF),
        ),
        [(OUT, layer), (EXP, layer)],
        dict(bias=((t, keys), F32)),
        settle=settle, limit=LIMITS[1],
    )


def fill_extended(ctx, ext, own, halo):
    t = ctx.plan.frames
    before = halo[EDGE - 8 : EDGE, :]
    after = halo[0:8, :] if ctx.plan.halos == 1 else halo[EDGE : EDGE + 8, :]
    ext[0:8, :] = before.astype(F32)
    ext[8 : 8 + t, :] = own[...].astype(F32)
    ext[8 + t : 16 + t, :] = after.astype(F32)


def tap_masks(ctx, row, rows):
    pos = ctx.first + row + lax.broadcasted_iota(jnp.int32, (rows, 128), 0)
    start, stop = ctx.segment(pos)
    before, after = pos - start, stop - pos
    return [(before >= K // 2 - k) if k <= K // 2 else (after > k - K // 2) for k in range(K)]


def mix_time(ctx, ext, z_ref, layer):
    t = ctx.plan.frames
    taps = [ctx.taps(k, layer) for k in range(K)]
    block = 64
    for row in range(0, t, block):
        masks = tap_masks(ctx, row, block)
        for c in range(0, D, 128):
            total = jnp.zeros((block, 128), F32)
            for k in range(K):
                at = 8 + row + k - K // 2
                window = ext[at : at + block, c : c + 128] * taps[k][:, c : c + 128]
                total = total + jnp.where(masks[k], window, 0.0)
            z_ref[row : row + block, c : c + 128] = total


def valid_rows(ctx):
    pos = ctx.first + lax.broadcasted_iota(jnp.int32, (ctx.plan.frames, 1), 0)
    return (pos < ctx.ends[UTT - 1]).astype(F32)


def fwd_conv(ctx, layer):
    fill_extended(ctx, ctx.ext, ctx.g, ctx.gh)
    mix_time(ctx, ctx.ext, ctx.z, layer)
    normed, _ = norm_stats(ctx.z[...])
    mixed = normed * ctx.small(3, layer)
    active = (mixed * sigmoid(mixed)).astype(BF)
    ctx.p3[:, 0:D] = active
    r3 = ctx.r2[...] + dot(active, ctx.weight(PRJ, layer)[...])
    ctx.r3[...] = r3
    normed, _ = norm_stats(r3)
    hidden = (normed * ctx.small(4, layer)).astype(BF)
    ctx.p3[:, D : 2 * D] = hidden
    ffn = feed_forward(ctx, hidden, UP2, DN2, layer, ctx.a2, ctx.p3, 2 * D, ctx.s2)
    r4 = r3 + 0.5 * ffn
    ctx.r4[...] = r4
    normed, _ = norm_stats(r4)
    result = (normed * ctx.small(5, layer) * valid_rows(ctx)).astype(BF)
    ctx.y[...] = result
    return result


def conv_outs(plan):
    t = plan.frames
    return dict(
        z=((t, D), F32),
        p3=((t, 2 * D + FH), BF),
        a2=((t, FH), BF),
        s2=((t, F), BF),
        r3=((t, D), F32),
        r4=((t, D), F32),
        y=((t, D), BF),
    )


def conv_scratch(plan):
    t = plan.frames
    return dict(ext=((t + 16, D), F32), act=((t, F), BF))


def call_conv_first(plan, mid, gh):
    def body(ctx):
        fwd_first(ctx, fwd_conv(ctx, 0).astype(F32), 1)

    return launch(
        plan, body, "conv_first", dict(g=mid.g, gh=gh, r2=mid.r2),
        dict(conv_outs(plan), **first_outs(plan)),
        [(PRJ, 0), (UP2, 0), (DN2, 0), (UP1, 1), (DN1, 1), (QKV, 1)],
        conv_scratch(plan), limit=LIMITS[2],
    )


def call_conv_last(plan, mid, gh, pieces, settle):
    outs = dict(conv_outs(plan), **last_outs(plan))
    del outs["p3"], outs["q3"]
    outs["c3"] = ((plan.frames, 2 * D + FH + D + FH + D // 2), BF)

    def body(ctx):
        ctx.p3, ctx.q3 = ctx.c3.at[:, 0 : 2 * D + FH], ctx.c3.at[:, 2 * D + FH :]
        fwd_conv(ctx, 1)
        join_frames(ctx, ctx.dy)
        bwd_last(ctx, ctx.dy[...], 1)

    return launch(
        plan, body, "conv_last", dict(g=mid.g, gh=gh, r2=mid.r2, **pieces), outs,
        [(PRJ, 1), (UP2, 1), (DN2, 1)],
        dict(conv_scratch(plan), dy=((plan.frames, D), BF)), settle=settle, limit=LIMITS[3],
    )


def feed_forward_back(ctx, step, up, down, layer, slope_ref, keep_ref, send_ref, send_at):
    total = jnp.zeros((step.shape[0], D), F32)
    for part, c in enumerate(range(0, F, CHUNK)):
        at = slice(c, c + CHUNK)
        grad = dot_nt(step, ctx.weight(down, layer, part)[at, :]) * slope_ref[:, at].astype(F32)
        grad = grad.astype(BF)
        ctx.act[:, at] = grad
        total = total + dot_nt(grad, ctx.weight(up, layer, part)[:, at])
    half_copies(ctx, ctx.act, keep_ref, send_ref, 0, send_at, F, 1)
    return total


def bwd_last(ctx, dy, layer):
    upstream = dy.astype(F32) * valid_rows(ctx)
    smalls = ctx.smalls
    smalls[...] = jnp.zeros(smalls.shape, F32)
    normed, inverse = norm_stats(ctx.r4[...])
    stream, gg = norm_back(upstream, normed, inverse, ctx.small(5, layer))
    smalls[5:6, :] = gg
    step = (0.5 * stream).astype(BF)
    ctx.q3[:, 0:D] = step
    inner = feed_forward_back(ctx, step, UP2, DN2, layer, ctx.s2, ctx.k3, ctx.q3, D)
    normed, inverse = norm_stats(ctx.r3[...])
    branch, gg = norm_back(inner, normed, inverse, ctx.small(4, layer))
    smalls[4:5, :] = gg
    stream = stream + branch
    ctx.dr3[...] = stream
    step = stream.astype(BF)
    ctx.act[:, 0:D] = step
    half_copies(ctx, ctx.act.at[:, 0:D], ctx.k3, ctx.q3, FH, D + FH, D, 1)
    normed, inverse = norm_stats(ctx.z[...])
    gain = ctx.small(3, layer)
    mixed = normed * gain
    logistic = sigmoid(mixed)
    slope = logistic * (1.0 + mixed * (1.0 - logistic))
    mix, gg = norm_back(dot_nt(step, ctx.weight(PRJ, layer)[...]) * slope, normed, inverse, gain)
    smalls[3:4, :] = gg
    ctx.dz[...] = mix.astype(BF)
    edge_rows(ctx, ctx.dz, ctx.dzs, EDGE)


def last_outs(plan):
    t = plan.frames
    return dict(
        smalls=((16, D), F32),
        q3=((t, D + FH + D // 2), BF),
        k3=((t, FH + D // 2), BF),
        dr3=((t, D), F32),
        dz=((t, D), BF),
        dzs=((plan.halos * EDGE, D), BF),
    )


def call_last(plan, late, dy, settle):
    t = plan.frames
    return launch(
        plan, lambda ctx: bwd_last(ctx, ctx.dy[...], 0), "last",
        dict(dy=dy, r4=late.r4, r3=late.r3, z=late.z, s2=late.s2),
        last_outs(plan),
        [(DN2, 0), (UP2, 0), (PRJ, 0)],
        dict(act=((t, F), BF)),
        settle=settle, limit=LIMITS[4],
    )


def mix_time_back(ctx, layer):
    t = ctx.plan.frames
    grads, gated = ctx.ext, ctx.ext2
    weights = [ctx.taps(k, layer) for k in range(K)]
    block = 64
    taps = [[jnp.zeros((8, 128), F32) for _ in range(D // 128)] for _ in range(K)]
    for row in range(0, t, block):
        masks = tap_masks(ctx, row, block)
        for ci, c in enumerate(range(0, D, 128)):
            own = grads[8 + row : 8 + row + block, c : c + 128]
            total = jnp.zeros((block, 128), F32)
            for k in range(K):
                at = 8 + row + k - K // 2
                product = jnp.where(masks[k], own * gated[at : at + block, c : c + 128], 0.0)
                taps[k][ci] = taps[k][ci] + jnp.sum(product.reshape(block // 8, 8, 128), axis=0)
                window = grads[at : at + block, c : c + 128] * weights[K - 1 - k][:, c : c + 128]
                total = total + jnp.where(masks[k], window, 0.0)
            ctx.dg[row : row + block, c : c + 128] = total
    for k in range(K):
        for ci, c in enumerate(range(0, D, 128)):
            ctx.smalls[6 + k : 7 + k, c : c + 128] = jnp.sum(taps[k][ci], axis=0, keepdims=True)


def bwd_attend(ctx, layer):
    t = ctx.plan.frames
    fill_extended(ctx, ctx.ext, ctx.dz, ctx.dzh)
    fill_extended(ctx, ctx.ext2, ctx.g, ctx.gh)
    ctx.smalls[...] = ctx.smalls_in[...]
    mix_time_back(ctx, layer)
    gated = ctx.dg[...]
    act = ctx.act
    act[:, 0:D] = (gated * ctx.gs[...].astype(F32)).astype(BF)
    act[:, D : 2 * D] = (gated * ctx.gt[...].astype(F32)).astype(BF)
    half_copies(ctx, act, ctx.k2, ctx.q2, 0, 0, 2 * D, 1)
    normed, inverse = norm_stats(ctx.r2[...])
    branch, gg = norm_back(
        dot_nt(act[...], ctx.weight(EXP, layer)[...]), normed, inverse, ctx.small(2, layer)
    )
    ctx.smalls[2:3, :] = gg
    stream = ctx.dr3[...] + branch
    ctx.dr2[...] = stream
    step = stream.astype(BF)
    act[:, 0:D] = step
    half_copies(ctx, act.at[:, 0:D], ctx.k2, ctx.q2, D, D, D, 1)
    grad_o = ctx.do
    grad_o[...] = dot_nt(step, ctx.weight(OUT, layer)[...]).astype(BF)
    qkv, probs, p2, kx = ctx.qkv, ctx.probs, ctx.p2, ctx.kx
    lane = lax.broadcasted_iota(jnp.int32, (t, 2 * HD), 1)
    scale = HD ** (-0.5)
    for p in range(H // 2):
        at = 2 * HD * p
        q = stacked_heads(qkv[:, at : at + 2 * HD] * jnp.asarray(scale, BF), lane)
        do = grad_o[:, at : at + 2 * HD]
        spread = stacked_heads(do.astype(F32) * p2[:, at : at + 2 * HD].astype(F32), lane)
        do = stacked_heads(do, lane)
        delta = jnp.sum(spread, axis=-1, keepdims=True)
        weights = probs[p]
        grad = dot_nt(do, kx[:, D + at : D + at + 2 * HD]) - delta
        grad = (weights.astype(F32) * grad).astype(BF)
        dq = dot(grad, kx[:, at : at + 2 * HD]) * scale
        ctx.dq[:, at : at + 2 * HD] = jnp.where(lane < HD, dq[0:t], dq[t:]).astype(BF)
        dk, dv = dot_tn(grad, q), dot_tn(weights, do)
        ctx.dkv[:, at : at + 2 * HD] = dk[0:t]
        ctx.dkv[:, D + at : D + at + 2 * HD] = dv[0:t]
        ctx.dkvh[:, at : at + 2 * HD] = dk[t:].astype(BF)
        ctx.dkvh[:, D + at : D + at + 2 * HD] = dv[t:].astype(BF)


def call_attend_back(plan, layer, first, mid, last, gh, dzh, settle):
    t = plan.frames
    return launch(
        plan,
        lambda ctx: bwd_attend(ctx, layer),
        "attend_back",
        dict(
            dz=last.dz, dzh=dzh, dr3=last.dr3, smalls_in=last.smalls,
            g=mid.g, gh=gh, gs=mid.gs, gt=mid.gt, r2=mid.r2,
            probs=mid.probs, p2=mid.p2, qkv=first.qkv, kx=mid.kx,
        ),
        dict(
            smalls=((16, D), F32),
            q2=((t, D + D // 2), BF),
            k2=((t, D + D // 2), BF),
            dr2=((t, D), F32),
            dq=((t, D), BF),
            dkv=((t, 2 * D), F32),
            dkvh=((plan.halos * W, 2 * D), BF),
        ),
        [(EXP, layer), (OUT, layer)],
        dict(
            ext=((t + 16, D), F32), ext2=((t + 16, D), F32), dg=((t, D), F32),
            act=((t, 2 * D), BF), do=((t, D), BF),
        ),
        settle=settle, limit=LIMITS[5],
    )


def bwd_first(ctx, layer):
    t = ctx.plan.frames
    ctx.smalls[...] = ctx.smalls_in[...]
    grads, acc, back = ctx.act, ctx.acc, ctx.back
    grads[:, 0:D] = ctx.dq[...]
    acc[...] = ctx.dkv[...]
    if ctx.plan.halos == 1:
        at = pl.multiple_of((1 - ctx.core) * (t - W), W)
        acc[pl.ds(at, W), :] += back[...].astype(F32)
    else:
        acc[t - W : t, :] += back[0:W, :].astype(F32)
        acc[0:W, :] += back[W : 2 * W, :].astype(F32)
    grads[:, D : 3 * D] = acc[...].astype(BF)
    half_copies(ctx, grads.at[:, 0 : 3 * D], ctx.k1, ctx.q1.at[0:t], FH, D + FH, 3 * D, 1)
    normed, inverse = norm_stats(ctx.r1[...])
    branch, gg = norm_back(
        dot_nt(grads[:, 0 : 3 * D], ctx.weight(QKV, layer)[...]), normed, inverse, ctx.small(1, layer)
    )
    ctx.smalls[1:2, :] = gg
    stream = ctx.dr2[...] + branch
    step = (0.5 * stream).astype(BF)
    ctx.q1[0:t, 0:D] = step
    inner = feed_forward_back(ctx, step, UP1, DN1, layer, ctx.s1, ctx.k1, ctx.q1.at[0:t], D)
    normed, inverse = norm_stats(ctx.x[...].astype(F32))
    branch, gg = norm_back(inner, normed, inverse, ctx.small(0, layer))
    ctx.smalls[0:1, :] = gg
    ctx.ig[...] = (stream + branch).astype(BF)
    ctx.q1[t : t + EDGE, 0:D] = ctx.smalls[...].astype(BF)
    ctx.q1[0:t, Q2_AT : Q2_AT + D + D // 2] = ctx.q2[...]


def call_first_back(plan, layer, x, first, att, back, settle):
    t = plan.frames
    return launch(
        plan,
        lambda ctx: bwd_first(ctx, layer),
        "first_back",
        dict(
            x=x, r1=first.r1, s1=first.s1, dr2=att.dr2, dq=att.dq, dkv=att.dkv, back=back,
            smalls_in=att.smalls, q2=att.q2,
        ),
        dict(
            smalls=((16, D), F32),
            q1=((t + EDGE, Q2_AT + D + D // 2), BF),
            k1=((t, FH + 3 * D // 2), BF),
            ig=((t, D), BF),
        ),
        [(QKV, layer), (DN1, layer), (UP1, layer)],
        dict(act=((t, F), BF), acc=((t, 2 * D), F32)),
        settle=settle, limit=LIMITS[6],
    )


ROWS = (128, 64, 192)


def both_tn(left, left_got, right, right_got):
    return dot_tn(left, right) + dot_tn(left_got, right_got)


def put_part(ref, value, q, at, col):
    width = value.shape[1]
    for b in range(2):
        ref[b, q, at : at + 64, col : col + width] = value[64 * b : 64 * (b + 1), :].astype(BF)


def put_ffn(ref, a, row, step, step_got, hid, hid_got, act, fwd_got, inner, bwd_got):
    for q in range(4):
        at = pl.multiple_of(q * 256 + a * 128, 128)
        got = pl.multiple_of(2 * D + q * 256 + a * 128, 128)
        value = both_tn(act[:, pl.ds(at, 128)], fwd_got[:, pl.ds(got, 128)], step, step_got)
        put_part(ref, value, q, row, 0)
    at = pl.multiple_of(a * D, D)
    got = pl.multiple_of(D + a * D, D)
    value = both_tn(hid, hid_got, inner[:, pl.ds(at, D)], bwd_got[:, pl.ds(got, D)])
    for q in range(4):
        put_part(ref, value[q * 128 : (q + 1) * 128, :], q, row + 64, 0)


def put_matrix(ref, a, left, left_got, left_at, right, own_at, right_got, got_at, width, at, col):
    own = pl.multiple_of(own_at + a * width, 128)
    got = pl.multiple_of(got_at + a * width, 128)
    value = both_tn(
        left[:, left_at : left_at + D], left_got[:, left_at : left_at + D],
        right[:, pl.ds(own, width)], right_got[:, pl.ds(got, width)],
    )
    for q in range(4):
        put_part(ref, value[q * 128 : (q + 1) * 128, :], q, at, col)


def call_bucket(plan, kinds, f, g):
    joint = hasattr(f, "c3")

    def body(ctx):
        side = ctx.side1
        t = plan.frames
        if joint and kinds != (2,):
            cut = 2 * D + FH
            ctx.p3, ctx.q3 = ctx.c3.at[:, 0:cut], ctx.c3.at[:, cut:]
            ctx.p3_got, ctx.q3_got = ctx.c3_got.at[:, 0:cut], ctx.c3_got.at[:, cut:]
        if kinds != (0,):
            q1_got = ctx.q1_got.at[0:t]
            q2_got = ctx.q1_got.at[0:t, Q2_AT : Q2_AT + D + D // 2]
        if 2 in kinds:
            small = ctx.smalls[...] + ctx.q1_got[t : t + EDGE, 0:D].astype(F32)
            small = jnp.where(ctx.core == 0, small[0:8], small[8:16])
            small = jnp.concatenate([small, jnp.zeros((56, D), F32)], axis=0).astype(BF)
        for ref, a in ((ctx.send, 1 - side), (ctx.keep, side)):
            at = 0
            if 0 in kinds:
                put_ffn(
                    ref, a, at, ctx.q3[:, 0:D], ctx.q3_got[:, 0:D], ctx.p3[:, D : 2 * D],
                    ctx.p3_got[:, D : 2 * D], ctx.a2, ctx.p3_got, ctx.k3, ctx.q3_got,
                )
                at += ROWS[0]
            if 1 in kinds:
                put_matrix(ref, a, ctx.p2, ctx.p2_got, D, ctx.k2, 0, q2_got, 0, 256, at, 0)
                put_matrix(ref, a, ctx.p2, ctx.p2_got, 0, ctx.k2, D, q2_got, D, 128, at, 256)
                put_matrix(ref, a, ctx.p3, ctx.p3_got, 0, ctx.k3, FH, ctx.q3_got, D + FH, 128, at, 384)
                at += ROWS[1]
            if 2 in kinds:
                put_ffn(
                    ref, a, at, ctx.q1[0:t, 0:D], ctx.q1_got[0:t, 0:D], ctx.p1[:, 0:D],
                    ctx.p1_got[:, 0:D], ctx.a1, ctx.p1_got, ctx.k1, q1_got,
                )
                put_matrix(
                    ref, a, ctx.p1, ctx.p1_got, D, ctx.k1, FH, q1_got, D + FH, 384, at + 128, 0
                )
                for q in range(4):
                    for b in range(2):
                        ref[b, q, at + 128 : at + 192, 384:512] = small[:, q * 128 : (q + 1) * 128]

    ins = {}
    names = ()
    if 2 in kinds:
        names += ("p1", "q1")
        ins.update(a1=f.a1, k1=f.k1, smalls=f.smalls)
    if kinds != (2,):
        names += ("c3",) if joint else ("p3", "q3")
        ins.update(k3=f.k3)
    if 0 in kinds:
        ins.update(a2=f.a2)
    if 1 in kinds:
        names += ("p2",)
        ins.update(k2=f.k2, q1_got=g.q1)
    for name in names:
        ins[name] = getattr(f, name)
        ins[name + "_got"] = getattr(g, name)
    shape = (2, 4, sum(ROWS[k] for k in kinds), D)
    part = launch(plan, body, "bucket", ins, dict(send=(shape, BF), keep=(shape, BF)), limit=LIMITS[7])
    part.got = exchange(plan, part.send, 0)
    return part


def exchange(plan, value, stage):
    pairs = []
    for core in range(2):
        bit = 1 if (core == 0) == (stage == 0) else 2
        pairs += [(core * 4 + i, core * 4 + (i ^ bit)) for i in range(4)]
    return lax.ppermute(value, MESH_AXES[:2], pairs)


def call_second(plan, parts):
    count = len(parts)
    rows = [p.keep.shape[2] for p in parts]

    def body(ctx):
        side = ctx.side2
        for ref, at in ((ctx.send, 1 - side), (ctx.mine, side)):
            row = 0
            for i in range(count):
                keep, got = getattr(ctx, "m%d" % i), getattr(ctx, "g%d" % i)
                value = keep[at].astype(F32) + got[at].astype(F32)
                ref[:, row : row + rows[i], :] = value.astype(BF)
                row += rows[i]

    ins = {"m%d" % i: p.keep for i, p in enumerate(parts)}
    ins.update({"g%d" % i: p.got for i, p in enumerate(parts)})
    shape = (4, sum(rows), D)
    half = launch(plan, body, "second", ins, dict(send=(shape, BF), mine=(shape, BF)), limit=16)
    half.got = exchange(plan, half.send, 1)
    return half


def call_third(plan, halves):
    rows = [h.mine.shape[1] for h in halves]

    def body(ctx):
        side = lax.rem(ctx.chip, 2)
        for ref, near in ((ctx.send, 1 - side), (ctx.mine, side)):
            at = 0
            for i, count in enumerate(rows):
                mine, got = getattr(ctx, "m%d" % i), getattr(ctx, "g%d" % i)
                for far in range(2):
                    q = 2 * far + near
                    value = mine[q].astype(F32) + got[q].astype(F32)
                    ref[far, at : at + count, :] = value.astype(BF)
                at += count

    ins = {"m%d" % i: h.mine for i, h in enumerate(halves)}
    ins.update({"g%d" % i: h.got for i, h in enumerate(halves)})
    shape = (2, sum(rows), D)
    made = launch(plan, body, "third", ins, dict(send=(shape, BF), mine=(shape, BF)), limit=4)
    made.got = exchange_seq(made.send, 1)
    return made


def call_fourth(plan, half):
    def body(ctx):
        side = lax.div(ctx.chip, 2)
        for ref, at in ((ctx.send, 1 - side), (ctx.mine, side)):
            ref[...] = (ctx.keep[at].astype(F32) + ctx.got[at].astype(F32)).astype(BF)

    shape = half.mine.shape[1:]
    made = launch(
        plan, body, "fourth", dict(keep=half.mine, got=half.got),
        dict(send=(shape, BF), mine=(shape, BF)), limit=4,
    )
    made.got = exchange_seq(made.send, 2)
    return made


def exchange_seq(value, bit):
    return lax.ppermute(value, MESH_AXES[2], [(i, i ^ bit) for i in range(4)])


def call_total(plan, half):
    def body(ctx):
        ctx.own[...] = (ctx.mine[...].astype(F32) + ctx.got[...].astype(F32)).astype(BF)

    total = launch(
        plan, body, "total", dict(mine=half.mine, got=half.got), dict(own=(half.mine.shape, BF)), limit=4
    )
    total.got = exchange(plan, total.own, 1)
    return total


def call_pair(plan, total, layer):
    def body(ctx):
        ctx.pair[ctx.side2] = ctx.own[...]
        ctx.pair[1 - ctx.side2] = ctx.got[...]

    shape = (2,) + total.own.shape
    pair = launch(
        plan, body, "pair", dict(own=total.own, got=total.got), dict(pair=(shape, BF)), limit=4
    ).pair
    pair_got = exchange(plan, pair, 0)
    over = [(1 - layer, layer)]
    return (
        pair, pair_got, lax.ppermute(pair, MESH_AXES[0], over), lax.ppermute(pair_got, MESH_AXES[0], over)
    )


def swap(value):
    return lax.ppermute(value, MESH_AXES[0], [(0, 1), (1, 0)])


def call_unpack(plan, which, spots):
    ins = {}
    for layer in range(2):
        for k in range(4):
            ins["l%d_%d" % (layer, k)] = spots[layer][1][k]
    ffn = dict(up=((128, F), F32), dn=((512, D), F32))
    rest = dict(out=((128, D), F32), exp=((128, 2 * D), F32), prj=((128, D), F32))
    last = dict(qkv=((128, 3 * D), F32), sml=((16, 128), F32))
    results = (ffn, rest, dict(ffn, **last))[which]

    def body(ctx):
        for layer in range(2):

            @pl.when(ctx.core == layer)
            def _(layer=layer):
                start = spots[layer][0]
                for k in range(4):
                    half = layer if k < 2 else 1 - layer
                    side = ctx.fast if half == 0 else ctx.slow
                    a = side if k % 2 == 0 else 1 - side
                    source = getattr(ctx, "l%d_%d" % (layer, k))
                    for b in range(2):
                        rows = slice(64 * b, 64 * b + 64)
                        first = source[b, start : start + 64, :].astype(F32)
                        if which != 1:
                            at = pl.multiple_of(half * 256 + a * 128 + b * 64, 64)
                            ctx.dn[pl.ds(at, 64), :] = first
                            at = pl.multiple_of(half * FH + a * D, D)
                            ctx.up[rows, pl.ds(at, D)] = source[b, start + 64 : start + 128, :].astype(F32)
                        else:
                            at = pl.multiple_of(half * 512 + a * 256, 256)
                            ctx.exp[rows, pl.ds(at, 256)] = first[:, 0:256]
                            at = pl.multiple_of(half * 256 + a * 128, 128)
                            ctx.out[rows, pl.ds(at, 128)] = first[:, 256:384]
                            ctx.prj[rows, pl.ds(at, 128)] = first[:, 384:512]
                        if which == 2:
                            third = source[b, start + 128 : start + 192, :].astype(F32)
                            at = pl.multiple_of(half * 768 + a * 384, 128)
                            ctx.qkv[rows, pl.ds(at, 384)] = third[:, 0:384]
                            if k % 2 == 0 and b == 0:
                                ctx.sml[half * 8 : half * 8 + 8, :] = third[0:8, 384:512]

    return launch(plan, body, "unpack", ins, {}, results=results, limit=16)


def pick_rows(plan, arrays, gains, taps):
    size = arrays[0].shape[1]
    half = plan.rows // 2

    def body(ctx):
        near = lax.div(ctx.row, half) == ctx.core
        copies = []
        for i in range(len(arrays)):
            source = getattr(ctx, "value%d" % i)
            for k in range(3):
                other = jnp.where(near, k, (0, 2, 3, 1)[k])
                copies.append(
                    pltpu.make_async_copy(
                        source.at[ctx.row ^ other], getattr(ctx, "p%d_%d" % (i, k)), ctx.sems[len(copies)]
                    )
                )
        small = [
            pltpu.make_async_copy(ctx.gains, ctx.gains_in, ctx.sems[20]),
            pltpu.make_async_copy(ctx.taps, ctx.taps_in, ctx.sems[21]),
        ]
        for copy in small + copies:
            copy.start()
        for copy in small:
            copy.wait()
        ctx.small[0:6, :] = ctx.gains_in[0].astype(F32)
        ctx.small[6:15, :] = ctx.taps_in[0].astype(F32)
        ctx.small[15:16, :] = jnp.zeros((1, D), F32)
        for copy in copies:
            copy.wait()

    names = [["p%d_%d" % (i, k) for k in range(3)] for i in range(len(arrays))]
    outs = {n: ((size, D), BF) for group in names for n in group}
    far = {"value%d" % i: v for i, v in enumerate(arrays)}
    picked = launch(
        plan, body, "pick_rows", {}, dict(outs, small=((16, D), F32)),
        scratch=dict(gains_in=((1, 6, D), BF), taps_in=((1, 9, D), BF)),
        far=dict(far, gains=gains, taps=taps), limit=4,
    )
    result = []
    for group in names:
        sent = [getattr(picked, n) for n in group]
        both, third = [], []
        for chip in range(plan.seq):
            c = (chip % 4) // 2
            both.append((c * plan.seq + chip, c * plan.seq + (chip ^ 1)))
            both.append(((1 - c) * plan.seq + chip, c * plan.seq + (chip ^ 2)))
            third.append(((1 - c) * plan.seq + chip, c * plan.seq + (chip ^ 3)))
        pieces = [
            sent[0], lax.ppermute(sent[1], MESH_AXES[::2], both),
            lax.ppermute(sent[2], MESH_AXES[::2], third),
        ]
        result.append({"piece%d" % k: v for k, v in enumerate(pieces)})
    return result, picked.small


def join_frames(ctx, target):
    plan = ctx.plan
    half = plan.rows // 2
    size = plan.frames // half
    near = lax.div(ctx.row, half) == ctx.core

    def put(piece, source):
        at = pl.multiple_of(lax.rem(source, half) * size, size)
        target[pl.ds(at, size), :] = piece[...]

    @pl.when(near)
    def _():
        put(ctx.piece0, ctx.row)
        put(ctx.piece1, ctx.row ^ 1)

    @pl.when(jnp.logical_not(near))
    def _():
        put(ctx.piece1, ctx.row ^ 2)
        put(ctx.piece2, ctx.row ^ 3)


def split_layers(plan, layers, settle):
    count = len(layers[0])

    def body(ctx):
        for layer in range(2):
            for i in range(count):
                value = getattr(ctx, "l%d_%d" % (layer, i))

                @pl.when(ctx.core == layer)
                def _(value=value, i=i):
                    ctx.keep[i] = value[...]

                @pl.when(ctx.core != layer)
                def _(value=value, i=i):
                    ctx.send[i] = value[...]

    shape = (count, plan.frames, D)
    ins = {"l%d_%d" % (l, i): v for l in range(2) for i, v in enumerate(layers[l])}
    out = launch(
        plan, body, "split", ins, dict(keep=(shape, BF), send=(shape, BF)), settle=settle, limit=16
    )
    return out.keep, swap(out.send)


def chips_apart(plan, value, bit):
    pairs = [(c * plan.seq + i, c * plan.seq + (i ^ bit)) for c in range(2) for i in range(plan.seq)]
    return lax.ppermute(value, MESH_AXES[::2], pairs)


def deal_rows(plan, keep, got):
    size = plan.frames // 2

    def body(ctx):
        for distance, target in ((0, ctx.rest.at[0]), (2, ctx.rest.at[1]), (1, ctx.near.at[0]), (3, ctx.near.at[1])):
            chip = ctx.row ^ distance
            at = pl.multiple_of(lax.rem(chip, 2) * size, size)

            @pl.when(lax.div(chip, 2) == ctx.core)
            def _(target=target, at=at):
                target[...] = ctx.keep[:, pl.ds(at, size), :]

            @pl.when(lax.div(chip, 2) != ctx.core)
            def _(target=target, at=at):
                target[...] = ctx.got[:, pl.ds(at, size), :]

    shape = (2, keep.shape[0], size, D)
    dealt = launch(
        plan, body, "deal_rows", dict(keep=keep, got=got), dict(near=(shape, BF), rest=(shape, BF)), limit=8
    )
    dealt.got = chips_apart(plan, dealt.near, 1)
    return dealt


def deal_far(plan, dealt):
    def body(ctx):
        ctx.far[0] = ctx.rest[1]
        ctx.far[1] = ctx.got[1]

    dealt.far = launch(
        plan, body, "deal_far", dict(rest=dealt.rest, got=dealt.got),
        dict(far=(dealt.rest.shape, BF)), limit=8,
    ).far
    dealt.far_got = chips_apart(plan, dealt.far, 2)
    return dealt


def place_rows(plan, dealt):
    def body(ctx):
        pieces = (ctx.rest.at[0], ctx.got.at[0], ctx.far.at[0], ctx.far.at[1])
        for distance, piece in enumerate(pieces):
            ctx.activations[ctx.row ^ distance] = piece[0]
            ctx.input_grads[ctx.row ^ distance] = piece[1].astype(F32)

    shape = (plan.rows,) + dealt.rest.shape[2:]
    return launch(
        plan, body, "place_rows", dict(rest=dealt.rest, got=dealt.got, far=dealt.far_got), {},
        results=dict(activations=(shape, BF), input_grads=(shape, F32)), limit=8,
    )


def halo_exchange(plan, send, rows):
    if plan.halos == 1:
        return swap(send)
    return jnp.concatenate(
        [
            lax.ppermute(send[0:rows], MESH_AXES[::2], plan.to_right),
            lax.ppermute(send[rows:], MESH_AXES[::2], plan.to_left),
        ],
        axis=0,
    )


def halo_return(plan, grads, rows):
    if plan.halos == 1:
        return swap(grads)
    return jnp.concatenate(
        [
            lax.ppermute(grads[0:rows], MESH_AXES[::2], plan.to_left),
            lax.ppermute(grads[rows:], MESH_AXES[::2], plan.to_right),
        ],
        axis=0,
    )


def plain_gradients(plan, layers):
    def whole(keep, send):
        return jnp.where(
            plan.core == 0,
            jnp.concatenate([keep, send], axis=1),
            jnp.concatenate([send, keep], axis=1),
        )

    stacked = []
    for f in layers:
        p1, p2, p3, q1, q2, q3, k1, k2, k3 = f.p1, f.p2, f.p3, f.q1, f.q2, f.q3, f.k1, f.k2, f.k3
        q1 = q1[: plan.frames]
        operands = (
            (p1[:, :D], whole(k1[:, :FH], q1[:, D : D + FH])),
            (whole(f.a1, p1[:, 2 * D :]), q1[:, :D]),
            (p1[:, D : 2 * D], whole(k1[:, FH:], q1[:, D + FH : Q2_AT])),
            (p2[:, :D], whole(k2[:, D:], q2[:, D:])),
            (p2[:, D:], whole(k2[:, :D], q2[:, :D])),
            (p3[:, :D], whole(k3[:, FH:], q3[:, D + FH :])),
            (p3[:, D : 2 * D], whole(k3[:, :FH], q3[:, D : D + FH])),
            (whole(f.a2, p3[:, 2 * D :]), q3[:, :D]),
        )
        grads = [dot_tn(a, b).astype(BF) for a, b in operands]
        grads.append(f.smalls[0:6].astype(BF))
        grads.append(f.smalls[6:15].astype(BF))
        stacked.append(grads)
    result = []
    for index in range(10):
        both = jnp.stack([stacked[0][index], stacked[1][index]])
        mine = lax.psum_scatter(both, MESH_AXES[0], scatter_dimension=0, tiled=False)
        dim = 0 if index < 8 else 1
        mine = lax.psum_scatter(mine, MESH_AXES[2], scatter_dimension=dim, tiled=True)
        result.append(lax.psum(mine, MESH_AXES[1]).astype(F32))
    up1, dn1, qkv, out, exp, prj, up2, dn2, gains, taps = result
    return up1, dn1, qkv, out, exp, taps, prj, up2, dn2, gains


def make_plan(mesh_shape, inputs, lengths, weights):
    plan = SimpleNamespace(token=None, lengths=lengths)
    plan.rows = inputs.shape[0]
    assert plan.rows == 4
    plan.dp, plan.seq = mesh_shape[MESH_AXES[1]], mesh_shape[MESH_AXES[2]]
    plan.length = inputs.shape[1] * plan.seq
    plan.frames = plan.rows * inputs.shape[1] // 2
    plan.halos = 1 if plan.seq == plan.rows else 2
    plan.direct = plan.dp == 4 and plan.seq == 4
    plan.blocks = plan.seq if plan.direct else 1
    plan.core = lax.axis_index(MESH_AXES[0])
    seq = plan.seq
    plan.to_right = [(q, seq + q) for q in range(seq)]
    plan.to_right += [(seq + q, q + plan.rows) for q in range(seq - plan.rows)]
    plan.to_left = [(b, a) for a, b in plan.to_right]
    plan.own = [w[0] for w in weights]
    return plan


def per_device(
    mesh_shape,
    inputs,
    cotangent,
    lengths,
    ffn_one_up,
    ffn_one_down,
    attn_project,
    attn_output,
    conv_expand,
    conv_depthwise,
    conv_project,
    ffn_two_up,
    ffn_two_down,
    norm_gains,
):
    matrices = (
        ffn_one_up, ffn_one_down, attn_project, attn_output, conv_expand, conv_project, ffn_two_up,
        ffn_two_down,
    )
    plan = make_plan(mesh_shape, inputs, lengths, matrices)
    direct = plan.direct
    (pieces, cotangent_pieces), plan.small_own = pick_rows(
        plan, (inputs, cotangent), norm_gains, conv_depthwise
    )
    plan.small_other = swap(plan.small_own)
    plan.other = [swap(w) for w in plan.own]

    def over(value):
        return swap(value) if direct else None

    def after(value, other):
        return lax.optimization_barrier((value, other))[0]

    def there(*values):
        return values if direct else ()

    first0 = call_first(plan, pieces)
    kvh0 = halo_exchange(plan, first0.kvs, W)
    mid0 = call_attend(plan, 0, first0, kvh0)
    gh0 = halo_exchange(plan, mid0.gsend, EDGE)
    turn = call_conv_first(plan, mid0, gh0)
    kvh1 = halo_exchange(plan, turn.kvs, W)
    got0 = SimpleNamespace(p1=over(first0.p1), p2=over(mid0.p2))
    mid1 = call_attend(plan, 1, turn, kvh1, there(got0.p1, got0.p2))
    gh1 = halo_exchange(plan, mid1.gsend, EDGE)
    got0.p3, got1 = over(turn.p3), SimpleNamespace(p1=over(turn.p1))
    end = call_conv_last(plan, mid1, gh1, cotangent_pieces, there(got0.p3, got1.p1))
    dzh1 = halo_exchange(plan, end.dzs, EDGE)
    launch(plan, lambda ctx: None, "between", {}, {}, limit=1)
    got1.c3, got1.p2 = over(after(end.c3, dzh1)), over(after(mid1.p2, dzh1))
    own1 = SimpleNamespace(
        p1=turn.p1, a1=turn.a1, p2=mid1.p2, c3=end.c3, a2=end.a2, k3=end.k3
    )
    own0 = SimpleNamespace(
        p1=first0.p1, a1=first0.a1, p2=mid0.p2, p3=turn.p3, a2=turn.a2
    )
    att1 = call_attend_back(plan, 1, turn, mid1, end, gh1, dzh1, ())
    back1 = halo_return(plan, att1.dkvh, W)
    own1.q2, own1.k2 = att1.q2, att1.k2
    if direct:
        two1 = call_bucket(plan, (0,), own1, got1)
    beg1 = call_first_back(plan, 1, turn.y, turn, att1, back1, there(got1.p2))
    own1.q1, own1.k1, own1.smalls = beg1.q1, beg1.k1, beg1.smalls
    got1.q1 = over(beg1.q1)
    last0 = call_last(plan, turn, beg1.ig, ())
    dzh0 = halo_exchange(plan, last0.dzs, EDGE)
    own0.q3, own0.k3 = last0.q3, last0.k3
    got0.q3 = over(last0.q3)
    if direct:
        one1 = call_bucket(plan, (2,), own1, got1)
    att0 = call_attend_back(plan, 0, first0, mid0, last0, gh0, dzh0, there(got0.q3))
    back0 = halo_return(plan, att0.dkvh, W)
    own0.q2, own0.k2 = att0.q2, att0.k2
    if direct:
        mid1b = call_bucket(plan, (1,), own1, got1)
    beg0 = call_first_back(plan, 0, first0.x, first0, att0, back0, ())
    own0.q1, own0.k1, own0.smalls = beg0.q1, beg0.k1, beg0.smalls
    got0.q1 = over(beg0.q1)
    keep, got = split_layers(plan, ((turn.y, beg0.ig), (end.y, beg1.ig)), ())
    if direct:
        two0 = call_bucket(plan, (0,), own0, got0)
    dealt = deal_rows(plan, keep, got)
    if direct:
        mid0b = call_bucket(plan, (1,), own0, got0)
        early1 = call_second(plan, [two1, mid1b])
        one0 = call_bucket(plan, (2,), own0, got0)
        one1 = call_second(plan, [one1])
    dealt = deal_far(plan, dealt)
    if direct:
        early0 = call_second(plan, [two0, mid0b])
        one1 = call_third(plan, [one1])
    framed = place_rows(plan, dealt)
    if direct:
        early1 = call_third(plan, [early1])
        one1 = call_fourth(plan, one1)
        early0 = call_third(plan, [early0])
        one0 = call_second(plan, [one0])
        early1 = call_fourth(plan, early1)
        one0 = call_third(plan, [one0])
        one1 = call_total(plan, one1)
        early0 = call_fourth(plan, early0)
        early1 = call_total(plan, early1)
        one1 = call_pair(plan, one1, 1)
        early1 = call_pair(plan, early1, 1)
        one0 = call_fourth(plan, one0)
        early0 = call_total(plan, early0)
        early0 = call_pair(plan, early0, 0)
        one0 = call_total(plan, one0)
        one0 = call_pair(plan, one0, 0)
        middle_at = ROWS[0]
        two = call_unpack(plan, 0, ((0, early0), (0, early1)))
        middle = call_unpack(plan, 1, ((middle_at, early0), (middle_at, early1)))
        one = call_unpack(plan, 2, ((0, one0), (0, one1)))
        results = (
            one.up, one.dn, one.qkv, middle.out, middle.exp, one.sml[6:15], middle.prj,
            two.up, two.dn, one.sml[0:6],
        )
    else:
        own1.p3, own1.q3 = end.c3[:, : 2 * D + FH], end.c3[:, 2 * D + FH :]
        results = plain_gradients(plan, (own0, own1))
    activations, input_grads = framed.activations, framed.input_grads
    return (activations[None], input_grads[None]) + tuple(r[None] for r in results)


def solution(mesh):
    section, dp, seq = MESH_AXES
    whole = P(section, None, None)
    sliced = P(section, seq, None)
    across = P(section, None, seq)
    framed = P(section, dp, seq, None)
    return jax.shard_map(
        functools.partial(per_device, dict(mesh.shape)),
        mesh=mesh,
        in_specs=(P(dp, seq, None), P(dp, seq, None), P(dp, None)) + (whole,) * 10,
        out_specs=(framed, framed) + (sliced,) * 5 + (across,) + (sliced,) * 3 + (across,),
        check_vma=False,
    )
```

```python
import functools
from types import SimpleNamespace

import jax
import jax.numpy as jnp
from jax import lax
from jax.experimental import pallas as pl
from jax.experimental.pallas import tpu as pltpu
from jax.sharding import PartitionSpec as P

D = 512
H = 8
HD = 64
F = 2048
FH = F // 2
K = 9
W = 128
UTT = 4
EPSILON = 1e-05
MASKED = -1e30
EDGE = 16
Q2_AT = D + FH + 3 * D // 2
CHUNK = 2048
MIB = 1024 * 1024
COST = 10**10
LIMITS = (16, 16, 20, 20, 16, 16, 16, 16)
MESH_AXES = ("section", "dp", "seq")

BF = jnp.bfloat16
F32 = jnp.float32

UP1, DN1, QKV, OUT, EXP, PRJ, UP2, DN2 = range(8)


def dot(a, b):
    return jnp.dot(a, b, preferred_element_type=F32)


def dot_nt(a, b):
    return lax.dot_general(a, b, (((1,), (1,)), ((), ())), preferred_element_type=F32)


def dot_tn(a, b):
    return lax.dot_general(a, b, (((0,), (0,)), ((), ())), preferred_element_type=F32)


def sigmoid(v):
    return 0.5 * jnp.tanh(0.5 * v) + 0.5


def norm_stats(v):
    centred = v - jnp.mean(v, axis=-1, keepdims=True)
    inverse = lax.rsqrt(jnp.mean(centred * centred, axis=-1, keepdims=True) + EPSILON)
    return centred * inverse, inverse


def norm_back(upstream, normed, inverse, gain):
    gain_grad = jnp.sum(upstream * normed, axis=0, keepdims=True)
    scaled = upstream * gain
    value_grad = inverse * (
        scaled
        - jnp.mean(scaled, axis=-1, keepdims=True)
        - normed * jnp.mean(scaled * normed, axis=-1, keepdims=True)
    )
    return value_grad, gain_grad


class Place:
    def __init__(self, plan, lengths):
        core, replica, chip = (lax.axis_index(name) for name in MESH_AXES)
        self.core, self.chip = core, chip
        self.row = lax.rem(chip, plan.rows)
        self.first = (lax.div(chip, plan.rows) * 2 + core) * plan.frames
        self.length = plan.length
        self.fast = lax.rem(replica, 2)
        self.slow = lax.rem(lax.div(replica, 2), 2)
        self.side1 = jnp.where(core == 0, self.fast, self.slow)
        self.side2 = jnp.where(core == 0, self.slow, self.fast)
        self.ends = []
        total = 0
        for u in range(UTT):
            total = total + lengths[self.row, u]
            self.ends.append(total)


class Ctx:
    def __init__(self, plan, place, table, held, waits):
        self.__dict__.update(place.__dict__)
        self.__dict__.update(table)
        self.plan = plan
        self.held = held
        self.waits = waits

    def weight(self, matrix, layer, part=None):
        queue = self.waits[(matrix, layer)]
        for index in range(len(queue)):
            if queue[index] is not None and (part is None or part == index):
                queue[index].wait()
                queue[index] = None
        return self.held[(matrix, layer)]

    def small(self, row, layer):
        mine = self.core == layer
        return jnp.where(mine, self.small_own[row : row + 1, :], self.small_other[row : row + 1, :])

    def taps(self, tap, layer):
        return self.small(6 + tap, layer)

    def segment(self, pos):
        start, stop = jnp.zeros(pos.shape, jnp.int32), jnp.full(pos.shape, self.length, jnp.int32)
        for end in self.ends:
            start = jnp.maximum(start, jnp.where(pos >= end, end, 0))
            stop = jnp.minimum(stop, jnp.where(pos >= end, self.length, end))
        return start, stop


def parts_of(matrix, shape):
    if matrix in (UP1, UP2):
        return [(slice(None), pl.ds(c, CHUNK)) for c in range(0, F, CHUNK)]
    if matrix in (DN1, DN2):
        return [(pl.ds(c, CHUNK), slice(None)) for c in range(0, F, CHUNK)]
    return [(slice(None), slice(None))]


def launch(plan, body, name, ins, outs, weights=(), scratch=None, far=None, results=None, settle=(),
           limit=16):
    scratch, far, results = scratch or {}, far or {}, results or {}
    near = dict(ins)
    near.update({"settle%d" % i: v for i, v in enumerate(settle)})
    if weights:
        near.update(small_own=plan.small_own, small_other=plan.small_other)
    if plan.token is not None:
        near.update(token_in=plan.token)
    pinned = [pltpu.with_memory_space_constraint(v, pltpu.VMEM) for v in near.values()]
    operands = [pltpu.with_memory_space_constraint(plan.lengths, pltpu.HBM)] + pinned
    operands += [pltpu.with_memory_space_constraint(v, pltpu.HBM) for v in far.values()]
    in_specs = [pl.BlockSpec(memory_space=pltpu.SMEM)]
    in_specs += [pl.BlockSpec(memory_space=pltpu.VMEM)] * len(near)
    in_specs += [pl.BlockSpec(memory_space=pl.ANY)] * len(far)
    copies = []
    for matrix, layer in weights:
        operands += [
            pltpu.with_memory_space_constraint(plan.own[matrix], pltpu.HBM),
            plan.other[matrix],
        ]
        in_specs += [pl.BlockSpec(memory_space=pl.ANY)] * 2
        copies.append(parts_of(matrix, plan.own[matrix].shape))
    held_shapes = [pltpu.VMEM(plan.own[m].shape, BF) for m, _ in weights]
    out_shape = [pltpu.VMEM(*s) for s in outs.values()]
    out_shape += [jax.ShapeDtypeStruct(*s) for s in results.values()]
    out_shape += [pltpu.VMEM((8, 128), jnp.int32)]
    out_specs = [pl.BlockSpec(memory_space=pltpu.VMEM)] * len(out_shape)
    sems = max(sum(len(c) for c in copies), 1) + 24

    def kernel(*refs):
        refs = list(refs)
        place = Place(plan, refs.pop(0))
        table = {}
        for n in list(near) + list(far):
            table[n] = refs.pop(0)
        sources = [(refs.pop(0), refs.pop(0)) for _ in weights]
        for n in list(outs) + list(results):
            table[n] = refs.pop(0)
        refs.pop(0)
        for n in scratch:
            table[n] = refs.pop(0)
        held_refs = [refs.pop(0) for _ in weights]
        sem = refs.pop(0)
        core = place.core
        held, waits = {}, {}
        for pair in weights:
            waits[pair] = []
        count = 0
        for part in range(max([len(c) for c in copies], default=0)):
            for pair, (own, other), into, slices in zip(weights, sources, held_refs, copies):
                held[pair] = into
                if part >= len(slices):
                    continue
                at = slices[part]

                @pl.when(core == pair[1])
                def _(own=own, into=into, at=at, count=count):
                    pltpu.make_async_copy(own.at[at], into.at[at], sem.at[count]).start()

                @pl.when(core != pair[1])
                def _(other=other, into=into, at=at, count=count):
                    pltpu.make_async_copy(other.at[at], into.at[at], sem.at[count]).start()

                waits[pair].append(pltpu.make_async_copy(own.at[at], into.at[at], sem.at[count]))
                count += 1
        ctx = Ctx(plan, place, table, held, waits)
        ctx.sems = [sem.at[sems - 24 + i] for i in range(24)]
        body(ctx)
        for pair in weights:
            ctx.weight(*pair)

    made = pl.pallas_call(
        kernel,
        out_shape=out_shape,
        in_specs=in_specs,
        out_specs=out_specs,
        scratch_shapes=[pltpu.VMEM(*s) for s in scratch.values()]
        + held_shapes
        + [pltpu.SemaphoreType.DMA((sems,))],
        compiler_params=pltpu.CompilerParams(vmem_limit_bytes=limit * MIB),
        cost_estimate=pl.CostEstimate(flops=COST, transcendentals=0, bytes_accessed=1),
        name=name,
    )(*operands)
    plan.token = made[-1]
    return SimpleNamespace(**dict(zip(list(outs) + list(results), made)))


def half_copies(ctx, value_ref, keep_ref, send_ref, keep_at, send_at, total, blocks):
    width = total // (2 * blocks)
    for j in range(blocks):
        mine = pl.multiple_of(j * 2 * width + ctx.core * width, width)
        theirs = pl.multiple_of(j * 2 * width + (1 - ctx.core) * width, width)
        keep_ref[:, keep_at + j * width : keep_at + (j + 1) * width] = value_ref[:, pl.ds(mine, width)]
        send_ref[:, send_at + j * width : send_at + (j + 1) * width] = value_ref[
            :, pl.ds(theirs, width)
        ]


def edge_rows(ctx, value_ref, send_ref, rows):
    frames = value_ref.shape[0]
    if ctx.plan.halos == 1:
        at = pl.multiple_of((1 - ctx.core) * (frames - rows), rows)
        send_ref[...] = value_ref[pl.ds(at, rows), :]
    else:
        send_ref[0:rows, :] = value_ref[frames - rows : frames, :]
        send_ref[rows : 2 * rows, :] = value_ref[0:rows, :]


def halo_starts(ctx, rows, frames):
    before = ctx.first - rows
    after = ctx.first + frames
    if ctx.plan.halos == 1:
        return [jnp.where(ctx.core == 0, after, before)]
    return [before, after]


def feed_forward(ctx, hidden, up, down, layer, keep_ref, send_ref, send_at, slope_ref):
    frames = hidden.shape[0]
    total = jnp.zeros((frames, D), F32)
    for part, c in enumerate(range(0, F, CHUNK)):
        at = slice(c, c + CHUNK)
        inner = dot(hidden, ctx.weight(up, layer, part)[:, at])
        logistic = sigmoid(inner)
        active = (inner * logistic).astype(BF)
        slope_ref[:, at] = (logistic * (1.0 + inner * (1.0 - logistic))).astype(BF)
        ctx.act[:, at] = active
        total = total + dot(active, ctx.weight(down, layer, part)[at, :])
    half_copies(ctx, ctx.act, keep_ref, send_ref, 0, send_at, F, ctx.plan.blocks)
    return total


def fwd_first(ctx, x, layer):
    normed, _ = norm_stats(x)
    hidden = (normed * ctx.small(0, layer)).astype(BF)
    ctx.p1[:, 0:D] = hidden
    ffn = feed_forward(ctx, hidden, UP1, DN1, layer, ctx.a1, ctx.p1, 2 * D, ctx.s1)
    r1 = x + 0.5 * ffn
    ctx.r1[...] = r1
    normed, _ = norm_stats(r1)
    hidden = (normed * ctx.small(1, layer)).astype(BF)
    ctx.p1[:, D : 2 * D] = hidden
    ctx.qkv[...] = dot(hidden, ctx.weight(QKV, layer)[...]).astype(BF)
    edge_rows(ctx, ctx.qkv.at[:, D : 3 * D], ctx.kvs, W)


def first_outs(plan):
    t = plan.frames
    return dict(
        p1=((t, 2 * D + FH), BF),
        a1=((t, FH), BF),
        s1=((t, F), BF),
        r1=((t, D), F32),
        qkv=((t, 3 * D), BF),
        kvs=((plan.halos * W, 2 * D), BF),
    )


def call_first(plan, pieces):
    def body(ctx):
        join_frames(ctx, ctx.x)
        fwd_first(ctx, ctx.x[...].astype(F32), 0)

    t = plan.frames
    return launch(
        plan, body, "first", pieces, dict(x=((t, D), BF), **first_outs(plan)),
        [(UP1, 0), (DN1, 0), (QKV, 0)], dict(act=((t, F), BF)), limit=LIMITS[0],
    )


def allowed_bias(ctx, key_start, keys):
    frames = ctx.plan.frames
    query = ctx.first + lax.broadcasted_iota(jnp.int32, (frames, 1), 0)
    start, stop = ctx.segment(query)
    low, high = jnp.maximum(start, query - W), jnp.minimum(stop - 1, query + W)
    key = key_start + lax.broadcasted_iota(jnp.int32, (frames, keys), 1)
    return jnp.where((key >= low) & (key <= high), 0.0, MASKED).astype(F32)


def stacked_heads(value, lane):
    zero = jnp.zeros_like(value)
    return jnp.concatenate([jnp.where(lane < HD, value, zero), jnp.where(lane < HD, zero, value)], axis=0)


def fwd_attend(ctx, layer):
    t = ctx.plan.frames
    halos = ctx.plan.halos
    qkv, probs, p2, bias, kx = ctx.qkv, ctx.probs, ctx.p2, ctx.bias, ctx.kx
    kx[0:t, :] = qkv[:, D : 3 * D]
    kx[t:, :] = ctx.kvh[...]
    starts = halo_starts(ctx, W, t)
    bias[:, 0:t] = allowed_bias(ctx, ctx.first, t)
    for h in range(halos):
        bias[:, t + h * W : t + (h + 1) * W] = allowed_bias(ctx, starts[h], W)
    lane = lax.broadcasted_iota(jnp.int32, (t, 2 * HD), 1)
    for p in range(H // 2):
        at = 2 * HD * p
        q = stacked_heads(qkv[:, at : at + 2 * HD] * jnp.asarray(HD ** (-0.5), BF), lane)
        scores = dot_nt(q, kx[:, at : at + 2 * HD]).reshape(2, t, -1) + bias[...][None]
        exponent = jnp.exp(scores - jnp.max(scores, axis=-1, keepdims=True))
        scale = 1.0 / jnp.sum(exponent, axis=-1, keepdims=True)
        weights = (exponent * scale).astype(BF).reshape(2 * t, -1)
        probs[p] = weights
        out = dot(weights, kx[:, D + at : D + at + 2 * HD])
        p2[:, at : at + 2 * HD] = jnp.where(lane < HD, out[0:t], out[t:]).astype(BF)
    r2 = ctx.r1[...] + dot(p2[:, 0:D], ctx.weight(OUT, layer)[...])
    ctx.r2[...] = r2
    normed, _ = norm_stats(r2)
    hidden = (normed * ctx.small(2, layer)).astype(BF)
    p2[:, D : 2 * D] = hidden
    expand = ctx.weight(EXP, layer)
    linear = dot(hidden, expand[:, 0:D])
    logistic = sigmoid(dot(hidden, expand[:, D : 2 * D]))
    gated = linear * logistic
    ctx.g[...] = gated.astype(BF)
    ctx.gs[...] = logistic.astype(BF)
    ctx.gt[...] = (gated * (1.0 - logistic)).astype(BF)
    edge_rows(ctx, ctx.g, ctx.gsend, EDGE)


def call_attend(plan, layer, first, kvh, settle=()):
    t = plan.frames
    keys = t + plan.halos * W
    return launch(
        plan,
        lambda ctx: fwd_attend(ctx, layer),
        "attend",
        dict(qkv=first.qkv, kvh=kvh, r1=first.r1),
        dict(
            probs=((H // 2, 2 * t, keys), BF),
            kx=((keys, 2 * D), BF),
            p2=((t, 2 * D), BF),
            r2=((t, D), F32),
            g=((t, D), BF),
            gs=((t, D), BF),
            gt=((t, D), BF),
            gsend=((plan.halos * EDGE, D), BF),
        ),
        [(OUT, layer), (EXP, layer)],
        dict(bias=((t, keys), F32)),
        settle=settle, limit=LIMITS[1],
    )


def fill_extended(ctx, ext, own, halo):
    t = ctx.plan.frames
    before = halo[EDGE - 8 : EDGE, :]
    after = halo[0:8, :] if ctx.plan.halos == 1 else halo[EDGE : EDGE + 8, :]
    ext[0:8, :] = before.astype(F32)
    ext[8 : 8 + t, :] = own[...].astype(F32)
    ext[8 + t : 16 + t, :] = after.astype(F32)


def tap_masks(ctx, row, rows):
    pos = ctx.first + row + lax.broadcasted_iota(jnp.int32, (rows, 128), 0)
    start, stop = ctx.segment(pos)
    before, after = pos - start, stop - pos
    return [(before >= K // 2 - k) if k <= K // 2 else (after > k - K // 2) for k in range(K)]


def mix_time(ctx, ext, z_ref, layer):
    t = ctx.plan.frames
    taps = [ctx.taps(k, layer) for k in range(K)]
    block = 64
    for row in range(0, t, block):
        masks = tap_masks(ctx, row, block)
        for c in range(0, D, 128):
            total = jnp.zeros((block, 128), F32)
            for k in range(K):
                at = 8 + row + k - K // 2
                window = ext[at : at + block, c : c + 128] * taps[k][:, c : c + 128]
                total = total + jnp.where(masks[k], window, 0.0)
            z_ref[row : row + block, c : c + 128] = total


def valid_rows(ctx):
    pos = ctx.first + lax.broadcasted_iota(jnp.int32, (ctx.plan.frames, 1), 0)
    return (pos < ctx.ends[UTT - 1]).astype(F32)


def fwd_conv(ctx, layer):
    fill_extended(ctx, ctx.ext, ctx.g, ctx.gh)
    mix_time(ctx, ctx.ext, ctx.z, layer)
    normed, _ = norm_stats(ctx.z[...])
    mixed = normed * ctx.small(3, layer)
    active = (mixed * sigmoid(mixed)).astype(BF)
    ctx.p3[:, 0:D] = active
    r3 = ctx.r2[...] + dot(active, ctx.weight(PRJ, layer)[...])
    ctx.r3[...] = r3
    normed, _ = norm_stats(r3)
    hidden = (normed * ctx.small(4, layer)).astype(BF)
    ctx.p3[:, D : 2 * D] = hidden
    ffn = feed_forward(ctx, hidden, UP2, DN2, layer, ctx.a2, ctx.p3, 2 * D, ctx.s2)
    r4 = r3 + 0.5 * ffn
    ctx.r4[...] = r4
    normed, _ = norm_stats(r4)
    result = (normed * ctx.small(5, layer) * valid_rows(ctx)).astype(BF)
    ctx.y[...] = result
    return result


def conv_outs(plan):
    t = plan.frames
    return dict(
        z=((t, D), F32),
        p3=((t, 2 * D + FH), BF),
        a2=((t, FH), BF),
        s2=((t, F), BF),
        r3=((t, D), F32),
        r4=((t, D), F32),
        y=((t, D), BF),
    )


def conv_scratch(plan):
    t = plan.frames
    return dict(ext=((t + 16, D), F32), act=((t, F), BF))


def call_conv_first(plan, mid, gh):
    def body(ctx):
        fwd_first(ctx, fwd_conv(ctx, 0).astype(F32), 1)

    return launch(
        plan, body, "conv_first", dict(g=mid.g, gh=gh, r2=mid.r2),
        dict(conv_outs(plan), **first_outs(plan)),
        [(PRJ, 0), (UP2, 0), (DN2, 0), (UP1, 1), (DN1, 1), (QKV, 1)],
        conv_scratch(plan), limit=LIMITS[2],
    )


def call_conv_last(plan, mid, gh, pieces, settle):
    outs = dict(conv_outs(plan), **last_outs(plan))
    del outs["p3"], outs["q3"]
    outs["c3"] = ((plan.frames, 2 * D + FH + D + FH + D // 2), BF)

    def body(ctx):
        ctx.p3, ctx.q3 = ctx.c3.at[:, 0 : 2 * D + FH], ctx.c3.at[:, 2 * D + FH :]
        fwd_conv(ctx, 1)
        join_frames(ctx, ctx.dy)
        bwd_last(ctx, ctx.dy[...], 1)

    return launch(
        plan, body, "conv_last", dict(g=mid.g, gh=gh, r2=mid.r2, **pieces), outs,
        [(PRJ, 1), (UP2, 1), (DN2, 1)],
        dict(conv_scratch(plan), dy=((plan.frames, D), BF)), settle=settle, limit=LIMITS[3],
    )


def feed_forward_back(ctx, step, up, down, layer, slope_ref, keep_ref, send_ref, send_at):
    total = jnp.zeros((step.shape[0], D), F32)
    for part, c in enumerate(range(0, F, CHUNK)):
        at = slice(c, c + CHUNK)
        grad = dot_nt(step, ctx.weight(down, layer, part)[at, :]) * slope_ref[:, at].astype(F32)
        grad = grad.astype(BF)
        ctx.act[:, at] = grad
        total = total + dot_nt(grad, ctx.weight(up, layer, part)[:, at])
    half_copies(ctx, ctx.act, keep_ref, send_ref, 0, send_at, F, 1)
    return total


def bwd_last(ctx, dy, layer):
    upstream = dy.astype(F32) * valid_rows(ctx)
    smalls = ctx.smalls
    smalls[...] = jnp.zeros(smalls.shape, F32)
    normed, inverse = norm_stats(ctx.r4[...])
    stream, gg = norm_back(upstream, normed, inverse, ctx.small(5, layer))
    smalls[5:6, :] = gg
    step = (0.5 * stream).astype(BF)
    ctx.q3[:, 0:D] = step
    inner = feed_forward_back(ctx, step, UP2, DN2, layer, ctx.s2, ctx.k3, ctx.q3, D)
    normed, inverse = norm_stats(ctx.r3[...])
    branch, gg = norm_back(inner, normed, inverse, ctx.small(4, layer))
    smalls[4:5, :] = gg
    stream = stream + branch
    ctx.dr3[...] = stream
    step = stream.astype(BF)
    ctx.act[:, 0:D] = step
    half_copies(ctx, ctx.act.at[:, 0:D], ctx.k3, ctx.q3, FH, D + FH, D, 1)
    normed, inverse = norm_stats(ctx.z[...])
    gain = ctx.small(3, layer)
    mixed = normed * gain
    logistic = sigmoid(mixed)
    slope = logistic * (1.0 + mixed * (1.0 - logistic))
    mix, gg = norm_back(dot_nt(step, ctx.weight(PRJ, layer)[...]) * slope, normed, inverse, gain)
    smalls[3:4, :] = gg
    ctx.dz[...] = mix.astype(BF)
    edge_rows(ctx, ctx.dz, ctx.dzs, EDGE)


def last_outs(plan):
    t = plan.frames
    return dict(
        smalls=((16, D), F32),
        q3=((t, D + FH + D // 2), BF),
        k3=((t, FH + D // 2), BF),
        dr3=((t, D), F32),
        dz=((t, D), BF),
        dzs=((plan.halos * EDGE, D), BF),
    )


def call_last(plan, late, dy, settle):
    t = plan.frames
    return launch(
        plan, lambda ctx: bwd_last(ctx, ctx.dy[...], 0), "last",
        dict(dy=dy, r4=late.r4, r3=late.r3, z=late.z, s2=late.s2),
        last_outs(plan),
        [(DN2, 0), (UP2, 0), (PRJ, 0)],
        dict(act=((t, F), BF)),
        settle=settle, limit=LIMITS[4],
    )


def mix_time_back(ctx, layer):
    t = ctx.plan.frames
    grads, gated = ctx.ext, ctx.ext2
    weights = [ctx.taps(k, layer) for k in range(K)]
    block = 64
    taps = [[jnp.zeros((8, 128), F32) for _ in range(D // 128)] for _ in range(K)]
    for row in range(0, t, block):
        masks = tap_masks(ctx, row, block)
        for ci, c in enumerate(range(0, D, 128)):
            own = grads[8 + row : 8 + row + block, c : c + 128]
            total = jnp.zeros((block, 128), F32)
            for k in range(K):
                at = 8 + row + k - K // 2
                product = jnp.where(masks[k], own * gated[at : at + block, c : c + 128], 0.0)
                taps[k][ci] = taps[k][ci] + jnp.sum(product.reshape(block // 8, 8, 128), axis=0)
                window = grads[at : at + block, c : c + 128] * weights[K - 1 - k][:, c : c + 128]
                total = total + jnp.where(masks[k], window, 0.0)
            ctx.dg[row : row + block, c : c + 128] = total
    for k in range(K):
        for ci, c in enumerate(range(0, D, 128)):
            ctx.smalls[6 + k : 7 + k, c : c + 128] = jnp.sum(taps[k][ci], axis=0, keepdims=True)


def bwd_attend(ctx, layer):
    t = ctx.plan.frames
    fill_extended(ctx, ctx.ext, ctx.dz, ctx.dzh)
    fill_extended(ctx, ctx.ext2, ctx.g, ctx.gh)
    ctx.smalls[...] = ctx.smalls_in[...]
    mix_time_back(ctx, layer)
    gated = ctx.dg[...]
    act = ctx.act
    act[:, 0:D] = (gated * ctx.gs[...].astype(F32)).astype(BF)
    act[:, D : 2 * D] = (gated * ctx.gt[...].astype(F32)).astype(BF)
    half_copies(ctx, act, ctx.k2, ctx.q2, 0, 0, 2 * D, 1)
    normed, inverse = norm_stats(ctx.r2[...])
    branch, gg = norm_back(
        dot_nt(act[...], ctx.weight(EXP, layer)[...]), normed, inverse, ctx.small(2, layer)
    )
    ctx.smalls[2:3, :] = gg
    stream = ctx.dr3[...] + branch
    ctx.dr2[...] = stream
    step = stream.astype(BF)
    act[:, 0:D] = step
    half_copies(ctx, act.at[:, 0:D], ctx.k2, ctx.q2, D, D, D, 1)
    grad_o = ctx.do
    grad_o[...] = dot_nt(step, ctx.weight(OUT, layer)[...]).astype(BF)
    qkv, probs, p2, kx = ctx.qkv, ctx.probs, ctx.p2, ctx.kx
    lane = lax.broadcasted_iota(jnp.int32, (t, 2 * HD), 1)
    scale = HD ** (-0.5)
    for p in range(H // 2):
        at = 2 * HD * p
        q = stacked_heads(qkv[:, at : at + 2 * HD] * jnp.asarray(scale, BF), lane)
        do = grad_o[:, at : at + 2 * HD]
        spread = stacked_heads(do.astype(F32) * p2[:, at : at + 2 * HD].astype(F32), lane)
        do = stacked_heads(do, lane)
        delta = jnp.sum(spread, axis=-1, keepdims=True)
        weights = probs[p]
        grad = dot_nt(do, kx[:, D + at : D + at + 2 * HD]) - delta
        grad = (weights.astype(F32) * grad).astype(BF)
        dq = dot(grad, kx[:, at : at + 2 * HD]) * scale
        ctx.dq[:, at : at + 2 * HD] = jnp.where(lane < HD, dq[0:t], dq[t:]).astype(BF)
        dk, dv = dot_tn(grad, q), dot_tn(weights, do)
        ctx.dkv[:, at : at + 2 * HD] = dk[0:t]
        ctx.dkv[:, D + at : D + at + 2 * HD] = dv[0:t]
        ctx.dkvh[:, at : at + 2 * HD] = dk[t:].astype(BF)
        ctx.dkvh[:, D + at : D + at + 2 * HD] = dv[t:].astype(BF)


def call_attend_back(plan, layer, first, mid, last, gh, dzh, settle):
    t = plan.frames
    return launch(
        plan,
        lambda ctx: bwd_attend(ctx, layer),
        "attend_back",
        dict(
            dz=last.dz, dzh=dzh, dr3=last.dr3, smalls_in=last.smalls,
            g=mid.g, gh=gh, gs=mid.gs, gt=mid.gt, r2=mid.r2,
            probs=mid.probs, p2=mid.p2, qkv=first.qkv, kx=mid.kx,
        ),
        dict(
            smalls=((16, D), F32),
            q2=((t, D + D // 2), BF),
            k2=((t, D + D // 2), BF),
            dr2=((t, D), F32),
            dq=((t, D), BF),
            dkv=((t, 2 * D), F32),
            dkvh=((plan.halos * W, 2 * D), BF),
        ),
        [(EXP, layer), (OUT, layer)],
        dict(
            ext=((t + 16, D), F32), ext2=((t + 16, D), F32), dg=((t, D), F32),
            act=((t, 2 * D), BF), do=((t, D), BF),
        ),
        settle=settle, limit=LIMITS[5],
    )


def bwd_first(ctx, layer):
    t = ctx.plan.frames
    ctx.smalls[...] = ctx.smalls_in[...]
    grads, acc, back = ctx.act, ctx.acc, ctx.back
    grads[:, 0:D] = ctx.dq[...]
    acc[...] = ctx.dkv[...]
    if ctx.plan.halos == 1:
        at = pl.multiple_of((1 - ctx.core) * (t - W), W)
        acc[pl.ds(at, W), :] += back[...].astype(F32)
    else:
        acc[t - W : t, :] += back[0:W, :].astype(F32)
        acc[0:W, :] += back[W : 2 * W, :].astype(F32)
    grads[:, D : 3 * D] = acc[...].astype(BF)
    half_copies(ctx, grads.at[:, 0 : 3 * D], ctx.k1, ctx.q1.at[0:t], FH, D + FH, 3 * D, 1)
    normed, inverse = norm_stats(ctx.r1[...])
    branch, gg = norm_back(
        dot_nt(grads[:, 0 : 3 * D], ctx.weight(QKV, layer)[...]), normed, inverse, ctx.small(1, layer)
    )
    ctx.smalls[1:2, :] = gg
    stream = ctx.dr2[...] + branch
    step = (0.5 * stream).astype(BF)
    ctx.q1[0:t, 0:D] = step
    inner = feed_forward_back(ctx, step, UP1, DN1, layer, ctx.s1, ctx.k1, ctx.q1.at[0:t], D)
    normed, inverse = norm_stats(ctx.x[...].astype(F32))
    branch, gg = norm_back(inner, normed, inverse, ctx.small(0, layer))
    ctx.smalls[0:1, :] = gg
    ctx.ig[...] = (stream + branch).astype(BF)
    ctx.q1[t : t + EDGE, 0:D] = ctx.smalls[...].astype(BF)
    ctx.q1[0:t, Q2_AT : Q2_AT + D + D // 2] = ctx.q2[...]


def call_first_back(plan, layer, x, first, att, back, settle):
    t = plan.frames
    return launch(
        plan,
        lambda ctx: bwd_first(ctx, layer),
        "first_back",
        dict(
            x=x, r1=first.r1, s1=first.s1, dr2=att.dr2, dq=att.dq, dkv=att.dkv, back=back,
            smalls_in=att.smalls, q2=att.q2,
        ),
        dict(
            smalls=((16, D), F32),
            q1=((t + EDGE, Q2_AT + D + D // 2), BF),
            k1=((t, FH + 3 * D // 2), BF),
            ig=((t, D), BF),
        ),
        [(QKV, layer), (DN1, layer), (UP1, layer)],
        dict(act=((t, F), BF), acc=((t, 2 * D), F32)),
        settle=settle, limit=LIMITS[6],
    )


ROWS = (128, 64, 192)


def both_tn(left, left_got, right, right_got):
    return dot_tn(left, right) + dot_tn(left_got, right_got)


def put_part(ref, value, q, at, col):
    width = value.shape[1]
    for b in range(2):
        ref[b, q, at : at + 64, col : col + width] = value[64 * b : 64 * (b + 1), :].astype(BF)


def put_ffn(ref, a, row, step, step_got, hid, hid_got, act, fwd_got, inner, bwd_got):
    for q in range(4):
        at = pl.multiple_of(q * 256 + a * 128, 128)
        got = pl.multiple_of(2 * D + q * 256 + a * 128, 128)
        value = both_tn(act[:, pl.ds(at, 128)], fwd_got[:, pl.ds(got, 128)], step, step_got)
        put_part(ref, value, q, row, 0)
    at = pl.multiple_of(a * D, D)
    got = pl.multiple_of(D + a * D, D)
    value = both_tn(hid, hid_got, inner[:, pl.ds(at, D)], bwd_got[:, pl.ds(got, D)])
    for q in range(4):
        put_part(ref, value[q * 128 : (q + 1) * 128, :], q, row + 64, 0)


def put_matrix(ref, a, left, left_got, left_at, right, own_at, right_got, got_at, width, at, col):
    own = pl.multiple_of(own_at + a * width, 128)
    got = pl.multiple_of(got_at + a * width, 128)
    value = both_tn(
        left[:, left_at : left_at + D], left_got[:, left_at : left_at + D],
        right[:, pl.ds(own, width)], right_got[:, pl.ds(got, width)],
    )
    for q in range(4):
        put_part(ref, value[q * 128 : (q + 1) * 128, :], q, at, col)


def call_bucket(plan, kinds, f, g):
    joint = hasattr(f, "c3")

    def body(ctx):
        side = ctx.side1
        t = plan.frames
        if joint and kinds != (2,):
            cut = 2 * D + FH
            ctx.p3, ctx.q3 = ctx.c3.at[:, 0:cut], ctx.c3.at[:, cut:]
            ctx.p3_got, ctx.q3_got = ctx.c3_got.at[:, 0:cut], ctx.c3_got.at[:, cut:]
        if kinds != (0,):
            q1_got = ctx.q1_got.at[0:t]
            q2_got = ctx.q1_got.at[0:t, Q2_AT : Q2_AT + D + D // 2]
        if 2 in kinds:
            small = ctx.smalls[...] + ctx.q1_got[t : t + EDGE, 0:D].astype(F32)
            small = jnp.where(ctx.core == 0, small[0:8], small[8:16])
            small = jnp.concatenate([small, jnp.zeros((56, D), F32)], axis=0).astype(BF)
        for ref, a in ((ctx.send, 1 - side), (ctx.keep, side)):
            at = 0
            if 0 in kinds:
                put_ffn(
                    ref, a, at, ctx.q3[:, 0:D], ctx.q3_got[:, 0:D], ctx.p3[:, D : 2 * D],
                    ctx.p3_got[:, D : 2 * D], ctx.a2, ctx.p3_got, ctx.k3, ctx.q3_got,
                )
                at += ROWS[0]
            if 1 in kinds:
                put_matrix(ref, a, ctx.p2, ctx.p2_got, D, ctx.k2, 0, q2_got, 0, 256, at, 0)
                put_matrix(ref, a, ctx.p2, ctx.p2_got, 0, ctx.k2, D, q2_got, D, 128, at, 256)
                put_matrix(ref, a, ctx.p3, ctx.p3_got, 0, ctx.k3, FH, ctx.q3_got, D + FH, 128, at, 384)
                at += ROWS[1]
            if 2 in kinds:
                put_ffn(
                    ref, a, at, ctx.q1[0:t, 0:D], ctx.q1_got[0:t, 0:D], ctx.p1[:, 0:D],
                    ctx.p1_got[:, 0:D], ctx.a1, ctx.p1_got, ctx.k1, q1_got,
                )
                put_matrix(
                    ref, a, ctx.p1, ctx.p1_got, D, ctx.k1, FH, q1_got, D + FH, 384, at + 128, 0
                )
                for q in range(4):
                    for b in range(2):
                        ref[b, q, at + 128 : at + 192, 384:512] = small[:, q * 128 : (q + 1) * 128]

    ins = {}
    names = ()
    if 2 in kinds:
        names += ("p1", "q1")
        ins.update(a1=f.a1, k1=f.k1, smalls=f.smalls)
    if kinds != (2,):
        names += ("c3",) if joint else ("p3", "q3")
        ins.update(k3=f.k3)
    if 0 in kinds:
        ins.update(a2=f.a2)
    if 1 in kinds:
        names += ("p2",)
        ins.update(k2=f.k2, q1_got=g.q1)
    for name in names:
        ins[name] = getattr(f, name)
        ins[name + "_got"] = getattr(g, name)
    shape = (2, 4, sum(ROWS[k] for k in kinds), D)
    part = launch(plan, body, "bucket", ins, dict(send=(shape, BF), keep=(shape, BF)), limit=LIMITS[7])
    part.got = exchange(plan, part.send, 0)
    return part


def exchange(plan, value, stage):
    pairs = []
    for core in range(2):
        bit = 1 if (core == 0) == (stage == 0) else 2
        pairs += [(core * 4 + i, core * 4 + (i ^ bit)) for i in range(4)]
    return lax.ppermute(value, MESH_AXES[:2], pairs)


def call_second(plan, parts):
    count = len(parts)
    rows = [p.keep.shape[2] for p in parts]

    def body(ctx):
        side = ctx.side2
        for ref, at in ((ctx.send, 1 - side), (ctx.mine, side)):
            row = 0
            for i in range(count):
                keep, got = getattr(ctx, "m%d" % i), getattr(ctx, "g%d" % i)
                value = keep[at].astype(F32) + got[at].astype(F32)
                ref[:, row : row + rows[i], :] = value.astype(BF)
                row += rows[i]

    ins = {"m%d" % i: p.keep for i, p in enumerate(parts)}
    ins.update({"g%d" % i: p.got for i, p in enumerate(parts)})
    shape = (4, sum(rows), D)
    half = launch(plan, body, "second", ins, dict(send=(shape, BF), mine=(shape, BF)), limit=16)
    half.got = exchange(plan, half.send, 1)
    return half


def call_third(plan, halves):
    rows = [h.mine.shape[1] for h in halves]

    def body(ctx):
        side = lax.rem(ctx.chip, 2)
        for ref, near in ((ctx.send, 1 - side), (ctx.mine, side)):
            at = 0
            for i, count in enumerate(rows):
                mine, got = getattr(ctx, "m%d" % i), getattr(ctx, "g%d" % i)
                for far in range(2):
                    q = 2 * far + near
                    value = mine[q].astype(F32) + got[q].astype(F32)
                    ref[far, at : at + count, :] = value.astype(BF)
                at += count

    ins = {"m%d" % i: h.mine for i, h in enumerate(halves)}
    ins.update({"g%d" % i: h.got for i, h in enumerate(halves)})
    shape = (2, sum(rows), D)
    made = launch(plan, body, "third", ins, dict(send=(shape, BF), mine=(shape, BF)), limit=4)
    made.got = exchange_seq(made.send, 1)
    return made


def call_fourth(plan, half):
    def body(ctx):
        side = lax.div(ctx.chip, 2)
        for ref, at in ((ctx.send, 1 - side), (ctx.mine, side)):
            ref[...] = (ctx.keep[at].astype(F32) + ctx.got[at].astype(F32)).astype(BF)

    shape = half.mine.shape[1:]
    made = launch(
        plan, body, "fourth", dict(keep=half.mine, got=half.got),
        dict(send=(shape, BF), mine=(shape, BF)), limit=4,
    )
    made.got = exchange_seq(made.send, 2)
    return made


def exchange_seq(value, bit):
    return lax.ppermute(value, MESH_AXES[2], [(i, i ^ bit) for i in range(4)])


def call_total(plan, half):
    def body(ctx):
        ctx.own[...] = (ctx.mine[...].astype(F32) + ctx.got[...].astype(F32)).astype(BF)

    total = launch(
        plan, body, "total", dict(mine=half.mine, got=half.got), dict(own=(half.mine.shape, BF)), limit=4
    )
    total.got = exchange(plan, total.own, 1)
    return total


def call_pair(plan, total):
    def body(ctx):
        ctx.pair[ctx.side2] = ctx.own[...]
        ctx.pair[1 - ctx.side2] = ctx.got[...]

    shape = (2,) + total.own.shape
    pair = launch(
        plan, body, "pair", dict(own=total.own, got=total.got), dict(pair=(shape, BF)), limit=4
    ).pair
    return pair, exchange(plan, pair, 0)


def call_cross(plan, layers):
    def body(ctx):
        for layer in range(2):

            @pl.when(ctx.core != layer)
            def _(layer=layer):
                for i in range(2):
                    ctx.send[i] = getattr(ctx, "l%d_%d" % (layer, i))[...]

    ins = {"l%d_%d" % (l, i): v for l in range(2) for i, v in enumerate(layers[l])}
    shape = (2,) + layers[0][0].shape
    return swap(launch(plan, body, "cross", ins, dict(send=(shape, BF)), limit=4).send)


def swap(value):
    return lax.ppermute(value, MESH_AXES[0], [(0, 1), (1, 0)])


def call_unpack(plan, which, starts, layers, crossed):
    ins = {"l%d_%d" % (l, i): v for l in range(2) for i, v in enumerate(layers[l])}
    ins.update(crossed=crossed)
    ffn = dict(up=((128, F), F32), dn=((512, D), F32))
    rest = dict(out=((128, D), F32), exp=((128, 2 * D), F32), prj=((128, D), F32))
    last = dict(qkv=((128, 3 * D), F32), gains=((6, 128), F32), taps=((9, 128), F32))
    results = (ffn, rest, dict(ffn, **last))[which]

    def body(ctx):
        for layer in range(2):

            @pl.when(ctx.core == layer)
            def _(layer=layer):
                start = starts[layer]
                for k in range(4):
                    half = layer if k < 2 else 1 - layer
                    side = ctx.fast if half == 0 else ctx.slow
                    a = side if k % 2 == 0 else 1 - side
                    source = getattr(ctx, "l%d_%d" % (layer, k)) if k < 2 else ctx.crossed.at[k - 2]
                    for b in range(2):
                        rows = slice(64 * b, 64 * b + 64)
                        first = source[b, start : start + 64, :].astype(F32)
                        if which != 1:
                            at = pl.multiple_of(half * 256 + a * 128 + b * 64, 64)
                            ctx.dn[pl.ds(at, 64), :] = first
                            at = pl.multiple_of(half * FH + a * D, D)
                            ctx.up[rows, pl.ds(at, D)] = source[b, start + 64 : start + 128, :].astype(F32)
                        else:
                            at = pl.multiple_of(half * 512 + a * 256, 256)
                            ctx.exp[rows, pl.ds(at, 256)] = first[:, 0:256]
                            at = pl.multiple_of(half * 256 + a * 128, 128)
                            ctx.out[rows, pl.ds(at, 128)] = first[:, 256:384]
                            ctx.prj[rows, pl.ds(at, 128)] = first[:, 384:512]
                        if which == 2:
                            third = source[b, start + 128 : start + 192, :].astype(F32)
                            at = pl.multiple_of(half * 768 + a * 384, 128)
                            ctx.qkv[rows, pl.ds(at, 384)] = third[:, 0:384]
                            if k % 2 == 0 and b == 0:
                                small = third[0:8, 384:512]
                                if half == 0:
                                    ctx.gains[...] = small[0:6]
                                    ctx.taps[0:2, :] = small[6:8]
                                else:
                                    ctx.taps[2:9, :] = small[0:7]

    return launch(plan, body, "unpack", ins, {}, results=results, limit=16)


def pick_rows(plan, arrays, gains, taps):
    size = arrays[0].shape[1]
    half = plan.rows // 2

    def body(ctx):
        near = lax.div(ctx.row, half) == ctx.core
        copies = []
        for i in range(len(arrays)):
            source = getattr(ctx, "value%d" % i)
            for k in range(3):
                other = jnp.where(near, k, (0, 2, 3, 1)[k])
                copies.append(
                    pltpu.make_async_copy(
                        source.at[ctx.row ^ other], getattr(ctx, "p%d_%d" % (i, k)), ctx.sems[len(copies)]
                    )
                )
        small = [
            pltpu.make_async_copy(ctx.gains, ctx.gains_in, ctx.sems[20]),
            pltpu.make_async_copy(ctx.taps, ctx.taps_in, ctx.sems[21]),
        ]
        for copy in small + copies:
            copy.start()
        for copy in small:
            copy.wait()
        ctx.small[0:6, :] = ctx.gains_in[0].astype(F32)
        ctx.small[6:15, :] = ctx.taps_in[0].astype(F32)
        ctx.small[15:16, :] = jnp.zeros((1, D), F32)
        for copy in copies:
            copy.wait()

    names = [["p%d_%d" % (i, k) for k in range(3)] for i in range(len(arrays))]
    outs = {n: ((size, D), BF) for group in names for n in group}
    far = {"value%d" % i: v for i, v in enumerate(arrays)}
    picked = launch(
        plan, body, "pick_rows", {}, dict(outs, small=((16, D), F32)),
        scratch=dict(gains_in=((1, 6, D), BF), taps_in=((1, 9, D), BF)),
        far=dict(far, gains=gains, taps=taps), limit=4,
    )
    result = []
    for group in names:
        sent = [getattr(picked, n) for n in group]
        both, third = [], []
        for chip in range(plan.seq):
            c = (chip % 4) // 2
            both.append((c * plan.seq + chip, c * plan.seq + (chip ^ 1)))
            both.append(((1 - c) * plan.seq + chip, c * plan.seq + (chip ^ 2)))
            third.append(((1 - c) * plan.seq + chip, c * plan.seq + (chip ^ 3)))
        pieces = [
            sent[0], lax.ppermute(sent[1], MESH_AXES[::2], both),
            lax.ppermute(sent[2], MESH_AXES[::2], third),
        ]
        result.append({"piece%d" % k: v for k, v in enumerate(pieces)})
    return result, picked.small


def join_frames(ctx, target):
    plan = ctx.plan
    half = plan.rows // 2
    size = plan.frames // half
    near = lax.div(ctx.row, half) == ctx.core

    def put(piece, source):
        at = pl.multiple_of(lax.rem(source, half) * size, size)
        target[pl.ds(at, size), :] = piece[...]

    @pl.when(near)
    def _():
        put(ctx.piece0, ctx.row)
        put(ctx.piece1, ctx.row ^ 1)

    @pl.when(jnp.logical_not(near))
    def _():
        put(ctx.piece1, ctx.row ^ 2)
        put(ctx.piece2, ctx.row ^ 3)


def split_layers(plan, layers, settle):
    count = len(layers[0])

    def body(ctx):
        for layer in range(2):
            for i in range(count):
                value = getattr(ctx, "l%d_%d" % (layer, i))

                @pl.when(ctx.core == layer)
                def _(value=value, i=i):
                    ctx.keep[i] = value[...]

                @pl.when(ctx.core != layer)
                def _(value=value, i=i):
                    ctx.send[i] = value[...]

    shape = (count, plan.frames, D)
    ins = {"l%d_%d" % (l, i): v for l in range(2) for i, v in enumerate(layers[l])}
    out = launch(
        plan, body, "split", ins, dict(keep=(shape, BF), send=(shape, BF)), settle=settle, limit=16
    )
    return out.keep, swap(out.send)


def chips_apart(plan, value, bit):
    pairs = [(c * plan.seq + i, c * plan.seq + (i ^ bit)) for c in range(2) for i in range(plan.seq)]
    return lax.ppermute(value, MESH_AXES[::2], pairs)


def deal_rows(plan, keep, got):
    size = plan.frames // 2

    def body(ctx):
        for distance, target in ((0, ctx.rest.at[0]), (2, ctx.rest.at[1]), (1, ctx.near.at[0]), (3, ctx.near.at[1])):
            chip = ctx.row ^ distance
            at = pl.multiple_of(lax.rem(chip, 2) * size, size)

            @pl.when(lax.div(chip, 2) == ctx.core)
            def _(target=target, at=at):
                target[...] = ctx.keep[:, pl.ds(at, size), :]

            @pl.when(lax.div(chip, 2) != ctx.core)
            def _(target=target, at=at):
                target[...] = ctx.got[:, pl.ds(at, size), :]

    shape = (2, keep.shape[0], size, D)
    dealt = launch(
        plan, body, "deal_rows", dict(keep=keep, got=got), dict(near=(shape, BF), rest=(shape, BF)), limit=8
    )
    dealt.got = chips_apart(plan, dealt.near, 1)
    return dealt


def deal_far(plan, dealt):
    def body(ctx):
        ctx.far[0] = ctx.rest[1]
        ctx.far[1] = ctx.got[1]

    dealt.far = launch(
        plan, body, "deal_far", dict(rest=dealt.rest, got=dealt.got),
        dict(far=(dealt.rest.shape, BF)), limit=8,
    ).far
    dealt.far_got = chips_apart(plan, dealt.far, 2)
    return dealt


def place_rows(plan, dealt):
    def body(ctx):
        pieces = (ctx.rest.at[0], ctx.got.at[0], ctx.far.at[0], ctx.far.at[1])
        for distance, piece in enumerate(pieces):
            ctx.activations[ctx.row ^ distance] = piece[0]
            ctx.input_grads[ctx.row ^ distance] = piece[1].astype(F32)

    shape = (plan.rows,) + dealt.rest.shape[2:]
    return launch(
        plan, body, "place_rows", dict(rest=dealt.rest, got=dealt.got, far=dealt.far_got), {},
        results=dict(activations=(shape, BF), input_grads=(shape, F32)), limit=8,
    )


def halo_exchange(plan, send, rows):
    if plan.halos == 1:
        return swap(send)
    return jnp.concatenate(
        [
            lax.ppermute(send[0:rows], MESH_AXES[::2], plan.to_right),
            lax.ppermute(send[rows:], MESH_AXES[::2], plan.to_left),
        ],
        axis=0,
    )


def halo_return(plan, grads, rows):
    if plan.halos == 1:
        return swap(grads)
    return jnp.concatenate(
        [
            lax.ppermute(grads[0:rows], MESH_AXES[::2], plan.to_left),
            lax.ppermute(grads[rows:], MESH_AXES[::2], plan.to_right),
        ],
        axis=0,
    )


def plain_gradients(plan, layers):
    def whole(keep, send):
        return jnp.where(
            plan.core == 0,
            jnp.concatenate([keep, send], axis=1),
            jnp.concatenate([send, keep], axis=1),
        )

    stacked = []
    for f in layers:
        p1, p2, p3, q1, q2, q3, k1, k2, k3 = f.p1, f.p2, f.p3, f.q1, f.q2, f.q3, f.k1, f.k2, f.k3
        q1 = q1[: plan.frames]
        operands = (
            (p1[:, :D], whole(k1[:, :FH], q1[:, D : D + FH])),
            (whole(f.a1, p1[:, 2 * D :]), q1[:, :D]),
            (p1[:, D : 2 * D], whole(k1[:, FH:], q1[:, D + FH : Q2_AT])),
            (p2[:, :D], whole(k2[:, D:], q2[:, D:])),
            (p2[:, D:], whole(k2[:, :D], q2[:, :D])),
            (p3[:, :D], whole(k3[:, FH:], q3[:, D + FH :])),
            (p3[:, D : 2 * D], whole(k3[:, :FH], q3[:, D : D + FH])),
            (whole(f.a2, p3[:, 2 * D :]), q3[:, :D]),
        )
        grads = [dot_tn(a, b).astype(BF) for a, b in operands]
        grads.append(f.smalls[0:6].astype(BF))
        grads.append(f.smalls[6:15].astype(BF))
        stacked.append(grads)
    result = []
    for index in range(10):
        both = jnp.stack([stacked[0][index], stacked[1][index]])
        mine = lax.psum_scatter(both, MESH_AXES[0], scatter_dimension=0, tiled=False)
        dim = 0 if index < 8 else 1
        mine = lax.psum_scatter(mine, MESH_AXES[2], scatter_dimension=dim, tiled=True)
        result.append(lax.psum(mine, MESH_AXES[1]).astype(F32))
    up1, dn1, qkv, out, exp, prj, up2, dn2, gains, taps = result
    return up1, dn1, qkv, out, exp, taps, prj, up2, dn2, gains


def make_plan(mesh_shape, inputs, lengths, weights):
    plan = SimpleNamespace(token=None, lengths=lengths)
    plan.rows = inputs.shape[0]
    assert plan.rows == 4
    plan.dp, plan.seq = mesh_shape[MESH_AXES[1]], mesh_shape[MESH_AXES[2]]
    plan.length = inputs.shape[1] * plan.seq
    plan.frames = plan.rows * inputs.shape[1] // 2
    plan.halos = 1 if plan.seq == plan.rows else 2
    plan.direct = plan.dp == 4 and plan.seq == 4
    plan.blocks = plan.seq if plan.direct else 1
    plan.core = lax.axis_index(MESH_AXES[0])
    seq = plan.seq
    plan.to_right = [(q, seq + q) for q in range(seq)]
    plan.to_right += [(seq + q, q + plan.rows) for q in range(seq - plan.rows)]
    plan.to_left = [(b, a) for a, b in plan.to_right]
    plan.own = [w[0] for w in weights]
    return plan


def per_device(
    mesh_shape,
    inputs,
    cotangent,
    lengths,
    ffn_one_up,
    ffn_one_down,
    attn_project,
    attn_output,
    conv_expand,
    conv_depthwise,
    conv_project,
    ffn_two_up,
    ffn_two_down,
    norm_gains,
):
    matrices = (
        ffn_one_up, ffn_one_down, attn_project, attn_output, conv_expand, conv_project, ffn_two_up,
        ffn_two_down,
    )
    plan = make_plan(mesh_shape, inputs, lengths, matrices)
    direct = plan.direct
    (pieces, cotangent_pieces), plan.small_own = pick_rows(
        plan, (inputs, cotangent), norm_gains, conv_depthwise
    )
    plan.small_other = swap(plan.small_own)
    plan.other = [swap(w) for w in plan.own]

    def over(value):
        return swap(value) if direct else None

    def after(value, other):
        return lax.optimization_barrier((value, other))[0]

    def there(*values):
        return values if direct else ()

    first0 = call_first(plan, pieces)
    kvh0 = halo_exchange(plan, first0.kvs, W)
    mid0 = call_attend(plan, 0, first0, kvh0)
    gh0 = halo_exchange(plan, mid0.gsend, EDGE)
    turn = call_conv_first(plan, mid0, gh0)
    kvh1 = halo_exchange(plan, turn.kvs, W)
    got0 = SimpleNamespace(p1=over(first0.p1), p2=over(mid0.p2))
    mid1 = call_attend(plan, 1, turn, kvh1, there(got0.p1, got0.p2))
    gh1 = halo_exchange(plan, mid1.gsend, EDGE)
    got0.p3, got1 = over(turn.p3), SimpleNamespace(p1=over(turn.p1))
    end = call_conv_last(plan, mid1, gh1, cotangent_pieces, there(got0.p3, got1.p1))
    dzh1 = halo_exchange(plan, end.dzs, EDGE)
    launch(plan, lambda ctx: None, "between", {}, {}, limit=1)
    got1.c3, got1.p2 = over(after(end.c3, dzh1)), over(after(mid1.p2, dzh1))
    own1 = SimpleNamespace(
        p1=turn.p1, a1=turn.a1, p2=mid1.p2, c3=end.c3, a2=end.a2, k3=end.k3
    )
    own0 = SimpleNamespace(
        p1=first0.p1, a1=first0.a1, p2=mid0.p2, p3=turn.p3, a2=turn.a2
    )
    att1 = call_attend_back(plan, 1, turn, mid1, end, gh1, dzh1, ())
    back1 = halo_return(plan, att1.dkvh, W)
    own1.q2, own1.k2 = att1.q2, att1.k2
    if direct:
        two1 = call_bucket(plan, (0,), own1, got1)
    beg1 = call_first_back(plan, 1, turn.y, turn, att1, back1, there(got1.p2))
    own1.q1, own1.k1, own1.smalls = beg1.q1, beg1.k1, beg1.smalls
    got1.q1 = over(beg1.q1)
    last0 = call_last(plan, turn, beg1.ig, ())
    dzh0 = halo_exchange(plan, last0.dzs, EDGE)
    own0.q3, own0.k3 = last0.q3, last0.k3
    got0.q3 = over(last0.q3)
    if direct:
        one1 = call_bucket(plan, (2,), own1, got1)
    att0 = call_attend_back(plan, 0, first0, mid0, last0, gh0, dzh0, there(got0.q3))
    back0 = halo_return(plan, att0.dkvh, W)
    own0.q2, own0.k2 = att0.q2, att0.k2
    if direct:
        mid1b = call_bucket(plan, (1,), own1, got1)
    beg0 = call_first_back(plan, 0, first0.x, first0, att0, back0, ())
    own0.q1, own0.k1, own0.smalls = beg0.q1, beg0.k1, beg0.smalls
    got0.q1 = over(beg0.q1)
    keep, got = split_layers(plan, ((turn.y, beg0.ig), (end.y, beg1.ig)), ())
    if direct:
        two0 = call_bucket(plan, (0,), own0, got0)
    dealt = deal_rows(plan, keep, got)
    if direct:
        mid0b = call_bucket(plan, (1,), own0, got0)
        early1 = call_second(plan, [two1, mid1b])
        one0 = call_bucket(plan, (2,), own0, got0)
        one1 = call_second(plan, [one1])
    dealt = deal_far(plan, dealt)
    if direct:
        early0 = call_second(plan, [two0, mid0b])
        one1 = call_third(plan, [one1])
    framed = place_rows(plan, dealt)
    if direct:
        early1 = call_third(plan, [early1])
        one1 = call_fourth(plan, one1)
        early0 = call_third(plan, [early0])
        one0 = call_second(plan, [one0])
        early1 = call_fourth(plan, early1)
        one0 = call_third(plan, [one0])
        one1 = call_total(plan, one1)
        early0 = call_fourth(plan, early0)
        early1 = call_total(plan, early1)
        one1 = call_pair(plan, one1)
        early1 = call_pair(plan, early1)
        one0 = call_fourth(plan, one0)
        early0 = call_total(plan, early0)
        early0 = call_pair(plan, early0)
        one0 = call_total(plan, one0)
        crossed = call_cross(plan, (early0, early1))
        one0 = call_pair(plan, one0)
        two = call_unpack(plan, 0, (0, 0), (early0, early1), crossed)
        middle = call_unpack(plan, 1, (ROWS[0], ROWS[0]), (early0, early1), crossed)
        crossed = call_cross(plan, (one0, one1))
        one = call_unpack(plan, 2, (0, 0), (one0, one1), crossed)
        results = (
            one.up, one.dn, one.qkv, middle.out, middle.exp, one.taps, middle.prj,
            two.up, two.dn, one.gains,
        )
    else:
        own1.p3, own1.q3 = end.c3[:, : 2 * D + FH], end.c3[:, 2 * D + FH :]
        results = plain_gradients(plan, (own0, own1))
    activations, input_grads = framed.activations, framed.input_grads
    return (activations[None], input_grads[None]) + tuple(r[None] for r in results)


def solution(mesh):
    section, dp, seq = MESH_AXES
    whole = P(section, None, None)
    sliced = P(section, seq, None)
    across = P(section, None, seq)
    framed = P(section, dp, seq, None)
    return jax.shard_map(
        functools.partial(per_device, dict(mesh.shape)),
        mesh=mesh,
        in_specs=(P(dp, seq, None), P(dp, seq, None), P(dp, None)) + (whole,) * 10,
        out_specs=(framed, framed) + (sliced,) * 5 + (across,) + (sliced,) * 3 + (across,),
        check_vma=False,
    )
```

```python
import functools
from types import SimpleNamespace

import jax
import jax.numpy as jnp
from jax import lax
from jax.experimental import pallas as pl
from jax.experimental.pallas import tpu as pltpu
from jax.sharding import PartitionSpec as P

D = 512
H = 8
HD = 64
F = 2048
FH = F // 2
K = 9
W = 128
UTT = 4
EPSILON = 1e-05
MASKED = -1e30
EDGE = 16
Q2_AT = D + FH + 3 * D // 2
CHUNK = 2048
MIB = 1024 * 1024
COST = 10**10
LIMITS = (12, 8, 18, 16, 11, 10, 12, 6)
MESH_AXES = ("section", "dp", "seq")

BF = jnp.bfloat16
F32 = jnp.float32

UP1, DN1, QKV, OUT, EXP, PRJ, UP2, DN2 = range(8)


def dot(a, b):
    return jnp.dot(a, b, preferred_element_type=F32)


def dot_nt(a, b):
    return lax.dot_general(a, b, (((1,), (1,)), ((), ())), preferred_element_type=F32)


def dot_tn(a, b):
    return lax.dot_general(a, b, (((0,), (0,)), ((), ())), preferred_element_type=F32)


def sigmoid(v):
    return 0.5 * jnp.tanh(0.5 * v) + 0.5


def norm_stats(v):
    centred = v - jnp.mean(v, axis=-1, keepdims=True)
    inverse = lax.rsqrt(jnp.mean(centred * centred, axis=-1, keepdims=True) + EPSILON)
    return centred * inverse, inverse


def norm_back(upstream, normed, inverse, gain):
    gain_grad = jnp.sum(upstream * normed, axis=0, keepdims=True)
    scaled = upstream * gain
    value_grad = inverse * (
        scaled
        - jnp.mean(scaled, axis=-1, keepdims=True)
        - normed * jnp.mean(scaled * normed, axis=-1, keepdims=True)
    )
    return value_grad, gain_grad


class Place:
    def __init__(self, plan, lengths):
        core, replica, chip = (lax.axis_index(name) for name in MESH_AXES)
        self.core, self.chip = core, chip
        self.row = lax.rem(chip, plan.rows)
        self.first = (lax.div(chip, plan.rows) * 2 + core) * plan.frames
        self.length = plan.length
        self.fast = lax.rem(replica, 2)
        self.slow = lax.rem(lax.div(replica, 2), 2)
        self.side1 = jnp.where(core == 0, self.fast, self.slow)
        self.side2 = jnp.where(core == 0, self.slow, self.fast)
        self.ends = []
        total = 0
        for u in range(UTT):
            total = total + lengths[self.row, u]
            self.ends.append(total)


class Ctx:
    def __init__(self, plan, place, table, held, waits):
        self.__dict__.update(place.__dict__)
        self.__dict__.update(table)
        self.plan = plan
        self.held = held
        self.waits = waits

    def weight(self, matrix, layer, part=None):
        queue = self.waits[(matrix, layer)]
        for index in range(len(queue)):
            if queue[index] is not None and (part is None or part == index):
                queue[index].wait()
                queue[index] = None
        return self.held[(matrix, layer)]

    def small(self, row, layer):
        mine = self.core == layer
        return jnp.where(mine, self.small_own[row : row + 1, :], self.small_other[row : row + 1, :])

    def taps(self, tap, layer):
        return self.small(6 + tap, layer)

    def segment(self, pos):
        start, stop = jnp.zeros(pos.shape, jnp.int32), jnp.full(pos.shape, self.length, jnp.int32)
        for end in self.ends:
            start = jnp.maximum(start, jnp.where(pos >= end, end, 0))
            stop = jnp.minimum(stop, jnp.where(pos >= end, self.length, end))
        return start, stop


def parts_of(matrix, shape):
    if matrix in (UP1, UP2):
        return [(slice(None), pl.ds(c, CHUNK)) for c in range(0, F, CHUNK)]
    if matrix in (DN1, DN2):
        return [(pl.ds(c, CHUNK), slice(None)) for c in range(0, F, CHUNK)]
    return [(slice(None), slice(None))]


def launch(plan, body, name, ins, outs, weights=(), scratch=None, far=None, results=None, settle=(),
           limit=6):
    scratch, far, results = scratch or {}, far or {}, results or {}
    near = dict(ins)
    near.update({"settle%d" % i: v for i, v in enumerate(settle)})
    if weights:
        near.update(small_own=plan.small_own, small_other=plan.small_other)
    if plan.token is not None:
        near.update(token_in=plan.token)
    pinned = [pltpu.with_memory_space_constraint(v, pltpu.VMEM) for v in near.values()]
    operands = [pltpu.with_memory_space_constraint(plan.lengths, pltpu.HBM)] + pinned
    operands += [pltpu.with_memory_space_constraint(v, pltpu.HBM) for v in far.values()]
    in_specs = [pl.BlockSpec(memory_space=pltpu.SMEM)]
    in_specs += [pl.BlockSpec(memory_space=pltpu.VMEM)] * len(near)
    in_specs += [pl.BlockSpec(memory_space=pl.ANY)] * len(far)
    copies = []
    for matrix, layer in weights:
        operands += [
            pltpu.with_memory_space_constraint(plan.own[matrix], pltpu.HBM),
            plan.other[matrix],
        ]
        in_specs += [pl.BlockSpec(memory_space=pl.ANY)] * 2
        copies.append(parts_of(matrix, plan.own[matrix].shape))
    held_shapes = [pltpu.VMEM(plan.own[m].shape, BF) for m, _ in weights]
    out_shape = [pltpu.VMEM(*s) for s in outs.values()]
    out_shape += [jax.ShapeDtypeStruct(*s) for s in results.values()]
    out_shape += [pltpu.VMEM((8, 128), jnp.int32)]
    out_specs = [pl.BlockSpec(memory_space=pltpu.VMEM)] * len(out_shape)
    sems = max(sum(len(c) for c in copies), 1) + 24

    def kernel(*refs):
        refs = list(refs)
        place = Place(plan, refs.pop(0))
        table = {}
        for n in list(near) + list(far):
            table[n] = refs.pop(0)
        sources = [(refs.pop(0), refs.pop(0)) for _ in weights]
        for n in list(outs) + list(results):
            table[n] = refs.pop(0)
        refs.pop(0)
        for n in scratch:
            table[n] = refs.pop(0)
        held_refs = [refs.pop(0) for _ in weights]
        sem = refs.pop(0)
        core = place.core
        held, waits = {}, {}
        for pair in weights:
            waits[pair] = []
        count = 0
        for part in range(max([len(c) for c in copies], default=0)):
            for pair, (own, other), into, slices in zip(weights, sources, held_refs, copies):
                held[pair] = into
                if part >= len(slices):
                    continue
                at = slices[part]

                @pl.when(core == pair[1])
                def _(own=own, into=into, at=at, count=count):
                    pltpu.make_async_copy(own.at[at], into.at[at], sem.at[count]).start()

                @pl.when(core != pair[1])
                def _(other=other, into=into, at=at, count=count):
                    pltpu.make_async_copy(other.at[at], into.at[at], sem.at[count]).start()

                waits[pair].append(pltpu.make_async_copy(own.at[at], into.at[at], sem.at[count]))
                count += 1
        ctx = Ctx(plan, place, table, held, waits)
        ctx.sems = [sem.at[sems - 24 + i] for i in range(24)]
        body(ctx)
        for pair in weights:
            ctx.weight(*pair)

    made = pl.pallas_call(
        kernel,
        out_shape=out_shape,
        in_specs=in_specs,
        out_specs=out_specs,
        scratch_shapes=[pltpu.VMEM(*s) for s in scratch.values()]
        + held_shapes
        + [pltpu.SemaphoreType.DMA((sems,))],
        compiler_params=pltpu.CompilerParams(vmem_limit_bytes=limit * MIB),
        cost_estimate=pl.CostEstimate(flops=COST, transcendentals=0, bytes_accessed=1),
        name=name,
    )(*operands)
    plan.token = made[-1]
    return SimpleNamespace(**dict(zip(list(outs) + list(results), made)))


def half_copies(ctx, value_ref, keep_ref, send_ref, keep_at, send_at, total, blocks):
    width = total // (2 * blocks)
    for j in range(blocks):
        mine = pl.multiple_of(j * 2 * width + ctx.core * width, width)
        theirs = pl.multiple_of(j * 2 * width + (1 - ctx.core) * width, width)
        keep_ref[:, keep_at + j * width : keep_at + (j + 1) * width] = value_ref[:, pl.ds(mine, width)]
        send_ref[:, send_at + j * width : send_at + (j + 1) * width] = value_ref[
            :, pl.ds(theirs, width)
        ]


def edge_rows(ctx, value_ref, send_ref, rows):
    frames = value_ref.shape[0]
    if ctx.plan.halos == 1:
        at = pl.multiple_of((1 - ctx.core) * (frames - rows), rows)
        send_ref[...] = value_ref[pl.ds(at, rows), :]
    else:
        send_ref[0:rows, :] = value_ref[frames - rows : frames, :]
        send_ref[rows : 2 * rows, :] = value_ref[0:rows, :]


def halo_starts(ctx, rows, frames):
    before = ctx.first - rows
    after = ctx.first + frames
    if ctx.plan.halos == 1:
        return [jnp.where(ctx.core == 0, after, before)]
    return [before, after]


def feed_forward(ctx, hidden, up, down, layer, keep_ref, send_ref, send_at, slope_ref):
    frames = hidden.shape[0]
    total = jnp.zeros((frames, D), F32)
    for part, c in enumerate(range(0, F, CHUNK)):
        at = slice(c, c + CHUNK)
        inner = dot(hidden, ctx.weight(up, layer, part)[:, at])
        logistic = sigmoid(inner)
        active = (inner * logistic).astype(BF)
        slope_ref[:, at] = (logistic * (1.0 + inner * (1.0 - logistic))).astype(BF)
        ctx.act[:, at] = active
        total = total + dot(active, ctx.weight(down, layer, part)[at, :])
    half_copies(ctx, ctx.act, keep_ref, send_ref, 0, send_at, F, ctx.plan.blocks)
    return total


def fwd_first(ctx, x, layer):
    normed, _ = norm_stats(x)
    hidden = (normed * ctx.small(0, layer)).astype(BF)
    ctx.p1[:, 0:D] = hidden
    ffn = feed_forward(ctx, hidden, UP1, DN1, layer, ctx.a1, ctx.p1, 2 * D, ctx.s1)
    r1 = x + 0.5 * ffn
    ctx.r1[...] = r1
    normed, _ = norm_stats(r1)
    hidden = (normed * ctx.small(1, layer)).astype(BF)
    ctx.p1[:, D : 2 * D] = hidden
    ctx.qkv[...] = dot(hidden, ctx.weight(QKV, layer)[...]).astype(BF)
    edge_rows(ctx, ctx.qkv.at[:, D : 3 * D], ctx.kvs, W)


def first_outs(plan):
    t = plan.frames
    return dict(
        p1=((t, 2 * D + FH), BF),
        a1=((t, FH), BF),
        s1=((t, F), BF),
        r1=((t, D), F32),
        qkv=((t, 3 * D), BF),
        kvs=((plan.halos * W, 2 * D), BF),
    )


def call_first(plan, pieces):
    def body(ctx):
        join_frames(ctx, ctx.x)
        fwd_first(ctx, ctx.x[...].astype(F32), 0)

    t = plan.frames
    return launch(
        plan, body, "first", pieces, dict(x=((t, D), BF), **first_outs(plan)),
        [(UP1, 0), (DN1, 0), (QKV, 0)], dict(act=((t, F), BF)), limit=LIMITS[0],
    )


def allowed_bias(ctx, key_start, keys):
    frames = ctx.plan.frames
    query = ctx.first + lax.broadcasted_iota(jnp.int32, (frames, 1), 0)
    start, stop = ctx.segment(query)
    low, high = jnp.maximum(start, query - W), jnp.minimum(stop - 1, query + W)
    key = key_start + lax.broadcasted_iota(jnp.int32, (frames, keys), 1)
    return jnp.where((key >= low) & (key <= high), 0.0, MASKED).astype(F32)


def stacked_heads(value, lane):
    zero = jnp.zeros_like(value)
    return jnp.concatenate([jnp.where(lane < HD, value, zero), jnp.where(lane < HD, zero, value)], axis=0)


def fwd_attend(ctx, layer):
    t = ctx.plan.frames
    halos = ctx.plan.halos
    qkv, probs, p2, bias, kx = ctx.qkv, ctx.probs, ctx.p2, ctx.bias, ctx.kx
    kx[0:t, :] = qkv[:, D : 3 * D]
    kx[t:, :] = ctx.kvh[...]
    starts = halo_starts(ctx, W, t)
    bias[:, 0:t] = allowed_bias(ctx, ctx.first, t)
    for h in range(halos):
        bias[:, t + h * W : t + (h + 1) * W] = allowed_bias(ctx, starts[h], W)
    lane = lax.broadcasted_iota(jnp.int32, (t, 2 * HD), 1)
    for p in range(H // 2):
        at = 2 * HD * p
        q = stacked_heads(qkv[:, at : at + 2 * HD] * jnp.asarray(HD ** (-0.5), BF), lane)
        scores = dot_nt(q, kx[:, at : at + 2 * HD]).reshape(2, t, -1) + bias[...][None]
        exponent = jnp.exp(scores - jnp.max(scores, axis=-1, keepdims=True))
        scale = 1.0 / jnp.sum(exponent, axis=-1, keepdims=True)
        weights = (exponent * scale).astype(BF).reshape(2 * t, -1)
        probs[p] = weights
        out = dot(weights, kx[:, D + at : D + at + 2 * HD])
        p2[:, at : at + 2 * HD] = jnp.where(lane < HD, out[0:t], out[t:]).astype(BF)
    r2 = ctx.r1[...] + dot(p2[:, 0:D], ctx.weight(OUT, layer)[...])
    ctx.r2[...] = r2
    normed, _ = norm_stats(r2)
    hidden = (normed * ctx.small(2, layer)).astype(BF)
    p2[:, D : 2 * D] = hidden
    expand = ctx.weight(EXP, layer)
    linear = dot(hidden, expand[:, 0:D])
    logistic = sigmoid(dot(hidden, expand[:, D : 2 * D]))
    gated = linear * logistic
    ctx.g[...] = gated.astype(BF)
    ctx.gs[...] = logistic.astype(BF)
    ctx.gt[...] = (gated * (1.0 - logistic)).astype(BF)
    edge_rows(ctx, ctx.g, ctx.gsend, EDGE)


def call_attend(plan, layer, first, kvh, settle=()):
    t = plan.frames
    keys = t + plan.halos * W
    return launch(
        plan,
        lambda ctx: fwd_attend(ctx, layer),
        "attend",
        dict(qkv=first.qkv, kvh=kvh, r1=first.r1),
        dict(
            probs=((H // 2, 2 * t, keys), BF),
            kx=((keys, 2 * D), BF),
            p2=((t, 2 * D), BF),
            r2=((t, D), F32),
            g=((t, D), BF),
            gs=((t, D), BF),
            gt=((t, D), BF),
            gsend=((plan.halos * EDGE, D), BF),
        ),
        [(OUT, layer), (EXP, layer)],
        dict(bias=((t, keys), F32)),
        settle=settle, limit=LIMITS[1],
    )


def fill_extended(ctx, ext, own, halo):
    t = ctx.plan.frames
    before = halo[EDGE - 8 : EDGE, :]
    after = halo[0:8, :] if ctx.plan.halos == 1 else halo[EDGE : EDGE + 8, :]
    ext[0:8, :] = before.astype(F32)
    ext[8 : 8 + t, :] = own[...].astype(F32)
    ext[8 + t : 16 + t, :] = after.astype(F32)


def tap_masks(ctx, row, rows):
    pos = ctx.first + row + lax.broadcasted_iota(jnp.int32, (rows, 128), 0)
    start, stop = ctx.segment(pos)
    before, after = pos - start, stop - pos
    return [(before >= K // 2 - k) if k <= K // 2 else (after > k - K // 2) for k in range(K)]


def mix_time(ctx, ext, z_ref, layer):
    t = ctx.plan.frames
    taps = [ctx.taps(k, layer) for k in range(K)]
    block = 64
    for row in range(0, t, block):
        masks = tap_masks(ctx, row, block)
        for c in range(0, D, 128):
            total = jnp.zeros((block, 128), F32)
            for k in range(K):
                at = 8 + row + k - K // 2
                window = ext[at : at + block, c : c + 128] * taps[k][:, c : c + 128]
                total = total + jnp.where(masks[k], window, 0.0)
            z_ref[row : row + block, c : c + 128] = total


def valid_rows(ctx):
    pos = ctx.first + lax.broadcasted_iota(jnp.int32, (ctx.plan.frames, 1), 0)
    return (pos < ctx.ends[UTT - 1]).astype(F32)


def fwd_conv(ctx, layer):
    fill_extended(ctx, ctx.ext, ctx.g, ctx.gh)
    mix_time(ctx, ctx.ext, ctx.z, layer)
    normed, _ = norm_stats(ctx.z[...])
    mixed = normed * ctx.small(3, layer)
    active = (mixed * sigmoid(mixed)).astype(BF)
    ctx.p3[:, 0:D] = active
    r3 = ctx.r2[...] + dot(active, ctx.weight(PRJ, layer)[...])
    ctx.r3[...] = r3
    normed, _ = norm_stats(r3)
    hidden = (normed * ctx.small(4, layer)).astype(BF)
    ctx.p3[:, D : 2 * D] = hidden
    ffn = feed_forward(ctx, hidden, UP2, DN2, layer, ctx.a2, ctx.p3, 2 * D, ctx.s2)
    r4 = r3 + 0.5 * ffn
    ctx.r4[...] = r4
    normed, _ = norm_stats(r4)
    result = (normed * ctx.small(5, layer) * valid_rows(ctx)).astype(BF)
    ctx.y[...] = result
    return result


def conv_outs(plan):
    t = plan.frames
    return dict(
        z=((t, D), F32),
        p3=((t, 2 * D + FH), BF),
        a2=((t, FH), BF),
        s2=((t, F), BF),
        r3=((t, D), F32),
        r4=((t, D), F32),
        y=((t, D), BF),
    )


def conv_scratch(plan):
    t = plan.frames
    return dict(ext=((t + 16, D), F32), act=((t, F), BF))


def call_conv_first(plan, mid, gh):
    def body(ctx):
        fwd_first(ctx, fwd_conv(ctx, 0).astype(F32), 1)

    return launch(
        plan, body, "conv_first", dict(g=mid.g, gh=gh, r2=mid.r2),
        dict(conv_outs(plan), **first_outs(plan)),
        [(PRJ, 0), (UP2, 0), (DN2, 0), (UP1, 1), (DN1, 1), (QKV, 1)],
        conv_scratch(plan), limit=LIMITS[2],
    )


def call_conv_last(plan, mid, gh, pieces, settle):
    outs = dict(conv_outs(plan), **last_outs(plan))
    del outs["p3"], outs["q3"]
    outs["c3"] = ((plan.frames, 2 * D + FH + D + FH + D // 2), BF)

    def body(ctx):
        ctx.p3, ctx.q3 = ctx.c3.at[:, 0 : 2 * D + FH], ctx.c3.at[:, 2 * D + FH :]
        fwd_conv(ctx, 1)
        join_frames(ctx, ctx.dy)
        bwd_last(ctx, ctx.dy[...], 1)

    return launch(
        plan, body, "conv_last", dict(g=mid.g, gh=gh, r2=mid.r2, **pieces), outs,
        [(PRJ, 1), (UP2, 1), (DN2, 1)],
        dict(conv_scratch(plan), dy=((plan.frames, D), BF)), settle=settle, limit=LIMITS[3],
    )


def feed_forward_back(ctx, step, up, down, layer, slope_ref, keep_ref, send_ref, send_at):
    total = jnp.zeros((step.shape[0], D), F32)
    for part, c in enumerate(range(0, F, CHUNK)):
        at = slice(c, c + CHUNK)
        grad = dot_nt(step, ctx.weight(down, layer, part)[at, :]) * slope_ref[:, at].astype(F32)
        grad = grad.astype(BF)
        ctx.act[:, at] = grad
        total = total + dot_nt(grad, ctx.weight(up, layer, part)[:, at])
    half_copies(ctx, ctx.act, keep_ref, send_ref, 0, send_at, F, 1)
    return total


def bwd_last(ctx, dy, layer):
    upstream = dy.astype(F32) * valid_rows(ctx)
    smalls = ctx.smalls
    smalls[...] = jnp.zeros(smalls.shape, F32)
    normed, inverse = norm_stats(ctx.r4[...])
    stream, gg = norm_back(upstream, normed, inverse, ctx.small(5, layer))
    smalls[5:6, :] = gg
    step = (0.5 * stream).astype(BF)
    ctx.q3[:, 0:D] = step
    inner = feed_forward_back(ctx, step, UP2, DN2, layer, ctx.s2, ctx.k3, ctx.q3, D)
    normed, inverse = norm_stats(ctx.r3[...])
    branch, gg = norm_back(inner, normed, inverse, ctx.small(4, layer))
    smalls[4:5, :] = gg
    stream = stream + branch
    ctx.dr3[...] = stream
    step = stream.astype(BF)
    ctx.act[:, 0:D] = step
    half_copies(ctx, ctx.act.at[:, 0:D], ctx.k3, ctx.q3, FH, D + FH, D, 1)
    normed, inverse = norm_stats(ctx.z[...])
    gain = ctx.small(3, layer)
    mixed = normed * gain
    logistic = sigmoid(mixed)
    slope = logistic * (1.0 + mixed * (1.0 - logistic))
    mix, gg = norm_back(dot_nt(step, ctx.weight(PRJ, layer)[...]) * slope, normed, inverse, gain)
    smalls[3:4, :] = gg
    ctx.dz[...] = mix.astype(BF)
    edge_rows(ctx, ctx.dz, ctx.dzs, EDGE)


def last_outs(plan):
    t = plan.frames
    return dict(
        smalls=((16, D), F32),
        q3=((t, D + FH + D // 2), BF),
        k3=((t, FH + D // 2), BF),
        dr3=((t, D), F32),
        dz=((t, D), BF),
        dzs=((plan.halos * EDGE, D), BF),
    )


def call_last(plan, late, dy, settle):
    t = plan.frames
    return launch(
        plan, lambda ctx: bwd_last(ctx, ctx.dy[...], 0), "last",
        dict(dy=dy, r4=late.r4, r3=late.r3, z=late.z, s2=late.s2),
        last_outs(plan),
        [(DN2, 0), (UP2, 0), (PRJ, 0)],
        dict(act=((t, F), BF)),
        settle=settle, limit=LIMITS[4],
    )


def mix_time_back(ctx, layer):
    t = ctx.plan.frames
    grads, gated = ctx.ext, ctx.ext2
    weights = [ctx.taps(k, layer) for k in range(K)]
    block = 64
    taps = [[jnp.zeros((8, 128), F32) for _ in range(D // 128)] for _ in range(K)]
    for row in range(0, t, block):
        masks = tap_masks(ctx, row, block)
        for ci, c in enumerate(range(0, D, 128)):
            own = grads[8 + row : 8 + row + block, c : c + 128]
            total = jnp.zeros((block, 128), F32)
            for k in range(K):
                at = 8 + row + k - K // 2
                product = jnp.where(masks[k], own * gated[at : at + block, c : c + 128], 0.0)
                taps[k][ci] = taps[k][ci] + jnp.sum(product.reshape(block // 8, 8, 128), axis=0)
                window = grads[at : at + block, c : c + 128] * weights[K - 1 - k][:, c : c + 128]
                total = total + jnp.where(masks[k], window, 0.0)
            ctx.dg[row : row + block, c : c + 128] = total
    for k in range(K):
        for ci, c in enumerate(range(0, D, 128)):
            ctx.smalls[6 + k : 7 + k, c : c + 128] = jnp.sum(taps[k][ci], axis=0, keepdims=True)


def bwd_attend(ctx, layer):
    t = ctx.plan.frames
    fill_extended(ctx, ctx.ext, ctx.dz, ctx.dzh)
    fill_extended(ctx, ctx.ext2, ctx.g, ctx.gh)
    ctx.smalls[...] = ctx.smalls_in[...]
    mix_time_back(ctx, layer)
    gated = ctx.dg[...]
    act = ctx.act
    act[:, 0:D] = (gated * ctx.gs[...].astype(F32)).astype(BF)
    act[:, D : 2 * D] = (gated * ctx.gt[...].astype(F32)).astype(BF)
    half_copies(ctx, act, ctx.k2, ctx.q2, 0, 0, 2 * D, 1)
    normed, inverse = norm_stats(ctx.r2[...])
    branch, gg = norm_back(
        dot_nt(act[...], ctx.weight(EXP, layer)[...]), normed, inverse, ctx.small(2, layer)
    )
    ctx.smalls[2:3, :] = gg
    stream = ctx.dr3[...] + branch
    ctx.dr2[...] = stream
    step = stream.astype(BF)
    act[:, 0:D] = step
    half_copies(ctx, act.at[:, 0:D], ctx.k2, ctx.q2, D, D, D, 1)
    grad_o = ctx.do
    grad_o[...] = dot_nt(step, ctx.weight(OUT, layer)[...]).astype(BF)
    qkv, probs, p2, kx = ctx.qkv, ctx.probs, ctx.p2, ctx.kx
    lane = lax.broadcasted_iota(jnp.int32, (t, 2 * HD), 1)
    scale = HD ** (-0.5)
    for p in range(H // 2):
        at = 2 * HD * p
        q = stacked_heads(qkv[:, at : at + 2 * HD] * jnp.asarray(scale, BF), lane)
        do = grad_o[:, at : at + 2 * HD]
        spread = stacked_heads(do.astype(F32) * p2[:, at : at + 2 * HD].astype(F32), lane)
        do = stacked_heads(do, lane)
        delta = jnp.sum(spread, axis=-1, keepdims=True)
        weights = probs[p]
        grad = dot_nt(do, kx[:, D + at : D + at + 2 * HD]) - delta
        grad = (weights.astype(F32) * grad).astype(BF)
        dq = dot(grad, kx[:, at : at + 2 * HD]) * scale
        ctx.dq[:, at : at + 2 * HD] = jnp.where(lane < HD, dq[0:t], dq[t:]).astype(BF)
        dk, dv = dot_tn(grad, q), dot_tn(weights, do)
        ctx.dkv[:, at : at + 2 * HD] = dk[0:t]
        ctx.dkv[:, D + at : D + at + 2 * HD] = dv[0:t]
        ctx.dkvh[:, at : at + 2 * HD] = dk[t:].astype(BF)
        ctx.dkvh[:, D + at : D + at + 2 * HD] = dv[t:].astype(BF)


def call_attend_back(plan, layer, first, mid, last, gh, dzh, settle):
    t = plan.frames
    return launch(
        plan,
        lambda ctx: bwd_attend(ctx, layer),
        "attend_back",
        dict(
            dz=last.dz, dzh=dzh, dr3=last.dr3, smalls_in=last.smalls,
            g=mid.g, gh=gh, gs=mid.gs, gt=mid.gt, r2=mid.r2,
            probs=mid.probs, p2=mid.p2, qkv=first.qkv, kx=mid.kx,
        ),
        dict(
            smalls=((16, D), F32),
            q2=((t, D + D // 2), BF),
            k2=((t, D + D // 2), BF),
            dr2=((t, D), F32),
            dq=((t, D), BF),
            dkv=((t, 2 * D), F32),
            dkvh=((plan.halos * W, 2 * D), BF),
        ),
        [(EXP, layer), (OUT, layer)],
        dict(
            ext=((t + 16, D), F32), ext2=((t + 16, D), F32), dg=((t, D), F32),
            act=((t, 2 * D), BF), do=((t, D), BF),
        ),
        settle=settle, limit=LIMITS[5],
    )


def bwd_first(ctx, layer):
    t = ctx.plan.frames
    ctx.smalls[...] = ctx.smalls_in[...]
    grads, acc, back = ctx.act, ctx.acc, ctx.back
    grads[:, 0:D] = ctx.dq[...]
    acc[...] = ctx.dkv[...]
    if ctx.plan.halos == 1:
        at = pl.multiple_of((1 - ctx.core) * (t - W), W)
        acc[pl.ds(at, W), :] += back[...].astype(F32)
    else:
        acc[t - W : t, :] += back[0:W, :].astype(F32)
        acc[0:W, :] += back[W : 2 * W, :].astype(F32)
    grads[:, D : 3 * D] = acc[...].astype(BF)
    half_copies(ctx, grads.at[:, 0 : 3 * D], ctx.k1, ctx.q1.at[0:t], FH, D + FH, 3 * D, 1)
    normed, inverse = norm_stats(ctx.r1[...])
    branch, gg = norm_back(
        dot_nt(grads[:, 0 : 3 * D], ctx.weight(QKV, layer)[...]), normed, inverse, ctx.small(1, layer)
    )
    ctx.smalls[1:2, :] = gg
    stream = ctx.dr2[...] + branch
    step = (0.5 * stream).astype(BF)
    ctx.q1[0:t, 0:D] = step
    inner = feed_forward_back(ctx, step, UP1, DN1, layer, ctx.s1, ctx.k1, ctx.q1.at[0:t], D)
    normed, inverse = norm_stats(ctx.x[...].astype(F32))
    branch, gg = norm_back(inner, normed, inverse, ctx.small(0, layer))
    ctx.smalls[0:1, :] = gg
    ctx.ig[...] = (stream + branch).astype(BF)
    ctx.q1[t : t + EDGE, 0:D] = ctx.smalls[...].astype(BF)
    ctx.q1[0:t, Q2_AT : Q2_AT + D + D // 2] = ctx.q2[...]


def call_first_back(plan, layer, x, first, att, back, settle):
    t = plan.frames
    return launch(
        plan,
        lambda ctx: bwd_first(ctx, layer),
        "first_back",
        dict(
            x=x, r1=first.r1, s1=first.s1, dr2=att.dr2, dq=att.dq, dkv=att.dkv, back=back,
            smalls_in=att.smalls, q2=att.q2,
        ),
        dict(
            smalls=((16, D), F32),
            q1=((t + EDGE, Q2_AT + D + D // 2), BF),
            k1=((t, FH + 3 * D // 2), BF),
            ig=((t, D), BF),
        ),
        [(QKV, layer), (DN1, layer), (UP1, layer)],
        dict(act=((t, F), BF), acc=((t, 2 * D), F32)),
        settle=settle, limit=LIMITS[6],
    )


ROWS = (128, 64, 192)


def both_tn(left, left_got, right, right_got):
    return dot_tn(left, right) + dot_tn(left_got, right_got)


def put_part(ref, value, q, at, col):
    width = value.shape[1]
    for b in range(2):
        ref[b, q, at : at + 64, col : col + width] = value[64 * b : 64 * (b + 1), :].astype(BF)


def put_ffn(ref, a, row, step, step_got, hid, hid_got, act, fwd_got, inner, bwd_got):
    for q in range(4):
        at = pl.multiple_of(q * 256 + a * 128, 128)
        got = pl.multiple_of(2 * D + q * 256 + a * 128, 128)
        value = both_tn(act[:, pl.ds(at, 128)], fwd_got[:, pl.ds(got, 128)], step, step_got)
        put_part(ref, value, q, row, 0)
    at = pl.multiple_of(a * D, D)
    got = pl.multiple_of(D + a * D, D)
    value = both_tn(hid, hid_got, inner[:, pl.ds(at, D)], bwd_got[:, pl.ds(got, D)])
    for q in range(4):
        put_part(ref, value[q * 128 : (q + 1) * 128, :], q, row + 64, 0)


def put_matrix(ref, a, left, left_got, left_at, right, own_at, right_got, got_at, width, at, col):
    own = pl.multiple_of(own_at + a * width, 128)
    got = pl.multiple_of(got_at + a * width, 128)
    value = both_tn(
        left[:, left_at : left_at + D], left_got[:, left_at : left_at + D],
        right[:, pl.ds(own, width)], right_got[:, pl.ds(got, width)],
    )
    for q in range(4):
        put_part(ref, value[q * 128 : (q + 1) * 128, :], q, at, col)


def call_bucket(plan, kinds, f, g):
    joint = hasattr(f, "c3")

    def body(ctx):
        side = ctx.side1
        t = plan.frames
        if joint and kinds != (2,):
            cut = 2 * D + FH
            ctx.p3, ctx.q3 = ctx.c3.at[:, 0:cut], ctx.c3.at[:, cut:]
            ctx.p3_got, ctx.q3_got = ctx.c3_got.at[:, 0:cut], ctx.c3_got.at[:, cut:]
        if kinds != (0,):
            q1_got = ctx.q1_got.at[0:t]
            q2_got = ctx.q1_got.at[0:t, Q2_AT : Q2_AT + D + D // 2]
        if 2 in kinds:
            small = ctx.smalls[...] + ctx.q1_got[t : t + EDGE, 0:D].astype(F32)
            small = jnp.where(ctx.core == 0, small[0:8], small[8:16])
            small = jnp.concatenate([small, jnp.zeros((56, D), F32)], axis=0).astype(BF)
        for ref, a in ((ctx.send, 1 - side), (ctx.keep, side)):
            at = 0
            if 0 in kinds:
                put_ffn(
                    ref, a, at, ctx.q3[:, 0:D], ctx.q3_got[:, 0:D], ctx.p3[:, D : 2 * D],
                    ctx.p3_got[:, D : 2 * D], ctx.a2, ctx.p3_got, ctx.k3, ctx.q3_got,
                )
                at += ROWS[0]
            if 1 in kinds:
                put_matrix(ref, a, ctx.p2, ctx.p2_got, D, ctx.k2, 0, q2_got, 0, 256, at, 0)
                put_matrix(ref, a, ctx.p2, ctx.p2_got, 0, ctx.k2, D, q2_got, D, 128, at, 256)
                put_matrix(ref, a, ctx.p3, ctx.p3_got, 0, ctx.k3, FH, ctx.q3_got, D + FH, 128, at, 384)
                at += ROWS[1]
            if 2 in kinds:
                put_ffn(
                    ref, a, at, ctx.q1[0:t, 0:D], ctx.q1_got[0:t, 0:D], ctx.p1[:, 0:D],
                    ctx.p1_got[:, 0:D], ctx.a1, ctx.p1_got, ctx.k1, q1_got,
                )
                put_matrix(
                    ref, a, ctx.p1, ctx.p1_got, D, ctx.k1, FH, q1_got, D + FH, 384, at + 128, 0
                )
                for q in range(4):
                    for b in range(2):
                        ref[b, q, at + 128 : at + 192, 384:512] = small[:, q * 128 : (q + 1) * 128]

    ins = {}
    names = ()
    if 2 in kinds:
        names += ("p1", "q1")
        ins.update(a1=f.a1, k1=f.k1, smalls=f.smalls)
    if kinds != (2,):
        names += ("c3",) if joint else ("p3", "q3")
        ins.update(k3=f.k3)
    if 0 in kinds:
        ins.update(a2=f.a2)
    if 1 in kinds:
        names += ("p2",)
        ins.update(k2=f.k2, q1_got=g.q1)
    for name in names:
        ins[name] = getattr(f, name)
        ins[name + "_got"] = getattr(g, name)
    shape = (2, 4, sum(ROWS[k] for k in kinds), D)
    part = launch(plan, body, "bucket", ins, dict(send=(shape, BF), keep=(shape, BF)), limit=LIMITS[7])
    part.got = exchange(plan, part.send, 0)
    return part


def exchange(plan, value, stage):
    pairs = []
    for core in range(2):
        bit = 1 if (core == 0) == (stage == 0) else 2
        pairs += [(core * 4 + i, core * 4 + (i ^ bit)) for i in range(4)]
    return lax.ppermute(value, MESH_AXES[:2], pairs)


def call_second(plan, parts):
    count = len(parts)
    rows = [p.keep.shape[2] for p in parts]

    def body(ctx):
        side = ctx.side2
        for ref, at in ((ctx.send, 1 - side), (ctx.mine, side)):
            row = 0
            for i in range(count):
                keep, got = getattr(ctx, "m%d" % i), getattr(ctx, "g%d" % i)
                value = keep[at].astype(F32) + got[at].astype(F32)
                ref[:, row : row + rows[i], :] = value.astype(BF)
                row += rows[i]

    ins = {"m%d" % i: p.keep for i, p in enumerate(parts)}
    ins.update({"g%d" % i: p.got for i, p in enumerate(parts)})
    shape = (4, sum(rows), D)
    half = launch(plan, body, "second", ins, dict(send=(shape, BF), mine=(shape, BF)), limit=6)
    half.got = exchange(plan, half.send, 1)
    return half


def call_third(plan, halves):
    rows = [h.mine.shape[1] for h in halves]

    def body(ctx):
        side = lax.rem(ctx.chip, 2)
        for ref, near in ((ctx.send, 1 - side), (ctx.mine, side)):
            at = 0
            for i, count in enumerate(rows):
                mine, got = getattr(ctx, "m%d" % i), getattr(ctx, "g%d" % i)
                for far in range(2):
                    q = 2 * far + near
                    value = mine[q].astype(F32) + got[q].astype(F32)
                    ref[far, at : at + count, :] = value.astype(BF)
                at += count

    ins = {"m%d" % i: h.mine for i, h in enumerate(halves)}
    ins.update({"g%d" % i: h.got for i, h in enumerate(halves)})
    shape = (2, sum(rows), D)
    made = launch(plan, body, "third", ins, dict(send=(shape, BF), mine=(shape, BF)), limit=4)
    made.got = exchange_seq(made.send, 1)
    return made


def call_fourth(plan, half):
    def body(ctx):
        side = lax.div(ctx.chip, 2)
        for ref, at in ((ctx.send, 1 - side), (ctx.mine, side)):
            ref[...] = (ctx.keep[at].astype(F32) + ctx.got[at].astype(F32)).astype(BF)

    shape = half.mine.shape[1:]
    made = launch(
        plan, body, "fourth", dict(keep=half.mine, got=half.got),
        dict(send=(shape, BF), mine=(shape, BF)), limit=4,
    )
    made.got = exchange_seq(made.send, 2)
    return made


def exchange_seq(value, bit):
    return lax.ppermute(value, MESH_AXES[2], [(i, i ^ bit) for i in range(4)])


def call_total(plan, half):
    def body(ctx):
        ctx.own[...] = (ctx.mine[...].astype(F32) + ctx.got[...].astype(F32)).astype(BF)

    total = launch(
        plan, body, "total", dict(mine=half.mine, got=half.got), dict(own=(half.mine.shape, BF)), limit=4
    )
    total.got = exchange(plan, total.own, 1)
    return total


def call_pair(plan, total):
    def body(ctx):
        ctx.pair[ctx.side2] = ctx.own[...]
        ctx.pair[1 - ctx.side2] = ctx.got[...]

    shape = (2,) + total.own.shape
    pair = launch(
        plan, body, "pair", dict(own=total.own, got=total.got), dict(pair=(shape, BF)), limit=4
    ).pair
    return pair, exchange(plan, pair, 0)


def call_cross(plan, layers):
    def body(ctx):
        for layer in range(2):

            @pl.when(ctx.core != layer)
            def _(layer=layer):
                for i in range(2):
                    ctx.send[i] = getattr(ctx, "l%d_%d" % (layer, i))[...]

    ins = {"l%d_%d" % (l, i): v for l in range(2) for i, v in enumerate(layers[l])}
    shape = (2,) + layers[0][0].shape
    return swap(launch(plan, body, "cross", ins, dict(send=(shape, BF)), limit=4).send)


def swap(value):
    return lax.ppermute(value, MESH_AXES[0], [(0, 1), (1, 0)])


def call_unpack(plan, which, starts, layers, crossed):
    ins = {"l%d_%d" % (l, i): v for l in range(2) for i, v in enumerate(layers[l])}
    ins.update(crossed=crossed)
    ffn = dict(up=((128, F), F32), dn=((512, D), F32))
    rest = dict(out=((128, D), F32), exp=((128, 2 * D), F32), prj=((128, D), F32))
    last = dict(qkv=((128, 3 * D), F32), gains=((6, 128), F32), taps=((9, 128), F32))
    results = (ffn, rest, dict(ffn, **last))[which]

    def body(ctx):
        for layer in range(2):

            @pl.when(ctx.core == layer)
            def _(layer=layer):
                start = starts[layer]
                for k in range(4):
                    half = layer if k < 2 else 1 - layer
                    side = ctx.fast if half == 0 else ctx.slow
                    a = side if k % 2 == 0 else 1 - side
                    source = getattr(ctx, "l%d_%d" % (layer, k)) if k < 2 else ctx.crossed.at[k - 2]
                    for b in range(2):
                        rows = slice(64 * b, 64 * b + 64)
                        first = source[b, start : start + 64, :].astype(F32)
                        if which != 1:
                            at = pl.multiple_of(half * 256 + a * 128 + b * 64, 64)
                            ctx.dn[pl.ds(at, 64), :] = first
                            at = pl.multiple_of(half * FH + a * D, D)
                            ctx.up[rows, pl.ds(at, D)] = source[b, start + 64 : start + 128, :].astype(F32)
                        else:
                            at = pl.multiple_of(half * 512 + a * 256, 256)
                            ctx.exp[rows, pl.ds(at, 256)] = first[:, 0:256]
                            at = pl.multiple_of(half * 256 + a * 128, 128)
                            ctx.out[rows, pl.ds(at, 128)] = first[:, 256:384]
                            ctx.prj[rows, pl.ds(at, 128)] = first[:, 384:512]
                        if which == 2:
                            third = source[b, start + 128 : start + 192, :].astype(F32)
                            at = pl.multiple_of(half * 768 + a * 384, 128)
                            ctx.qkv[rows, pl.ds(at, 384)] = third[:, 0:384]
                            if k % 2 == 0 and b == 0:
                                small = third[0:8, 384:512]
                                if half == 0:
                                    ctx.gains[...] = small[0:6]
                                    ctx.taps[0:2, :] = small[6:8]
                                else:
                                    ctx.taps[2:9, :] = small[0:7]

    return launch(plan, body, "unpack", ins, {}, results=results, limit=6)


def pick_rows(plan, arrays, gains, taps):
    size = arrays[0].shape[1]
    half = plan.rows // 2

    def body(ctx):
        near = lax.div(ctx.row, half) == ctx.core
        copies = []
        for i in range(len(arrays)):
            source = getattr(ctx, "value%d" % i)
            for k in range(3):
                other = jnp.where(near, k, (0, 2, 3, 1)[k])
                copies.append(
                    pltpu.make_async_copy(
                        source.at[ctx.row ^ other], getattr(ctx, "p%d_%d" % (i, k)), ctx.sems[len(copies)]
                    )
                )
        small = [
            pltpu.make_async_copy(ctx.gains, ctx.gains_in, ctx.sems[20]),
            pltpu.make_async_copy(ctx.taps, ctx.taps_in, ctx.sems[21]),
        ]
        for copy in small + copies:
            copy.start()
        for copy in small:
            copy.wait()
        ctx.small[0:6, :] = ctx.gains_in[0].astype(F32)
        ctx.small[6:15, :] = ctx.taps_in[0].astype(F32)
        ctx.small[15:16, :] = jnp.zeros((1, D), F32)
        for copy in copies:
            copy.wait()

    names = [["p%d_%d" % (i, k) for k in range(3)] for i in range(len(arrays))]
    outs = {n: ((size, D), BF) for group in names for n in group}
    far = {"value%d" % i: v for i, v in enumerate(arrays)}
    picked = launch(
        plan, body, "pick_rows", {}, dict(outs, small=((16, D), F32)),
        scratch=dict(gains_in=((1, 6, D), BF), taps_in=((1, 9, D), BF)),
        far=dict(far, gains=gains, taps=taps), limit=4,
    )
    result = []
    for group in names:
        sent = [getattr(picked, n) for n in group]
        both, third = [], []
        for chip in range(plan.seq):
            c = (chip % 4) // 2
            both.append((c * plan.seq + chip, c * plan.seq + (chip ^ 1)))
            both.append(((1 - c) * plan.seq + chip, c * plan.seq + (chip ^ 2)))
            third.append(((1 - c) * plan.seq + chip, c * plan.seq + (chip ^ 3)))
        pieces = [
            sent[0], lax.ppermute(sent[1], MESH_AXES[::2], both),
            lax.ppermute(sent[2], MESH_AXES[::2], third),
        ]
        result.append({"piece%d" % k: v for k, v in enumerate(pieces)})
    return result, picked.small


def join_frames(ctx, target):
    plan = ctx.plan
    half = plan.rows // 2
    size = plan.frames // half
    near = lax.div(ctx.row, half) == ctx.core

    def put(piece, source):
        at = pl.multiple_of(lax.rem(source, half) * size, size)
        target[pl.ds(at, size), :] = piece[...]

    @pl.when(near)
    def _():
        put(ctx.piece0, ctx.row)
        put(ctx.piece1, ctx.row ^ 1)

    @pl.when(jnp.logical_not(near))
    def _():
        put(ctx.piece1, ctx.row ^ 2)
        put(ctx.piece2, ctx.row ^ 3)


def split_layers(plan, layers, settle):
    count = len(layers[0])

    def body(ctx):
        for layer in range(2):
            for i in range(count):
                value = getattr(ctx, "l%d_%d" % (layer, i))

                @pl.when(ctx.core == layer)
                def _(value=value, i=i):
                    ctx.keep[i] = value[...]

                @pl.when(ctx.core != layer)
                def _(value=value, i=i):
                    ctx.send[i] = value[...]

    shape = (count, plan.frames, D)
    ins = {"l%d_%d" % (l, i): v for l in range(2) for i, v in enumerate(layers[l])}
    out = launch(
        plan, body, "split", ins, dict(keep=(shape, BF), send=(shape, BF)), settle=settle, limit=6
    )
    return out.keep, swap(out.send)


def chips_apart(plan, value, bit):
    pairs = [(c * plan.seq + i, c * plan.seq + (i ^ bit)) for c in range(2) for i in range(plan.seq)]
    return lax.ppermute(value, MESH_AXES[::2], pairs)


def deal_rows(plan, keep, got):
    size = plan.frames // 2

    def body(ctx):
        for distance, target in ((0, ctx.rest.at[0]), (2, ctx.rest.at[1]), (1, ctx.near.at[0]), (3, ctx.near.at[1])):
            chip = ctx.row ^ distance
            at = pl.multiple_of(lax.rem(chip, 2) * size, size)

            @pl.when(lax.div(chip, 2) == ctx.core)
            def _(target=target, at=at):
                target[...] = ctx.keep[:, pl.ds(at, size), :]

            @pl.when(lax.div(chip, 2) != ctx.core)
            def _(target=target, at=at):
                target[...] = ctx.got[:, pl.ds(at, size), :]

    shape = (2, keep.shape[0], size, D)
    dealt = launch(
        plan, body, "deal_rows", dict(keep=keep, got=got), dict(near=(shape, BF), rest=(shape, BF)), limit=8
    )
    dealt.got = chips_apart(plan, dealt.near, 1)
    return dealt


def deal_far(plan, dealt):
    def body(ctx):
        ctx.far[0] = ctx.rest[1]
        ctx.far[1] = ctx.got[1]

    dealt.far = launch(
        plan, body, "deal_far", dict(rest=dealt.rest, got=dealt.got),
        dict(far=(dealt.rest.shape, BF)), limit=8,
    ).far
    dealt.far_got = chips_apart(plan, dealt.far, 2)
    return dealt


def place_rows(plan, dealt):
    def body(ctx):
        pieces = (ctx.rest.at[0], ctx.got.at[0], ctx.far.at[0], ctx.far.at[1])
        for distance, piece in enumerate(pieces):
            ctx.activations[ctx.row ^ distance] = piece[0]
            ctx.input_grads[ctx.row ^ distance] = piece[1].astype(F32)

    shape = (plan.rows,) + dealt.rest.shape[2:]
    return launch(
        plan, body, "place_rows", dict(rest=dealt.rest, got=dealt.got, far=dealt.far_got), {},
        results=dict(activations=(shape, BF), input_grads=(shape, F32)), limit=8,
    )


def halo_exchange(plan, send, rows):
    if plan.halos == 1:
        return swap(send)
    return jnp.concatenate(
        [
            lax.ppermute(send[0:rows], MESH_AXES[::2], plan.to_right),
            lax.ppermute(send[rows:], MESH_AXES[::2], plan.to_left),
        ],
        axis=0,
    )


def halo_return(plan, grads, rows):
    if plan.halos == 1:
        return swap(grads)
    return jnp.concatenate(
        [
            lax.ppermute(grads[0:rows], MESH_AXES[::2], plan.to_left),
            lax.ppermute(grads[rows:], MESH_AXES[::2], plan.to_right),
        ],
        axis=0,
    )


def plain_gradients(plan, layers):
    def whole(keep, send):
        return jnp.where(
            plan.core == 0,
            jnp.concatenate([keep, send], axis=1),
            jnp.concatenate([send, keep], axis=1),
        )

    stacked = []
    for f in layers:
        p1, p2, p3, q1, q2, q3, k1, k2, k3 = f.p1, f.p2, f.p3, f.q1, f.q2, f.q3, f.k1, f.k2, f.k3
        q1 = q1[: plan.frames]
        operands = (
            (p1[:, :D], whole(k1[:, :FH], q1[:, D : D + FH])),
            (whole(f.a1, p1[:, 2 * D :]), q1[:, :D]),
            (p1[:, D : 2 * D], whole(k1[:, FH:], q1[:, D + FH : Q2_AT])),
            (p2[:, :D], whole(k2[:, D:], q2[:, D:])),
            (p2[:, D:], whole(k2[:, :D], q2[:, :D])),
            (p3[:, :D], whole(k3[:, FH:], q3[:, D + FH :])),
            (p3[:, D : 2 * D], whole(k3[:, :FH], q3[:, D : D + FH])),
            (whole(f.a2, p3[:, 2 * D :]), q3[:, :D]),
        )
        grads = [dot_tn(a, b).astype(BF) for a, b in operands]
        grads.append(f.smalls[0:6].astype(BF))
        grads.append(f.smalls[6:15].astype(BF))
        stacked.append(grads)
    result = []
    for index in range(10):
        both = jnp.stack([stacked[0][index], stacked[1][index]])
        mine = lax.psum_scatter(both, MESH_AXES[0], scatter_dimension=0, tiled=False)
        dim = 0 if index < 8 else 1
        mine = lax.psum_scatter(mine, MESH_AXES[2], scatter_dimension=dim, tiled=True)
        result.append(lax.psum(mine, MESH_AXES[1]).astype(F32))
    up1, dn1, qkv, out, exp, prj, up2, dn2, gains, taps = result
    return up1, dn1, qkv, out, exp, taps, prj, up2, dn2, gains


def make_plan(mesh_shape, inputs, lengths, weights):
    plan = SimpleNamespace(token=None, lengths=lengths)
    plan.rows = inputs.shape[0]
    assert plan.rows == 4
    plan.dp, plan.seq = mesh_shape[MESH_AXES[1]], mesh_shape[MESH_AXES[2]]
    plan.length = inputs.shape[1] * plan.seq
    plan.frames = plan.rows * inputs.shape[1] // 2
    plan.halos = 1 if plan.seq == plan.rows else 2
    plan.direct = plan.dp == 4 and plan.seq == 4
    plan.blocks = plan.seq if plan.direct else 1
    plan.core = lax.axis_index(MESH_AXES[0])
    seq = plan.seq
    plan.to_right = [(q, seq + q) for q in range(seq)]
    plan.to_right += [(seq + q, q + plan.rows) for q in range(seq - plan.rows)]
    plan.to_left = [(b, a) for a, b in plan.to_right]
    plan.own = [w[0] for w in weights]
    return plan


def per_device(
    mesh_shape,
    inputs,
    cotangent,
    lengths,
    ffn_one_up,
    ffn_one_down,
    attn_project,
    attn_output,
    conv_expand,
    conv_depthwise,
    conv_project,
    ffn_two_up,
    ffn_two_down,
    norm_gains,
):
    matrices = (
        ffn_one_up, ffn_one_down, attn_project, attn_output, conv_expand, conv_project, ffn_two_up,
        ffn_two_down,
    )
    plan = make_plan(mesh_shape, inputs, lengths, matrices)
    direct = plan.direct
    (pieces, cotangent_pieces), plan.small_own = pick_rows(
        plan, (inputs, cotangent), norm_gains, conv_depthwise
    )
    plan.small_other = swap(plan.small_own)
    plan.other = [swap(w) for w in plan.own]

    def over(value):
        return swap(value) if direct else None

    def after(value, other):
        return lax.optimization_barrier((value, other))[0]

    def there(*values):
        return values if direct else ()

    first0 = call_first(plan, pieces)
    kvh0 = halo_exchange(plan, first0.kvs, W)
    mid0 = call_attend(plan, 0, first0, kvh0)
    gh0 = halo_exchange(plan, mid0.gsend, EDGE)
    turn = call_conv_first(plan, mid0, gh0)
    kvh1 = halo_exchange(plan, turn.kvs, W)
    got0 = SimpleNamespace(p1=over(first0.p1), p2=over(mid0.p2))
    mid1 = call_attend(plan, 1, turn, kvh1, there(got0.p1, got0.p2))
    gh1 = halo_exchange(plan, mid1.gsend, EDGE)
    got0.p3, got1 = over(turn.p3), SimpleNamespace(p1=over(turn.p1))
    end = call_conv_last(plan, mid1, gh1, cotangent_pieces, there(got0.p3, got1.p1))
    dzh1 = halo_exchange(plan, end.dzs, EDGE)
    launch(plan, lambda ctx: None, "between", {}, {}, limit=1)
    got1.c3, got1.p2 = over(after(end.c3, dzh1)), over(after(mid1.p2, dzh1))
    own1 = SimpleNamespace(
        p1=turn.p1, a1=turn.a1, p2=mid1.p2, c3=end.c3, a2=end.a2, k3=end.k3
    )
    own0 = SimpleNamespace(
        p1=first0.p1, a1=first0.a1, p2=mid0.p2, p3=turn.p3, a2=turn.a2
    )
    att1 = call_attend_back(plan, 1, turn, mid1, end, gh1, dzh1, ())
    back1 = halo_return(plan, att1.dkvh, W)
    own1.q2, own1.k2 = att1.q2, att1.k2
    if direct:
        two1 = call_bucket(plan, (0,), own1, got1)
    beg1 = call_first_back(plan, 1, turn.y, turn, att1, back1, there(got1.p2))
    own1.q1, own1.k1, own1.smalls = beg1.q1, beg1.k1, beg1.smalls
    got1.q1 = over(beg1.q1)
    last0 = call_last(plan, turn, beg1.ig, ())
    dzh0 = halo_exchange(plan, last0.dzs, EDGE)
    own0.q3, own0.k3 = last0.q3, last0.k3
    got0.q3 = over(last0.q3)
    if direct:
        one1 = call_bucket(plan, (2,), own1, got1)
    att0 = call_attend_back(plan, 0, first0, mid0, last0, gh0, dzh0, there(got0.q3))
    back0 = halo_return(plan, att0.dkvh, W)
    own0.q2, own0.k2 = att0.q2, att0.k2
    if direct:
        mid1b = call_bucket(plan, (1,), own1, got1)
    beg0 = call_first_back(plan, 0, first0.x, first0, att0, back0, ())
    own0.q1, own0.k1, own0.smalls = beg0.q1, beg0.k1, beg0.smalls
    got0.q1 = over(beg0.q1)
    keep, got = split_layers(plan, ((turn.y, beg0.ig), (end.y, beg1.ig)), ())
    if direct:
        two0 = call_bucket(plan, (0,), own0, got0)
    dealt = deal_rows(plan, keep, got)
    if direct:
        mid0b = call_bucket(plan, (1,), own0, got0)
        early1 = call_second(plan, [two1, mid1b])
        one0 = call_bucket(plan, (2,), own0, got0)
        one1 = call_second(plan, [one1])
    dealt = deal_far(plan, dealt)
    if direct:
        early0 = call_second(plan, [two0, mid0b])
        one1 = call_third(plan, [one1])
    framed = place_rows(plan, dealt)
    if direct:
        early1 = call_third(plan, [early1])
        one1 = call_fourth(plan, one1)
        early0 = call_third(plan, [early0])
        one0 = call_second(plan, [one0])
        early1 = call_fourth(plan, early1)
        one1 = call_total(plan, one1)
        early0 = call_fourth(plan, early0)
        one0 = call_third(plan, [one0])
        early1 = call_total(plan, early1)
        one1 = call_pair(plan, one1)
        early1 = call_pair(plan, early1)
        one0 = call_fourth(plan, one0)
        early0 = call_total(plan, early0)
        early0 = call_pair(plan, early0)
        one0 = call_total(plan, one0)
        crossed = call_cross(plan, (early0, early1))
        one0 = call_pair(plan, one0)
        two = call_unpack(plan, 0, (0, 0), (early0, early1), crossed)
        middle = call_unpack(plan, 1, (ROWS[0], ROWS[0]), (early0, early1), crossed)
        crossed = call_cross(plan, (one0, one1))
        one = call_unpack(plan, 2, (0, 0), (one0, one1), crossed)
        results = (
            one.up, one.dn, one.qkv, middle.out, middle.exp, one.taps, middle.prj,
            two.up, two.dn, one.gains,
        )
    else:
        own1.p3, own1.q3 = end.c3[:, : 2 * D + FH], end.c3[:, 2 * D + FH :]
        results = plain_gradients(plan, (own0, own1))
    activations, input_grads = framed.activations, framed.input_grads
    return (activations[None], input_grads[None]) + tuple(r[None] for r in results)


def solution(mesh):
    section, dp, seq = MESH_AXES
    whole = P(section, None, None)
    sliced = P(section, seq, None)
    across = P(section, None, seq)
    framed = P(section, dp, seq, None)
    return jax.shard_map(
        functools.partial(per_device, dict(mesh.shape)),
        mesh=mesh,
        in_specs=(P(dp, seq, None), P(dp, seq, None), P(dp, None)) + (whole,) * 10,
        out_specs=(framed, framed) + (sliced,) * 5 + (across,) + (sliced,) * 3 + (across,),
        check_vma=False,
    )
```
